32 devices in a mesh: sub: 8 (over z, x), blk: 4 (over y, core).
Axes of the slice: x: 2, y: 2, z: 4, core: 2. Of those that a mesh axis runs over, the one named last changes fastest.
Arguments:
- residual: float32 [32, 16384], P(None, ('sub', 'blk')), may hold values from -6 to 6
- fine_inverse: float32 [8, 2560, 2048], P('sub', None, 'blk'), may hold values from -1 to 1.1
- coarse_inverse: float32 [2048, 4, 512], P('sub', 'blk'), may hold values from -0.5 to 0.5, as said below
- wanted_rows: int32 [8, 2, 256], P('sub'), may hold values from 0 to 2047
- wanted_count: int32 [8, 2], P('sub'), may hold values from 32 to 256, as said below
- aggregate: int32 [16384], P(('sub', 'blk')), may hold values from 0 to 255
Outputs:
- preconditioned: float32 [32, 16384], P(None, ('sub', 'blk'))
The draws below stay inside these ranges and needn't reach their ends.
Inputs may be any that keep to these rules, and one draw needn't show every extreme that they name: M of the steps is symmetric: coarse_inverse[i, b, s * 64 + q] equals coarse_inverse[s * 256 + b * 64 + q, b2, s2 * 64 + q2] where i = s2 * 256 + b2 * 64 + q2. `wanted_count`: counts vary from side to side; in every draw some subdomain other than the first and last takes exactly 256 rows from one side.
All inputs are finite; a program needn't handle non-finite values.
Results may differ from the reference program's by a relative error of at most 0.000052.
Values sent between devices are 32-bit elements; how exact they have to be, the bound alone decides.
No kernel may reach another device: no remote copies, remote signals or barrier semaphores. Data moves between devices by JAX's collectives and lax.ppermute only.
A program may use at most 64 MiB of HBM per device.

```python
import math
import jax
import jax.numpy as jnp
from jax import lax

PROBES = 32
OWN = 2048
HMAX = 256
CPS = 256
SUBDOMAINS = 8
EXT = 2560
ROWS = 16384
NC = 2048
CPART = 64
N_BLK = 4


def draw_fine_inverse(key, part):
    noise_field = jnp.clip(jax.random.normal(key, (SUBDOMAINS, EXT, OWN), jnp.float32), -5.0, 5.0)
    row_ids = lax.broadcasted_iota(jnp.int32, (1, EXT, OWN), 1)
    col_ids = lax.broadcasted_iota(jnp.int32, (1, EXT, OWN), 2)
    diagonal = (row_ids == col_ids + HMAX).astype(jnp.float32)
    return 0.6 * diagonal + noise_field * (0.6 / math.sqrt(EXT))


def draw_coarse_inverse(key, part):
    noise_field = jnp.clip(jax.random.normal(key, (NC, NC), jnp.float32), -5.0, 5.0)
    mirrored = noise_field + noise_field.T
    row_ids = lax.broadcasted_iota(jnp.int32, (NC, NC), 0)
    col_ids = lax.broadcasted_iota(jnp.int32, (NC, NC), 1)
    symmetric = 0.3 * (row_ids == col_ids).astype(jnp.float32) + mirrored * (0.3 / math.sqrt(2.0 * NC))
    groups = CPS // CPART
    grouped = symmetric.reshape(NC, SUBDOMAINS, groups, CPART).transpose(0, 2, 1, 3)
    return grouped.reshape(NC, groups, SUBDOMAINS * CPART)


def draw_wanted_count(key, part):
    key_counts, key_sub, key_side = jax.random.split(key, 3)
    counts = jax.random.randint(key_counts, (SUBDOMAINS, 2), HMAX // 8, HMAX + 1, dtype=jnp.int32)
    chosen_sub = jax.random.randint(key_sub, (), 1, SUBDOMAINS - 1, dtype=jnp.int32)
    chosen_side = jax.random.randint(key_side, (), 0, 2, dtype=jnp.int32)
    sub_ids = lax.broadcasted_iota(jnp.int32, (SUBDOMAINS, 2), 0)
    side_ids = lax.broadcasted_iota(jnp.int32, (SUBDOMAINS, 2), 1)
    return jnp.where((sub_ids == chosen_sub) & (side_ids == chosen_side), HMAX, counts)


def touch_ends(values, stream_key, least, top_value):
    extent = values.shape
    place = [jax.random.randint(jax.random.fold_in(stream_key, axis), (), 0, extent[axis]) for axis in range(len(extent))]
    values = values.at[tuple(place)].set(least)
    longest = extent.index(max(extent))
    place[longest] = (place[longest] + 1) % extent[longest]
    return values.at[tuple(place)].set(top_value)


def level_of(stream_key, shape, pieces, low, top_value):
    level = 1.0
    for axis_at, shards_of in pieces:
        draws = jax.random.uniform(jax.random.fold_in(jax.random.fold_in(stream_key, 6), axis_at), (shards_of,), jnp.float32, low / len(pieces), top_value / len(pieces))
        level = level * jnp.repeat(jnp.exp(draws), shape[axis_at] // shards_of).reshape((-1,) + (1,) * (len(shape) - 1 - axis_at))
    return level


def noise(rng, dims, spread, bound, pieces=(), kind=jnp.bfloat16):
    level = level_of(rng, dims, pieces, -0.22, 0.18) if pieces else 1.0
    drawn = jax.random.normal(rng, dims, jnp.float32) * spread * level
    return jnp.minimum(jnp.maximum(drawn, -bound), bound).astype(kind)


def setup_inputs(seed: int = 0) -> dict:
    arg_keys = jax.random.split(jax.random.key(seed), 7)
    residual = noise(arg_keys[0], (PROBES, ROWS), 1.0, 6.0, ((1, 32),), jnp.float32)
    fine_inverse = draw_fine_inverse(jax.random.fold_in(arg_keys[6], 71), 0)
    coarse_inverse = draw_coarse_inverse(jax.random.fold_in(arg_keys[6], 71), 0)
    wanted_rows = touch_ends(jax.random.randint(arg_keys[3], (SUBDOMAINS, 2, HMAX), 0, OWN), jax.random.fold_in(arg_keys[3], 1), 0, OWN - 1).astype(jnp.int32)
    wanted_count = draw_wanted_count(jax.random.fold_in(arg_keys[6], 71), 0)
    aggregate = touch_ends(jax.random.randint(arg_keys[5], (ROWS,), 0, CPS), jax.random.fold_in(arg_keys[5], 1), 0, CPS - 1).astype(jnp.int32)
    return {"residual": residual, "fine_inverse": fine_inverse, "coarse_inverse": coarse_inverse, "wanted_rows": wanted_rows, "wanted_count": wanted_count, "aggregate": aggregate}


def pick_rows(source, row_lists, row_totals):
    picked = jnp.take_along_axis(source, row_lists[None, :, :], axis=2)
    slot_ids = jnp.arange(HMAX, dtype=jnp.int32)
    kept_mask = slot_ids[None, :] < row_totals[:, None]
    return jnp.where(kept_mask[None, :, :], picked, jnp.zeros_like(picked))


def reference(residual, fine_inverse, coarse_inverse, wanted_rows, wanted_count, aggregate):
    probes = residual.shape[0]
    blocks = residual.reshape(probes, SUBDOMAINS, OWN)
    zeros_block = jnp.zeros((probes, 1, OWN), jnp.float32)
    left_blocks = jnp.concatenate([zeros_block, blocks[:, :-1, :]], axis=1)
    right_blocks = jnp.concatenate([blocks[:, 1:, :], zeros_block], axis=1)
    left_halo = pick_rows(left_blocks, wanted_rows[:, 0, :], wanted_count[:, 0])
    right_halo = pick_rows(right_blocks, wanted_rows[:, 1, :], wanted_count[:, 1])
    extended = jnp.concatenate([left_halo, blocks, right_halo], axis=2)
    fine_part = jnp.einsum("pse,seo->pso", extended, fine_inverse, precision=lax.Precision.HIGHEST)
    dof_ids = (jnp.arange(ROWS, dtype=jnp.int32) // OWN) * CPS + aggregate
    coarse_rhs = jax.ops.segment_sum(residual.T, dof_ids, num_segments=NC)
    ordered = coarse_rhs.reshape(SUBDOMAINS, N_BLK, CPART, probes).transpose(1, 0, 2, 3).reshape(NC, probes)
    flat_inverse = coarse_inverse.reshape(NC, NC)
    coarse_solution = jnp.dot(flat_inverse, ordered, precision=lax.Precision.HIGHEST, preferred_element_type=jnp.float32)
    lifted = coarse_solution[dof_ids, :]
    return fine_part.reshape(probes, ROWS) + lifted.T
```

```python
import functools

import jax
import jax.numpy as jnp
from jax import lax
from jax.experimental import pallas as pl
from jax.experimental.pallas import tpu as pltpu
from jax.sharding import PartitionSpec as P

BF16 = jnp.bfloat16
F32 = jnp.float32
NN = (((1,), (0,)), ((), ()))
NT = (((1,), (1,)), ((), ()))
LANES = 128


def split3(x):
    hi = x.astype(BF16)
    rest = x - hi.astype(F32)
    mid = rest.astype(BF16)
    low = (rest - mid.astype(F32)).astype(BF16)
    return jnp.concatenate([hi, mid, low], axis=0)


def split2(x):
    hi = x.astype(BF16)
    low = (x - hi.astype(F32)).astype(BF16)
    return hi, low


def dot(a, b, dims=NN):
    return lax.dot_general(a, b, dims, preferred_element_type=F32)


def dot3(x, weights):
    rows = x.shape[0]
    x_hi, x_low = split2(x)
    w_hi, w_low = split2(weights)
    both = dot(jnp.concatenate([x_hi, x_low], axis=0), w_hi)
    return both[:rows] + both[rows:] + dot(x_hi, w_low)


def fold3(acc, rows):
    return acc[:rows] + acc[rows : 2 * rows] + acc[2 * rows :]


def head_kernel(width, own_ref, coarse_ref, lists_ref, send_ref, halo_ref):
    shards, padded, cols = own_ref.shape
    rows = padded - 8
    coarse_len = coarse_ref.shape[0]
    rhs = jnp.zeros((3 * rows, coarse_len), F32)
    picked = [jnp.zeros((3 * rows, lists_ref.shape[1]), F32) for _ in range(2)]
    levels = lax.broadcasted_iota(jnp.int32, (coarse_len, cols), 0)
    local = lax.broadcasted_iota(jnp.int32, (cols, lists_ref.shape[1]), 0)
    for shard in range(shards):
        block = split3(own_ref[shard, :rows])
        unknowns = own_ref[shard, rows : rows + 1].astype(jnp.int32)
        onehot = (levels == unknowns).astype(F32).astype(BF16)
        rhs = rhs + dot(block, onehot, NT)
        for side in range(2):
            wanted = lists_ref[side : side + 1] - shard * cols
            chosen = (local == wanted).astype(F32).astype(BF16)
            picked[side] = picked[side] + dot(block, chosen)
    for side in range(2):
        halo_ref[side] = fold3(picked[side], rows)
    value = dot3(fold3(rhs, rows), coarse_ref[...])
    half = rows // 2
    lane = lax.broadcasted_iota(jnp.int32, (half, LANES), 1)
    for tile in range(value.shape[1] // LANES):
        part = value[:, tile * LANES : (tile + 1) * LANES]
        turned = pltpu.roll(part, width, 1)
        first = jnp.where(lane < width, part[:half], turned[half:])
        second = jnp.where(lane < width, turned[:half], part[half:])
        for copy in range(shards):
            send_ref[2 * tile, copy] = first
            send_ref[2 * tile + 1, copy] = second


def own_kernel(margin, own_ref, fine_ref, out_ref, fine_buf, sems):
    shards, padded, cols = own_ref.shape
    rows = padded - 8

    def fetch(shard):
        return pltpu.make_async_copy(
            fine_ref.at[0, pl.ds(margin + shard * cols, cols)], fine_buf.at[shard], sems.at[shard]
        )

    for shard in range(shards):
        fetch(shard).start()
    total = jnp.zeros(out_ref.shape, F32)
    for shard in range(shards):
        fetch(shard).wait()
        total = total + dot3(own_ref[shard, :rows], fine_buf[shard])
    out_ref[...] = total


def tail_kernel(
    width, counts_ref, got_ref, left_ref, right_ref, fine_ref, agg_ref, own_ref, out_ref, fine_buf, sems
):
    subs, shards, half, _ = got_ref.shape
    margin = left_ref.shape[1]
    ext = fine_ref.shape[1]

    def fetch(side, start):
        return pltpu.make_async_copy(fine_ref.at[0, pl.ds(start, margin)], fine_buf.at[side], sems.at[side])

    copies = [fetch(0, 0), fetch(1, ext - margin)]
    for copy in copies:
        copy.start()
    sums = [got_ref[0, shard] for shard in range(shards)]
    for sub in range(1, subs):
        for shard in range(shards):
            sums[shard] = sums[shard] + got_ref[sub, shard]
    lane = lax.broadcasted_iota(jnp.int32, (half, LANES), 1)
    top, bottom = [], []
    for pair in range(shards // 2):
        first, second = sums[2 * pair], sums[2 * pair + 1]
        top.append(jnp.where(lane < width, first, pltpu.roll(second, width, 1)))
        bottom.append(jnp.where(lane < width, pltpu.roll(first, width, 1), second))
    coarse = jnp.concatenate([jnp.concatenate(top, axis=1), jnp.concatenate(bottom, axis=1)], axis=0)
    levels = lax.broadcasted_iota(jnp.int32, (coarse.shape[1], out_ref.shape[1]), 0)
    onehot = (levels == agg_ref[...]).astype(F32).astype(BF16)
    total = own_ref[...] + fold3(dot(split3(coarse), onehot), coarse.shape[0])
    slots = lax.broadcasted_iota(jnp.int32, left_ref.shape, 1)
    for side, halo_ref in enumerate((left_ref, right_ref)):
        copies[side].wait()
        halo = jnp.where(slots < counts_ref[0, side], halo_ref[...], 0.0)
        total = total + dot3(halo, fine_buf[side])
    out_ref[...] = total


def whole(space=pltpu.VMEM):
    return pl.BlockSpec(memory_space=space)


def on_device(residual, fine_inverse, coarse_inverse, wanted_rows, wanted_count, aggregate):
    subs = lax.axis_size("sub")
    shards = lax.axis_size("blk")
    probes, cols = residual.shape
    margin = wanted_rows.shape[2]
    coarse_len = coarse_inverse.shape[0]
    width = coarse_len // shards
    up = [(i, i + 1) for i in range(subs - 1)]
    down = [(i + 1, i) for i in range(subs - 1)]

    from_right = lax.ppermute(wanted_rows[0, 0:1], "sub", down)
    from_left = lax.ppermute(wanted_rows[0, 1:2], "sub", up)
    lists = jnp.concatenate([from_right, from_left], axis=0)

    codes = jnp.broadcast_to(aggregate.astype(F32)[None], (8, cols))
    packed = jnp.concatenate([residual, codes], axis=0)
    copies = jnp.broadcast_to(packed[None], (shards,) + packed.shape)
    own = lax.all_to_all(copies, "blk", 0, 0, tiled=True)

    send, halos = pl.pallas_call(
        functools.partial(head_kernel, width),
        out_shape=(
            jax.ShapeDtypeStruct((subs, shards, probes // 2, LANES), F32),
            jax.ShapeDtypeStruct((2, probes, margin), F32),
        ),
        in_specs=[whole(), whole(), whole()],
        out_specs=(whole(), whole()),
        name="head",
    )(own, coarse_inverse[:, 0, :], lists)

    left = lax.ppermute(halos[0], "sub", up)
    right = lax.ppermute(halos[1], "sub", down)
    flat = send.reshape((subs * shards,) + send.shape[2:])
    got = lax.all_to_all(flat, ("sub", "blk"), 0, 0, tiled=True)
    got = got.reshape(send.shape)

    owned = pl.pallas_call(
        functools.partial(own_kernel, margin),
        out_shape=jax.ShapeDtypeStruct((probes, cols), F32),
        in_specs=[whole(), whole(pl.ANY)],
        out_specs=whole(),
        scratch_shapes=[
            pltpu.VMEM((shards, cols, cols), F32),
            pltpu.SemaphoreType.DMA((shards,)),
        ],
        compiler_params=pltpu.CompilerParams(vmem_limit_bytes=24 << 20),
        cost_estimate=pl.CostEstimate(
            flops=6 * probes * shards * cols * cols,
            bytes_accessed=4 * shards * cols * cols,
            transcendentals=0,
        ),
        name="owned",
    )(own, fine_inverse)

    return pl.pallas_call(
        functools.partial(tail_kernel, width),
        out_shape=jax.ShapeDtypeStruct((probes, cols), F32),
        in_specs=[whole(pltpu.SMEM), whole(), whole(), whole(), whole(pl.ANY), whole(), whole()],
        out_specs=whole(),
        scratch_shapes=[
            pltpu.VMEM((2, margin, cols), F32),
            pltpu.SemaphoreType.DMA((2,)),
        ],
        compiler_params=pltpu.CompilerParams(vmem_limit_bytes=24 << 20),
        name="tail",
    )(wanted_count, got, left, right, fine_inverse, aggregate[None], owned)


def solution(mesh):
    in_specs = (
        P(None, ("sub", "blk")),
        P("sub", None, "blk"),
        P("sub", "blk", None),
        P("sub", None, None),
        P("sub", None),
        P(("sub", "blk")),
    )
    out_specs = P(None, ("sub", "blk"))
    return jax.shard_map(
        on_device, mesh=mesh, in_specs=in_specs, out_specs=out_specs, check_vma=False
    )
```

```python
import functools

import jax
import jax.numpy as jnp
from jax import lax
from jax.experimental import pallas as pl
from jax.experimental.pallas import tpu as pltpu
from jax.sharding import PartitionSpec as P

BF16 = jnp.bfloat16
F32 = jnp.float32
NN = (((1,), (0,)), ((), ()))
NT = (((1,), (1,)), ((), ()))
LANES = 128
MIB = 1 << 20


def split3(x):
    hi = x.astype(BF16)
    rest = x - hi.astype(F32)
    mid = rest.astype(BF16)
    low = (rest - mid.astype(F32)).astype(BF16)
    return jnp.concatenate([hi, mid, low], axis=0)


def split2(x):
    hi = x.astype(BF16)
    low = (x - hi.astype(F32)).astype(BF16)
    return hi, low


def dot(a, b, dims=NN):
    return lax.dot_general(a, b, dims, preferred_element_type=F32)


def dot3(x, weights):
    rows = x.shape[0]
    x_hi, x_low = split2(x)
    w_hi, w_low = split2(weights)
    both = dot(jnp.concatenate([x_hi, x_low], axis=0), w_hi)
    return both[:rows] + both[rows:] + dot(x_hi, w_low)


def fold3(acc):
    rows = acc.shape[0] // 3
    return acc[:rows] + acc[rows : 2 * rows] + acc[2 * rows :]


def onehot(condition):
    return condition.astype(F32).astype(BF16)


def parity():
    return lax.rem(lax.axis_index("sub"), 2)


def shard_rows(ref, shard, rows, tiles):
    return jnp.concatenate([ref[shard, pl.ds(t * rows, rows)] for t in range(tiles)], axis=1)


def pick(ref, first, rows, tiles, shards, wanted):
    cols = tiles * LANES
    local = lax.broadcasted_iota(jnp.int32, (cols, wanted.shape[1]), 0)
    total = jnp.zeros((3 * rows, wanted.shape[1]), F32)
    for shard in range(shards):
        block = split3(shard_rows(ref, first + shard, rows, tiles))
        total = total + dot(block, onehot(local == wanted - shard * cols))
    return fold3(total)


def pack_kernel(residual_ref, agg_ref, out_ref):
    rows, cols = residual_ref.shape
    tiles = cols // LANES
    codes = [agg_ref[:, t * LANES : (t + 1) * LANES].astype(F32) for t in range(tiles)]
    codes.append(jnp.zeros((out_ref.shape[1] - rows * tiles - tiles, LANES), F32))
    last = jnp.concatenate(codes, axis=0)
    for receiver in range(out_ref.shape[0]):
        for t in range(tiles):
            out_ref[receiver, t * rows : (t + 1) * rows] = residual_ref[:, t * LANES : (t + 1) * LANES]
        out_ref[receiver, rows * tiles :] = last


def coarse_kernel(width, rows, tiles, shards, pair_ref, coarse_ref, fine_ref, send_ref, fine_out, sem):
    fetch = pltpu.make_async_copy(fine_ref, fine_out, sem)
    fetch.start()
    first = parity() * shards
    cols = tiles * LANES
    coarse_len = width * shards
    levels = lax.broadcasted_iota(jnp.int32, (coarse_len, cols), 0)
    rhs = jnp.zeros((3 * rows, coarse_len), F32)
    for shard in range(shards):
        block = split3(shard_rows(pair_ref, first + shard, rows, tiles))
        codes = [pair_ref[first + shard, pl.ds(tiles * rows + t, 1)] for t in range(tiles)]
        unknowns = jnp.concatenate(codes, axis=1).astype(jnp.int32)
        rhs = rhs + dot(block, onehot(levels == unknowns), NT)
    rhs = fold3(rhs)
    half = rows // 2
    lane = lax.broadcasted_iota(jnp.int32, (half, LANES), 1)
    stride = coarse_ref.shape[0] // coarse_len
    step = 2 if stride % 2 == 0 else 1
    for tile in range(0, stride, step):
        parts = [coarse_ref[pl.ds(tile + k, coarse_len, stride=stride), :] for k in range(step)]
        value = dot3(rhs, jnp.concatenate(parts, axis=1))
        for k in range(step):
            part = value[:, k * LANES : (k + 1) * LANES]
            turned = pltpu.roll(part, width, 1)
            left = jnp.where(lane < width, part[:half], turned[half:])
            right = jnp.where(lane < width, turned[:half], part[half:])
            for copy in range(shards):
                send_ref[2 * (tile + k), copy] = left
                send_ref[2 * (tile + k) + 1, copy] = right
    fetch.wait()


def halo_kernel(rows, tiles, shards, pair_ref, lists_ref, out_ref):
    odd = parity()
    wanted = jnp.where(odd == 1, lists_ref[0:1], lists_ref[1:2])
    out_ref[...] = pick(pair_ref, odd * shards, rows, tiles, shards, wanted)


def own_kernel(rows, tiles, shards, counts_ref, pair_ref, lists_ref, fine_ref, out_ref):
    odd = parity()
    cols = tiles * LANES
    margin = lists_ref.shape[1]
    ext = fine_ref.shape[1]
    total = jnp.zeros(out_ref.shape, F32)
    for shard in range(shards):
        block = shard_rows(pair_ref, odd * shards + shard, rows, tiles)
        total = total + dot3(block, fine_ref[0, margin + shard * cols : margin + (shard + 1) * cols])
    slots = lax.broadcasted_iota(jnp.int32, (1, margin), 1)
    wanted = jnp.where(odd == 1, lists_ref[0:1], lists_ref[1:2])
    wanted = jnp.where(slots < counts_ref[0, 1 - odd], wanted, -1)
    halo = pick(pair_ref, (1 - odd) * shards, rows, tiles, shards, wanted)
    start = pl.multiple_of((1 - odd) * (ext - margin), margin)
    out_ref[...] = total + dot3(halo, fine_ref[0, pl.ds(start, margin)])


def tail_kernel(width, counts_ref, got_ref, halo_ref, fine_ref, agg_ref, own_ref, out_ref):
    subs, shards, half, _ = got_ref.shape
    odd = parity()
    margin = halo_ref.shape[1]
    ext = fine_ref.shape[1]
    slots = lax.broadcasted_iota(jnp.int32, halo_ref.shape, 1)
    halo = jnp.where(slots < counts_ref[0, odd], halo_ref[...], 0.0)
    start = pl.multiple_of(odd * (ext - margin), margin)
    total = own_ref[...] + dot3(halo, fine_ref[0, pl.ds(start, margin)])
    sums = [got_ref[0, shard] for shard in range(shards)]
    for sub in range(1, subs):
        for shard in range(shards):
            sums[shard] = sums[shard] + got_ref[sub, shard]
    lane = lax.broadcasted_iota(jnp.int32, (half, LANES), 1)
    top, bottom = [], []
    for pair in range(shards // 2):
        left, right = sums[2 * pair], sums[2 * pair + 1]
        top.append(jnp.where(lane < width, left, pltpu.roll(right, width, 1)))
        bottom.append(jnp.where(lane < width, pltpu.roll(left, width, 1), right))
    coarse = jnp.concatenate([jnp.concatenate(top, axis=1), jnp.concatenate(bottom, axis=1)], axis=0)
    levels = lax.broadcasted_iota(jnp.int32, (coarse.shape[1], out_ref.shape[1]), 0)
    out_ref[...] = total + fold3(dot(split3(coarse), onehot(levels == agg_ref[...])))


def whole(space=pltpu.VMEM):
    return pl.BlockSpec(memory_space=space)


def limit(mib):
    return pltpu.CompilerParams(vmem_limit_bytes=mib * MIB)


def on_device(residual, fine_inverse, coarse_inverse, wanted_rows, wanted_count, aggregate):
    subs = lax.axis_size("sub")
    shards = lax.axis_size("blk")
    rows, cols = residual.shape
    tiles = cols // LANES
    margin = wanted_rows.shape[2]
    coarse_len = coarse_inverse.shape[0]
    width = coarse_len // shards
    group = 2 * shards
    packed_rows = -(-(rows * tiles + tiles) // 8) * 8
    pairs = [list(range(k, k + group)) for k in range(0, subs * shards, group)]
    swaps = [(i, i + 1) for i in range(1, subs - 1, 2)] + [(i + 1, i) for i in range(1, subs - 1, 2)]
    codes = aggregate[None]

    packed = pl.pallas_call(
        pack_kernel,
        out_shape=jax.ShapeDtypeStruct((group, packed_rows, LANES), F32),
        in_specs=[whole(), whole()],
        out_specs=whole(),
        compiler_params=limit(4),
        name="pack",
    )(residual, codes)
    pair = lax.all_to_all(packed, ("sub", "blk"), 0, 0, axis_index_groups=pairs, tiled=True)
    lists = lax.ppermute(wanted_rows[0], "sub", swaps)

    send, fine = pl.pallas_call(
        functools.partial(coarse_kernel, width, rows, tiles, shards),
        out_shape=(
            jax.ShapeDtypeStruct((subs, shards, rows // 2, LANES), F32),
            jax.ShapeDtypeStruct(fine_inverse.shape, F32),
        ),
        in_specs=[whole(), whole(), whole(pl.ANY)],
        out_specs=(whole(), whole()),
        scratch_shapes=[pltpu.SemaphoreType.DMA],
        compiler_params=limit(54),
        name="coarse",
    )(pair, coarse_inverse.reshape(-1, LANES), fine_inverse)
    flat = send.reshape((subs * shards,) + send.shape[2:])
    got = lax.all_to_all(flat, ("sub", "blk"), 0, 0, tiled=True).reshape(send.shape)

    outgoing = pl.pallas_call(
        functools.partial(halo_kernel, rows, tiles, shards),
        out_shape=jax.ShapeDtypeStruct((rows, margin), F32),
        in_specs=[whole(), whole()],
        out_specs=whole(),
        compiler_params=limit(8),
        name="halo",
    )(pair, lists)
    halo = lax.ppermute(outgoing, "sub", swaps)

    owned = pl.pallas_call(
        functools.partial(own_kernel, rows, tiles, shards),
        out_shape=jax.ShapeDtypeStruct((rows, cols), F32),
        in_specs=[whole(pltpu.SMEM), whole(), whole(), whole()],
        out_specs=whole(),
        compiler_params=limit(16),
        cost_estimate=pl.CostEstimate(
            flops=8 * rows * shards * cols * cols,
            bytes_accessed=4 * shards * cols * cols,
            transcendentals=0,
        ),
        name="owned",
    )(wanted_count, pair, wanted_rows[0], fine)

    return pl.pallas_call(
        functools.partial(tail_kernel, width),
        out_shape=jax.ShapeDtypeStruct((rows, cols), F32),
        in_specs=[whole(pltpu.SMEM)] + [whole()] * 5,
        out_specs=whole(),
        compiler_params=limit(16),
        name="tail",
    )(wanted_count, got, halo, fine, codes, owned)


def solution(mesh):
    in_specs = (
        P(None, ("sub", "blk")),
        P("sub", None, "blk"),
        P("sub", "blk", None),
        P("sub", None, None),
        P("sub", None),
        P(("sub", "blk")),
    )
    out_specs = P(None, ("sub", "blk"))
    return jax.shard_map(
        on_device, mesh=mesh, in_specs=in_specs, out_specs=out_specs, check_vma=False
    )
```

```python
import functools

import jax
import jax.numpy as jnp
from jax import lax
from jax.experimental import pallas as pl
from jax.experimental.pallas import tpu as pltpu
from jax.sharding import PartitionSpec as P

BF16 = jnp.bfloat16
F32 = jnp.float32
NN = (((1,), (0,)), ((), ()))
NT = (((1,), (1,)), ((), ()))
LANES = 128
MIB = 1 << 20


def split3(x):
    hi = x.astype(BF16)
    rest = x - hi.astype(F32)
    mid = rest.astype(BF16)
    low = (rest - mid.astype(F32)).astype(BF16)
    return jnp.concatenate([hi, mid, low], axis=0)


def split2(x):
    hi = x.astype(BF16)
    low = (x - hi.astype(F32)).astype(BF16)
    return hi, low


def dot(a, b, dims=NN):
    return lax.dot_general(a, b, dims, preferred_element_type=F32)


def dot_halves(x, w_hi, w_low):
    rows = x.shape[0]
    x_hi, x_low = split2(x)
    both = dot(jnp.concatenate([x_hi, x_low], axis=0), w_hi)
    return both[:rows] + both[rows:] + dot(x_hi, w_low)


def fold3(acc):
    rows = acc.shape[0] // 3
    return acc[:rows] + acc[rows : 2 * rows] + acc[2 * rows :]


def onehot(condition):
    return condition.astype(F32).astype(BF16)


def shard_rows(ref, shard, rows, tiles):
    return jnp.concatenate([ref[shard, pl.ds(t * rows, rows)] for t in range(tiles)], axis=1)


def fold_chunks(part, width):
    half = part.shape[0] // 2
    lane = lax.broadcasted_iota(jnp.int32, (half, LANES), 1)
    turned = pltpu.roll(part, width, 1)
    left = jnp.where(lane < width, part[:half], turned[half:])
    right = jnp.where(lane < width, turned[:half], part[half:])
    return left, right


def unfold_chunks(chunks, width):
    lane = lax.broadcasted_iota(jnp.int32, chunks[0].shape, 1)
    top, bottom = [], []
    for pair in range(len(chunks) // 2):
        left, right = chunks[2 * pair], chunks[2 * pair + 1]
        top.append(jnp.where(lane < width, left, pltpu.roll(right, width, 1)))
        bottom.append(jnp.where(lane < width, pltpu.roll(left, width, 1), right))
    return jnp.concatenate([jnp.concatenate(top, axis=1), jnp.concatenate(bottom, axis=1)], axis=0)


def pack_kernel(residual_ref, agg_ref, lists_ref, out_ref, lists_out, residual_buf, agg_buf, lists_buf, sems):
    fetches = [
        pltpu.make_async_copy(residual_ref, residual_buf, sems.at[0]),
        pltpu.make_async_copy(agg_ref, agg_buf, sems.at[1]),
        pltpu.make_async_copy(lists_ref, lists_buf, sems.at[2]),
    ]
    for fetch in fetches:
        fetch.start()
    for fetch in fetches:
        fetch.wait()
    rows, cols = residual_ref.shape
    tiles = cols // LANES
    codes = [agg_buf[:, t * LANES : (t + 1) * LANES].astype(F32) for t in range(tiles)]
    codes.append(jnp.zeros((out_ref.shape[1] - rows * tiles - tiles, LANES), F32))
    last = jnp.concatenate(codes, axis=0)
    for receiver in range(out_ref.shape[0]):
        for t in range(tiles):
            out_ref[receiver, t * rows : (t + 1) * rows] = residual_buf[:, t * LANES : (t + 1) * LANES]
        out_ref[receiver, rows * tiles :] = last
    for receiver in range(lists_out.shape[0]):
        lists_out[receiver] = lists_buf[...]


def coarse_kernel(width, rows, tiles, own_ref, lists_ref, coarse_ref, send_ref):
    subs = lists_ref.shape[0]
    shards = own_ref.shape[0]
    cols = tiles * LANES
    coarse_len = width * shards
    me, part_id = lax.axis_index("sub"), lax.axis_index("blk")
    per_tile = LANES // width
    last = subs - 1
    above = lists_ref[jnp.minimum(me + 1, last), 0:1]
    below = lists_ref[jnp.maximum(me - 1, 0), 1:2]
    wanted = [above[:, :LANES], below[:, :LANES]]
    for t in range(1, above.shape[1] // LANES):
        here = part_id // per_tile == t
        for side, row in enumerate((above, below)):
            wanted[side] = jnp.where(here, row[:, t * LANES : (t + 1) * LANES], wanted[side])
    wanted = jnp.concatenate(wanted, axis=1)
    levels = lax.broadcasted_iota(jnp.int32, (coarse_len, cols), 0)
    local = lax.broadcasted_iota(jnp.int32, (cols, 2 * LANES), 0)
    rhs = jnp.zeros((3 * rows, coarse_len), F32)
    picked = jnp.zeros((3 * rows, 2 * LANES), F32)
    for shard in range(shards):
        block = split3(shard_rows(own_ref, shard, rows, tiles))
        codes = [own_ref[shard, pl.ds(tiles * rows + t, 1)] for t in range(tiles)]
        unknowns = jnp.concatenate(codes, axis=1).astype(jnp.int32)
        rhs = rhs + dot(block, onehot(levels == unknowns), NT)
        picked = picked + dot(block, onehot(local == wanted - shard * cols))
    rhs, picked = fold3(rhs), fold3(picked)
    half = rows // 2
    quarters = []
    for side in range(2):
        left, right = fold_chunks(picked[:, side * LANES : (side + 1) * LANES], width)
        quarters.append(jnp.where(lax.rem(part_id, per_tile) == 0, left, right))
    stride = coarse_ref.shape[0] // coarse_len
    for tile in range(0, stride, 2):
        parts = [coarse_ref[pl.ds(tile + k, coarse_len, stride=stride), :] for k in range(2)]
        value = dot_halves(rhs, *split2(jnp.concatenate(parts, axis=1)))
        for k in range(2):
            chunks = fold_chunks(value[:, k * LANES : (k + 1) * LANES], width)
            for e in range(2):
                to = 2 * (tile + k) + e
                send_ref[to, :half] = chunks[e]
                margin = jnp.where(me + 1 == to, quarters[0], jnp.where(me == to + 1, quarters[1], 0.0))
                send_ref[to, half:] = margin


def own_kernel(
    rows, tiles, margin, own_ref, agg_ref, fine_ref, out_ref, hi_ref, low_ref, hot_ref, fine_buf, sems
):
    shards = own_ref.shape[0]
    cols = tiles * LANES
    ext = fine_ref.shape[1]
    pieces = [(margin + shard * cols, cols) for shard in range(shards)]
    pieces += [(0, margin), (ext - margin, margin)]
    copies = []
    for k, (start, size) in enumerate(pieces):
        copies.append(
            pltpu.make_async_copy(
                fine_ref.at[0, pl.ds(start, size)], fine_buf.at[pl.ds(start, size)], sems.at[k]
            )
        )
        copies[k].start()
    levels = lax.broadcasted_iota(jnp.int32, hot_ref.shape, 0)
    hot_ref[...] = onehot(levels == agg_ref[...])
    total = jnp.zeros(out_ref.shape, F32)
    for shard in range(shards):
        start = pieces[shard][0]
        copies[shard].wait()
        block = shard_rows(own_ref, shard, rows, tiles)
        total = total + dot_halves(block, *split2(fine_buf[start : start + cols]))
    out_ref[...] = total
    for side in range(2):
        start = pieces[shards + side][0]
        copies[shards + side].wait()
        hi_ref[side], low_ref[side] = split2(fine_buf[start : start + margin])


def reduce_kernel(got_ref, out_ref):
    subs = got_ref.shape[0]
    half = got_ref.shape[1] // 2
    me = lax.axis_index("sub")
    last = subs - 1
    total = got_ref[0, :half]
    for sub in range(1, subs):
        total = total + got_ref[sub, :half]
    left = jnp.where(me > 0, got_ref[jnp.maximum(me - 1, 0), half:], 0.0)
    right = jnp.where(me < last, got_ref[jnp.minimum(me + 1, last), half:], 0.0)
    for receiver in range(out_ref.shape[0]):
        out_ref[receiver, :half] = total
        out_ref[receiver, half : 2 * half] = left
        out_ref[receiver, 2 * half :] = right


def tail_kernel(width, counts_ref, got_ref, hi_ref, low_ref, hot_ref, own_ref, out_ref):
    shards = got_ref.shape[0]
    half = got_ref.shape[1] // 3
    coarse = unfold_chunks([got_ref[k, :half] for k in range(shards)], width)
    total = own_ref[...] + fold3(dot(split3(coarse), hot_ref[...]))
    for side in range(2):
        first = (1 + side) * half
        halo = unfold_chunks([got_ref[k, first : first + half] for k in range(shards)], width)
        slots = lax.broadcasted_iota(jnp.int32, halo.shape, 1)
        halo = jnp.where(slots < counts_ref[0, side], halo, 0.0)
        total = total + dot_halves(halo, hi_ref[side], low_ref[side])
    out_ref[...] = total


def whole(space=pltpu.VMEM):
    return pl.BlockSpec(memory_space=space)


def limit(mib):
    return pltpu.CompilerParams(vmem_limit_bytes=mib * MIB)


def on_device(residual, fine_inverse, coarse_inverse, wanted_rows, wanted_count, aggregate):
    subs = lax.axis_size("sub")
    shards = lax.axis_size("blk")
    rows, cols = residual.shape
    tiles = cols // LANES
    sides, margin = wanted_rows.shape[1:]
    coarse_len = coarse_inverse.shape[0]
    width = coarse_len // shards
    half = rows // 2
    packed_rows = -(-(rows * tiles + tiles) // 8) * 8
    codes = aggregate[None]

    packed, lists = pl.pallas_call(
        pack_kernel,
        out_shape=(
            jax.ShapeDtypeStruct((shards, packed_rows, LANES), F32),
            jax.ShapeDtypeStruct((subs, sides, margin), jnp.int32),
        ),
        in_specs=[whole(pl.ANY)] * 3,
        out_specs=(whole(), whole()),
        scratch_shapes=[
            pltpu.VMEM(residual.shape, F32),
            pltpu.VMEM(codes.shape, jnp.int32),
            pltpu.VMEM(wanted_rows.shape[1:], jnp.int32),
            pltpu.SemaphoreType.DMA((3,)),
        ],
        compiler_params=limit(60),
        name="pack",
    )(residual, codes, wanted_rows[0])
    own = lax.all_to_all(packed, "blk", 0, 0, tiled=True)
    lists = lax.all_to_all(lists, "sub", 0, 0, tiled=True)

    send = pl.pallas_call(
        functools.partial(coarse_kernel, width, rows, tiles),
        out_shape=jax.ShapeDtypeStruct((subs, 2 * half, LANES), F32),
        in_specs=[whole()] * 3,
        out_specs=whole(),
        compiler_params=limit(12),
        name="coarse",
    )(own, lists, coarse_inverse.reshape(-1, LANES))
    got = lax.all_to_all(send, "sub", 0, 0, tiled=True)

    owned, w_hi, w_low, hot = pl.pallas_call(
        functools.partial(own_kernel, rows, tiles, margin),
        out_shape=(
            jax.ShapeDtypeStruct((rows, cols), F32),
            jax.ShapeDtypeStruct((2, margin, cols), BF16),
            jax.ShapeDtypeStruct((2, margin, cols), BF16),
            jax.ShapeDtypeStruct((coarse_len, cols), BF16),
        ),
        in_specs=[whole(), whole(), whole(pl.ANY)],
        out_specs=(whole(),) * 4,
        scratch_shapes=[
            pltpu.VMEM(fine_inverse.shape[1:], F32),
            pltpu.SemaphoreType.DMA((shards + 2,)),
        ],
        compiler_params=limit(48),
        cost_estimate=pl.CostEstimate(
            flops=6 * rows * shards * cols * cols,
            bytes_accessed=4 * (shards * cols + 2 * margin) * cols,
            transcendentals=0,
        ),
        name="owned",
    )(own, codes, fine_inverse)

    shared = pl.pallas_call(
        reduce_kernel,
        out_shape=jax.ShapeDtypeStruct((shards, 3 * half, LANES), F32),
        in_specs=[whole()],
        out_specs=whole(),
        compiler_params=limit(8),
        name="reduce",
    )(got)
    parts = lax.all_to_all(shared, "blk", 0, 0, tiled=True)

    return pl.pallas_call(
        functools.partial(tail_kernel, width),
        out_shape=jax.ShapeDtypeStruct((rows, cols), F32),
        in_specs=[whole(pltpu.SMEM)] + [whole()] * 5,
        out_specs=whole(),
        compiler_params=limit(12),
        name="tail",
    )(wanted_count, parts, w_hi, w_low, hot, owned)


def solution(mesh):
    in_specs = (
        P(None, ("sub", "blk")),
        P("sub", None, "blk"),
        P("sub", "blk", None),
        P("sub", None, None),
        P("sub", None),
        P(("sub", "blk")),
    )
    out_specs = P(None, ("sub", "blk"))
    return jax.shard_map(
        on_device, mesh=mesh, in_specs=in_specs, out_specs=out_specs, check_vma=False
    )
```

```python
import functools

import jax
import jax.numpy as jnp
from jax import lax
from jax.experimental import pallas as pl
from jax.experimental.pallas import tpu as pltpu
from jax.sharding import PartitionSpec as P

BF16 = jnp.bfloat16
F32 = jnp.float32
NN = (((1,), (0,)), ((), ()))
NT = (((1,), (1,)), ((), ()))
LANES = 128
MIB = 1 << 20


def split3(x):
    hi = x.astype(BF16)
    rest = x - hi.astype(F32)
    mid = rest.astype(BF16)
    low = (rest - mid.astype(F32)).astype(BF16)
    return jnp.concatenate([hi, mid, low], axis=0)


def split2(x):
    hi = x.astype(BF16)
    low = (x - hi.astype(F32)).astype(BF16)
    return hi, low


def dot(a, b, dims=NN):
    return lax.dot_general(a, b, dims, preferred_element_type=F32)


def dot_halves(x, w_hi, w_low):
    rows = x.shape[0]
    x_hi, x_low = split2(x)
    both = dot(jnp.concatenate([x_hi, x_low], axis=0), w_hi)
    return both[:rows] + both[rows:] + dot(x_hi, w_low)


def fold3(acc):
    rows = acc.shape[0] // 3
    return acc[:rows] + acc[rows : 2 * rows] + acc[2 * rows :]


def onehot(condition):
    return condition.astype(F32).astype(BF16)


def shard_rows(ref, shard, rows, tiles):
    return jnp.concatenate([ref[shard, pl.ds(t * rows, rows)] for t in range(tiles)], axis=1)


def pick(ref, rows, tiles, wanted):
    cols = tiles * LANES
    local = lax.broadcasted_iota(jnp.int32, (cols, wanted.shape[1]), 0)
    total = jnp.zeros((3 * rows, wanted.shape[1]), F32)
    for shard in range(ref.shape[0]):
        block = split3(shard_rows(ref, shard, rows, tiles))
        total = total + dot(block, onehot(local == wanted - shard * cols))
    return fold3(total)


def parity():
    return lax.rem(lax.axis_index("sub"), 2)


def pack_kernel(residual_ref, agg_ref, coarse_ref, out_ref, coarse_out, residual_buf, agg_buf, sems):
    fetches = [
        pltpu.make_async_copy(residual_ref, residual_buf, sems.at[0]),
        pltpu.make_async_copy(agg_ref, agg_buf, sems.at[1]),
        pltpu.make_async_copy(coarse_ref, coarse_out, sems.at[2]),
    ]
    for fetch in fetches:
        fetch.start()
    fetches[0].wait()
    fetches[1].wait()
    rows, cols = residual_buf.shape
    tiles = cols // LANES
    codes = [agg_buf[:, t * LANES : (t + 1) * LANES].astype(F32) for t in range(tiles)]
    codes.append(jnp.zeros((out_ref.shape[1] - rows * tiles - tiles, LANES), F32))
    last = jnp.concatenate(codes, axis=0)
    for receiver in range(out_ref.shape[0]):
        for t in range(tiles):
            out_ref[receiver, t * rows : (t + 1) * rows] = residual_buf[:, t * LANES : (t + 1) * LANES]
        out_ref[receiver, rows * tiles :] = last
    fetches[2].wait()


def coarse_kernel(width, rows, tiles, own_ref, coarse_ref, send_ref):
    shards = own_ref.shape[0]
    cols = tiles * LANES
    coarse_len = width * shards
    levels = lax.broadcasted_iota(jnp.int32, (coarse_len, cols), 0)
    rhs = jnp.zeros((3 * rows, coarse_len), F32)
    for shard in range(shards):
        block = split3(shard_rows(own_ref, shard, rows, tiles))
        codes = [own_ref[shard, pl.ds(tiles * rows + t, 1)] for t in range(tiles)]
        unknowns = jnp.concatenate(codes, axis=1).astype(jnp.int32)
        rhs = rhs + dot(block, onehot(levels == unknowns), NT)
    rhs = fold3(rhs)
    half = rows // 2
    lane = lax.broadcasted_iota(jnp.int32, (half, LANES), 1)
    stride = coarse_ref.shape[0] // coarse_len
    for tile in range(0, stride, 2):
        parts = [coarse_ref[pl.ds(tile + k, coarse_len, stride=stride), :] for k in range(2)]
        value = dot_halves(rhs, *split2(jnp.concatenate(parts, axis=1)))
        for k in range(2):
            part = value[:, k * LANES : (k + 1) * LANES]
            turned = pltpu.roll(part, width, 1)
            left = jnp.where(lane < width, part[:half], turned[half:])
            right = jnp.where(lane < width, turned[:half], part[half:])
            for copy in range(shards):
                send_ref[2 * (tile + k), copy] = left
                send_ref[2 * (tile + k) + 1, copy] = right


def outer_kernel(rows, tiles, own_ref, lists_ref, out_ref):
    wanted = jnp.where(parity() == 1, lists_ref[0:1], lists_ref[1:2])
    out_ref[...] = pick(own_ref, rows, tiles, wanted)


def own_kernel(
    rows, tiles, margin, own_ref, agg_ref, fine_ref, out_ref, hi_ref, low_ref, hot_ref, fine_buf, agg_buf, sems
):
    shards = own_ref.shape[0]
    cols = tiles * LANES
    ext = fine_ref.shape[1]
    pieces = [(margin + shard * cols, cols) for shard in range(shards)]
    pieces += [(0, margin), (ext - margin, margin)]
    copies = []
    for k, (start, size) in enumerate(pieces):
        copies.append(
            pltpu.make_async_copy(
                fine_ref.at[0, pl.ds(start, size)], fine_buf.at[pl.ds(start, size)], sems.at[k]
            )
        )
        copies[k].start()
    fetch = pltpu.make_async_copy(agg_ref, agg_buf, sems.at[shards + 2])
    fetch.start()
    fetch.wait()
    levels = lax.broadcasted_iota(jnp.int32, hot_ref.shape, 0)
    hot_ref[...] = onehot(levels == agg_buf[...])
    total = jnp.zeros(out_ref.shape, F32)
    for shard in range(shards):
        start = pieces[shard][0]
        copies[shard].wait()
        block = shard_rows(own_ref, shard, rows, tiles)
        total = total + dot_halves(block, *split2(fine_buf[start : start + cols]))
    out_ref[...] = total
    for side in range(2):
        start = pieces[shards + side][0]
        copies[shards + side].wait()
        hi_ref[side], low_ref[side] = split2(fine_buf[start : start + margin])


def inner_kernel(rows, tiles, counts_ref, other_ref, lists_ref, hi_ref, low_ref, total_ref, out_ref):
    odd = parity()
    slots = lax.broadcasted_iota(jnp.int32, (1, lists_ref.shape[1]), 1)
    wanted = jnp.where(odd == 1, lists_ref[0:1], lists_ref[1:2])
    wanted = jnp.where(slots < counts_ref[0, 1 - odd], wanted, -1)
    halo = pick(other_ref, rows, tiles, wanted)
    out_ref[...] = total_ref[...] + dot_halves(halo, hi_ref[1 - odd], low_ref[1 - odd])


def tail_kernel(width, counts_ref, got_ref, halo_ref, hi_ref, low_ref, hot_ref, total_ref, out_ref):
    subs, shards, half, _ = got_ref.shape
    odd = parity()
    slots = lax.broadcasted_iota(jnp.int32, halo_ref.shape, 1)
    halo = jnp.where(slots < counts_ref[0, odd], halo_ref[...], 0.0)
    total = total_ref[...] + dot_halves(halo, hi_ref[odd], low_ref[odd])
    sums = [got_ref[0, shard] for shard in range(shards)]
    for sub in range(1, subs):
        for shard in range(shards):
            sums[shard] = sums[shard] + got_ref[sub, shard]
    lane = lax.broadcasted_iota(jnp.int32, (half, LANES), 1)
    top, bottom = [], []
    for pair in range(shards // 2):
        left, right = sums[2 * pair], sums[2 * pair + 1]
        top.append(jnp.where(lane < width, left, pltpu.roll(right, width, 1)))
        bottom.append(jnp.where(lane < width, pltpu.roll(left, width, 1), right))
    coarse = jnp.concatenate([jnp.concatenate(top, axis=1), jnp.concatenate(bottom, axis=1)], axis=0)
    out_ref[...] = total + fold3(dot(split3(coarse), hot_ref[...]))


def whole(space=pltpu.VMEM):
    return pl.BlockSpec(memory_space=space)


def limit(mib):
    return pltpu.CompilerParams(vmem_limit_bytes=mib * MIB)


def in_hbm(x):
    return pltpu.with_memory_space_constraint(x, pltpu.HBM)


def weight(flops):
    return pl.CostEstimate(flops=flops, bytes_accessed=0, transcendentals=0)


def on_device(residual, fine_inverse, coarse_inverse, wanted_rows, wanted_count, aggregate):
    subs = lax.axis_size("sub")
    shards = lax.axis_size("blk")
    rows, cols = residual.shape
    tiles = cols // LANES
    margin = wanted_rows.shape[2]
    coarse_len = coarse_inverse.shape[0]
    width = coarse_len // shards
    packed_rows = -(-(rows * tiles + tiles) // 8) * 8
    inner = [(i, i + 1) for i in range(0, subs, 2)] + [(i + 1, i) for i in range(0, subs, 2)]
    outer = [(i, i + 1) for i in range(1, subs - 1, 2)] + [(i + 1, i) for i in range(1, subs - 1, 2)]
    codes = in_hbm(aggregate[None])
    table = coarse_inverse.reshape(-1, LANES)

    packed, table = pl.pallas_call(
        pack_kernel,
        out_shape=(
            jax.ShapeDtypeStruct((shards, packed_rows, LANES), F32),
            jax.ShapeDtypeStruct(table.shape, F32),
        ),
        in_specs=[whole(pl.ANY)] * 3,
        out_specs=(whole(), whole()),
        scratch_shapes=[
            pltpu.VMEM(residual.shape, F32),
            pltpu.VMEM(codes.shape, jnp.int32),
            pltpu.SemaphoreType.DMA((3,)),
        ],
        compiler_params=limit(4),
        name="pack",
    )(in_hbm(residual), codes, in_hbm(table))
    own = lax.all_to_all(packed, "blk", 0, 0, tiled=True)
    lists = lax.ppermute(wanted_rows[0], "sub", outer)

    send = pl.pallas_call(
        functools.partial(coarse_kernel, width, rows, tiles),
        out_shape=jax.ShapeDtypeStruct((subs, shards, rows // 2, LANES), F32),
        in_specs=[whole()] * 2,
        out_specs=whole(),
        compiler_params=limit(12),
        cost_estimate=weight(8 * 10**9),
        name="coarse",
    )(own, table)
    flat = send.reshape((subs * shards,) + send.shape[2:])
    got = lax.all_to_all(flat, ("sub", "blk"), 0, 0, tiled=True).reshape(send.shape)

    outgoing = pl.pallas_call(
        functools.partial(outer_kernel, rows, tiles),
        out_shape=jax.ShapeDtypeStruct((rows, margin), F32),
        in_specs=[whole(), whole()],
        out_specs=whole(),
        compiler_params=limit(8),
        name="outer",
    )(own, lists)
    halo = lax.ppermute(outgoing, "sub", outer)
    other = lax.ppermute(own, "sub", inner)

    owned, w_hi, w_low, hot = pl.pallas_call(
        functools.partial(own_kernel, rows, tiles, margin),
        out_shape=(
            jax.ShapeDtypeStruct((rows, cols), F32),
            jax.ShapeDtypeStruct((2, margin, cols), BF16),
            jax.ShapeDtypeStruct((2, margin, cols), BF16),
            jax.ShapeDtypeStruct((coarse_len, cols), BF16),
        ),
        in_specs=[whole(), whole(pl.ANY), whole(pl.ANY)],
        out_specs=(whole(),) * 4,
        scratch_shapes=[
            pltpu.VMEM(fine_inverse.shape[1:], F32),
            pltpu.VMEM(codes.shape, jnp.int32),
            pltpu.SemaphoreType.DMA((shards + 3,)),
        ],
        compiler_params=limit(16),
        cost_estimate=weight(40 * 10**9),
        name="owned",
    )(own, codes, in_hbm(fine_inverse))

    fine = pl.pallas_call(
        functools.partial(inner_kernel, rows, tiles),
        out_shape=jax.ShapeDtypeStruct((rows, cols), F32),
        in_specs=[whole(pltpu.SMEM)] + [whole()] * 5,
        out_specs=whole(),
        compiler_params=limit(8),
        name="inner",
    )(wanted_count, other, wanted_rows[0], w_hi, w_low, owned)

    return pl.pallas_call(
        functools.partial(tail_kernel, width),
        out_shape=jax.ShapeDtypeStruct((rows, cols), F32),
        in_specs=[whole(pltpu.SMEM)] + [whole()] * 6,
        out_specs=whole(),
        compiler_params=limit(12),
        name="tail",
    )(wanted_count, got, halo, w_hi, w_low, hot, fine)


def solution(mesh):
    in_specs = (
        P(None, ("sub", "blk")),
        P("sub", None, "blk"),
        P("sub", "blk", None),
        P("sub", None, None),
        P("sub", None),
        P(("sub", "blk")),
    )
    out_specs = P(None, ("sub", "blk"))
    return jax.shard_map(
        on_device, mesh=mesh, in_specs=in_specs, out_specs=out_specs, check_vma=False
    )
```

```python
import functools

import jax
import jax.numpy as jnp
from jax import lax
from jax.experimental import pallas as pl
from jax.experimental.pallas import tpu as pltpu
from jax.sharding import PartitionSpec as P

BF16 = jnp.bfloat16
F32 = jnp.float32
NN = (((1,), (0,)), ((), ()))
NT = (((1,), (1,)), ((), ()))
LANES = 128
MIB = 1 << 20


def split3(x):
    hi = x.astype(BF16)
    rest = x - hi.astype(F32)
    mid = rest.astype(BF16)
    low = (rest - mid.astype(F32)).astype(BF16)
    return jnp.concatenate([hi, mid, low], axis=0)


def split2(x):
    hi = x.astype(BF16)
    low = (x - hi.astype(F32)).astype(BF16)
    return hi, low


def dot(a, b, dims=NN):
    return lax.dot_general(a, b, dims, preferred_element_type=F32)


def dot_halves(x, w_hi, w_low):
    rows = x.shape[0]
    x_hi, x_low = split2(x)
    both = dot(jnp.concatenate([x_hi, x_low], axis=0), w_hi)
    return both[:rows] + both[rows:] + dot(x_hi, w_low)


def fold3(acc):
    rows = acc.shape[0] // 3
    return acc[:rows] + acc[rows : 2 * rows] + acc[2 * rows :]


def onehot(condition):
    return condition.astype(F32).astype(BF16)


def shard_rows(ref, shard, rows, tiles):
    return jnp.concatenate([ref[shard, pl.ds(t * rows, rows)] for t in range(tiles)], axis=1)


def pick(ref, rows, tiles, wanted):
    cols = tiles * LANES
    local = lax.broadcasted_iota(jnp.int32, (cols, wanted.shape[1]), 0)
    total = jnp.zeros((3 * rows, wanted.shape[1]), F32)
    for shard in range(ref.shape[0]):
        block = split3(shard_rows(ref, shard, rows, tiles))
        total = total + dot(block, onehot(local == wanted - shard * cols))
    return fold3(total)


def parity():
    return lax.rem(lax.axis_index("sub"), 2)


def pack_kernel(
    residual_ref, agg_ref, lists_ref, counts_ref, coarse_ref,
    out_ref, lists_out, coarse_out,
    residual_buf, agg_buf, lists_buf, counts_buf, packed_buf, sems,
):
    sources = (residual_ref, agg_ref, lists_ref, counts_ref, coarse_ref)
    targets = (residual_buf, agg_buf, lists_buf, counts_buf, coarse_out)
    fetches = [pltpu.make_async_copy(a, b, sems.at[k]) for k, (a, b) in enumerate(zip(sources, targets))]
    for fetch in fetches:
        fetch.start()
    rows, cols = residual_buf.shape
    tiles = cols // LANES
    fetches[0].wait()
    for t in range(tiles):
        packed_buf[t * rows : (t + 1) * rows] = residual_buf[:, t * LANES : (t + 1) * LANES]
    fetches[1].wait()
    codes = [agg_buf[:, t * LANES : (t + 1) * LANES].astype(F32) for t in range(tiles)]
    codes.append(jnp.zeros((packed_buf.shape[0] - rows * tiles - tiles, LANES), F32))
    packed_buf[rows * tiles :] = jnp.concatenate(codes, axis=0)
    sends = []
    for k in range(out_ref.shape[0]):
        sends.append(pltpu.make_async_copy(packed_buf, out_ref.at[k], sems.at[len(fetches) + k]))
        sends[k].start()
    fetches[2].wait()
    fetches[3].wait()
    slots = lax.broadcasted_iota(jnp.int32, (1, lists_buf.shape[1]), 1)
    for side in range(2):
        used = slots < counts_buf[:, side : side + 1]
        lists_out[side : side + 1] = jnp.where(used, lists_buf[side : side + 1], -1)
    fetches[4].wait()
    for send in sends:
        send.wait()


def coarse_kernel(width, rows, tiles, own_ref, coarse_ref, send_ref, chunk_buf, sems):
    shards = own_ref.shape[0]
    cols = tiles * LANES
    coarse_len = width * shards
    levels = lax.broadcasted_iota(jnp.int32, (coarse_len, cols), 0)
    rhs = jnp.zeros((3 * rows, coarse_len), F32)
    for shard in range(shards):
        block = split3(shard_rows(own_ref, shard, rows, tiles))
        codes = [own_ref[shard, pl.ds(tiles * rows + t, 1)] for t in range(tiles)]
        unknowns = jnp.concatenate(codes, axis=1).astype(jnp.int32)
        rhs = rhs + dot(block, onehot(levels == unknowns), NT)
    rhs = fold3(rhs)
    half = rows // 2
    lane = lax.broadcasted_iota(jnp.int32, (half, LANES), 1)
    stride = coarse_ref.shape[0] // coarse_len
    sends = []
    for tile in range(0, stride, 2):
        parts = [coarse_ref[pl.ds(tile + k, coarse_len, stride=stride), :] for k in range(2)]
        value = dot_halves(rhs, *split2(jnp.concatenate(parts, axis=1)))
        for k in range(2):
            part = value[:, k * LANES : (k + 1) * LANES]
            turned = pltpu.roll(part, width, 1)
            chunk_buf[2 * (tile + k)] = jnp.where(lane < width, part[:half], turned[half:])
            chunk_buf[2 * (tile + k) + 1] = jnp.where(lane < width, turned[:half], part[half:])
        ready = pl.ds(2 * tile, 4)
        for copy in range(shards):
            send = pltpu.make_async_copy(
                chunk_buf.at[ready], send_ref.at[ready, copy], sems.at[len(sends)]
            )
            send.start()
            sends.append(send)
    for send in sends:
        send.wait()


def margin_kernel(rows, tiles, own_ref, outer_lists_ref, inner_lists_ref, outer_ref, inner_ref):
    odd = parity()
    wanted = jnp.where(odd == 1, outer_lists_ref[0:1], outer_lists_ref[1:2])
    outer_ref[...] = pick(own_ref, rows, tiles, wanted)
    wanted = jnp.where(odd == 1, inner_lists_ref[1:2], inner_lists_ref[0:1])
    inner_ref[...] = pick(own_ref, rows, tiles, wanted)


def own_kernel(
    rows, tiles, margin, own_ref, agg_ref, fine_ref, out_ref, hi_ref, low_ref, hot_ref, agg_buf, fine_buf, sems
):
    shards = own_ref.shape[0]
    ext = fine_ref.shape[1]
    step = 2 * LANES
    starts = list(range(margin, ext - margin, step)) + [0, ext - margin]
    sizes = [step] * (len(starts) - 2) + [margin] * 2
    fetch = pltpu.make_async_copy(agg_ref, agg_buf, sems.at[len(starts)])
    fetch.start()
    copies = []
    for k, (start, size) in enumerate(zip(starts, sizes)):
        copies.append(
            pltpu.make_async_copy(
                fine_ref.at[0, pl.ds(start, size)], fine_buf.at[pl.ds(start, size)], sems.at[k]
            )
        )
        copies[k].start()
    fetch.wait()
    levels = lax.broadcasted_iota(jnp.int32, hot_ref.shape, 0)
    hot_ref[...] = onehot(levels == agg_buf[...])
    total = jnp.zeros(out_ref.shape, F32)
    for k, start in enumerate(starts[:-2]):
        shard, tile = divmod(2 * k, tiles)
        block = jnp.concatenate([own_ref[shard, pl.ds((tile + t) * rows, rows)] for t in range(2)], axis=1)
        copies[k].wait()
        total = total + dot_halves(block, *split2(fine_buf[start : start + step]))
    out_ref[...] = total
    for side in range(2):
        start = starts[side - 2]
        copies[side - 2].wait()
        hi_ref[side], low_ref[side] = split2(fine_buf[start : start + margin])


def tail_kernel(width, got_ref, outer_ref, inner_ref, hi_ref, low_ref, hot_ref, total_ref, out_ref):
    subs, shards, half, _ = got_ref.shape
    odd = parity()
    outer, inner = outer_ref[...], inner_ref[...]
    total = total_ref[...]
    total = total + dot_halves(jnp.where(odd == 1, inner, outer), hi_ref[0], low_ref[0])
    total = total + dot_halves(jnp.where(odd == 1, outer, inner), hi_ref[1], low_ref[1])
    sums = [got_ref[0, shard] for shard in range(shards)]
    for sub in range(1, subs):
        for shard in range(shards):
            sums[shard] = sums[shard] + got_ref[sub, shard]
    lane = lax.broadcasted_iota(jnp.int32, (half, LANES), 1)
    top, bottom = [], []
    for pair in range(shards // 2):
        left, right = sums[2 * pair], sums[2 * pair + 1]
        top.append(jnp.where(lane < width, left, pltpu.roll(right, width, 1)))
        bottom.append(jnp.where(lane < width, pltpu.roll(left, width, 1), right))
    coarse = jnp.concatenate([jnp.concatenate(top, axis=1), jnp.concatenate(bottom, axis=1)], axis=0)
    out_ref[...] = total + fold3(dot(split3(coarse), hot_ref[...]))


def whole(space=pltpu.VMEM):
    return pl.BlockSpec(memory_space=space)


def limit(mib):
    return pltpu.CompilerParams(vmem_limit_bytes=mib * MIB)


def in_hbm(x):
    return pltpu.with_memory_space_constraint(x, pltpu.HBM)


def weight(flops):
    return pl.CostEstimate(flops=flops, bytes_accessed=0, transcendentals=0)


def on_device(residual, fine_inverse, coarse_inverse, wanted_rows, wanted_count, aggregate):
    subs = lax.axis_size("sub")
    shards = lax.axis_size("blk")
    rows, cols = residual.shape
    tiles = cols // LANES
    margin = wanted_rows.shape[2]
    coarse_len = coarse_inverse.shape[0]
    width = coarse_len // shards
    packed_rows = -(-(rows * tiles + tiles) // 8) * 8
    inner = [(i, i + 1) for i in range(0, subs, 2)] + [(i + 1, i) for i in range(0, subs, 2)]
    outer = [(i, i + 1) for i in range(1, subs - 1, 2)] + [(i + 1, i) for i in range(1, subs - 1, 2)]
    codes = aggregate[None]
    lists = wanted_rows[0]
    table = coarse_inverse.reshape(-1, LANES)
    packed_shape = (packed_rows, LANES)

    packed, lists, table = pl.pallas_call(
        pack_kernel,
        out_shape=(
            jax.ShapeDtypeStruct((shards,) + packed_shape, F32),
            jax.ShapeDtypeStruct(lists.shape, jnp.int32),
            jax.ShapeDtypeStruct(table.shape, F32),
        ),
        in_specs=[whole(pl.ANY)] * 5,
        out_specs=(whole(pl.ANY), whole(), whole()),
        scratch_shapes=[
            pltpu.VMEM(residual.shape, F32),
            pltpu.VMEM(codes.shape, jnp.int32),
            pltpu.VMEM(lists.shape, jnp.int32),
            pltpu.VMEM(wanted_count.shape, jnp.int32),
            pltpu.VMEM(packed_shape, F32),
            pltpu.SemaphoreType.DMA((5 + shards,)),
        ],
        compiler_params=limit(4),
        name="pack",
    )(in_hbm(residual), in_hbm(codes), in_hbm(lists), in_hbm(wanted_count), in_hbm(table))
    own = lax.all_to_all(packed, "blk", 0, 0, tiled=True)
    outer_lists = lax.ppermute(lists, "sub", outer)
    inner_lists = lax.ppermute(lists, "sub", inner)

    send = pl.pallas_call(
        functools.partial(coarse_kernel, width, rows, tiles),
        out_shape=jax.ShapeDtypeStruct((subs, shards, rows // 2, LANES), F32),
        in_specs=[whole()] * 2,
        out_specs=whole(pl.ANY),
        scratch_shapes=[
            pltpu.VMEM((subs, rows // 2, LANES), F32),
            pltpu.SemaphoreType.DMA((shards * subs // 4,)),
        ],
        compiler_params=limit(12),
        cost_estimate=weight(8 * 10**9),
        name="coarse",
    )(own, table)
    flat = send.reshape((subs * shards,) + send.shape[2:])
    got = lax.all_to_all(flat, ("sub", "blk"), 0, 0, tiled=True).reshape(send.shape)

    outgoing, ingoing = pl.pallas_call(
        functools.partial(margin_kernel, rows, tiles),
        out_shape=(jax.ShapeDtypeStruct((rows, margin), F32),) * 2,
        in_specs=[whole()] * 3,
        out_specs=(whole(), whole()),
        compiler_params=limit(8),
        cost_estimate=weight(4 * 10**9),
        name="margins",
    )(own, outer_lists, inner_lists)
    outer_halo = lax.ppermute(outgoing, "sub", outer)
    inner_halo = lax.ppermute(ingoing, "sub", inner)

    owned, w_hi, w_low, hot = pl.pallas_call(
        functools.partial(own_kernel, rows, tiles, margin),
        out_shape=(
            jax.ShapeDtypeStruct((rows, cols), F32),
            jax.ShapeDtypeStruct((2, margin, cols), BF16),
            jax.ShapeDtypeStruct((2, margin, cols), BF16),
            jax.ShapeDtypeStruct((coarse_len, cols), BF16),
        ),
        in_specs=[whole(), whole(pl.ANY), whole(pl.ANY)],
        out_specs=(whole(),) * 4,
        scratch_shapes=[
            pltpu.VMEM(codes.shape, jnp.int32),
            pltpu.VMEM(fine_inverse.shape[1:], F32),
            pltpu.SemaphoreType.DMA((shards * tiles // 2 + 3,)),
        ],
        compiler_params=limit(16),
        cost_estimate=weight(40 * 10**9),
        name="owned",
    )(own, in_hbm(codes), in_hbm(fine_inverse))

    return pl.pallas_call(
        functools.partial(tail_kernel, width),
        out_shape=jax.ShapeDtypeStruct((rows, cols), F32),
        in_specs=[whole()] * 7,
        out_specs=whole(),
        compiler_params=limit(12),
        name="tail",
    )(got, outer_halo, inner_halo, w_hi, w_low, hot, owned)


def solution(mesh):
    in_specs = (
        P(None, ("sub", "blk")),
        P("sub", None, "blk"),
        P("sub", "blk", None),
        P("sub", None, None),
        P("sub", None),
        P(("sub", "blk")),
    )
    out_specs = P(None, ("sub", "blk"))
    return jax.shard_map(
        on_device, mesh=mesh, in_specs=in_specs, out_specs=out_specs, check_vma=False
    )
```

```python
import functools

import jax
import jax.numpy as jnp
from jax import lax
from jax.experimental import pallas as pl
from jax.experimental.pallas import tpu as pltpu
from jax.sharding import PartitionSpec as P

BF16 = jnp.bfloat16
F32 = jnp.float32
NN = (((1,), (0,)), ((), ()))
NT = (((1,), (1,)), ((), ()))
LANES = 128
MIB = 1 << 20


def split3(x):
    hi = x.astype(BF16)
    rest = x - hi.astype(F32)
    mid = rest.astype(BF16)
    low = (rest - mid.astype(F32)).astype(BF16)
    return jnp.concatenate([hi, mid, low], axis=0)


def split2(x):
    hi = x.astype(BF16)
    low = (x - hi.astype(F32)).astype(BF16)
    return hi, low


def dot(a, b, dims=NN):
    return lax.dot_general(a, b, dims, preferred_element_type=F32)


def dot_halves(x, w_hi, w_low):
    rows = x.shape[0]
    x_hi, x_low = split2(x)
    both = dot(jnp.concatenate([x_hi, x_low], axis=0), w_hi)
    return both[:rows] + both[rows:] + dot(x_hi, w_low)


def fold3(acc):
    rows = acc.shape[0] // 3
    return acc[:rows] + acc[rows : 2 * rows] + acc[2 * rows :]


def onehot(condition):
    return condition.astype(F32).astype(BF16)


def shard_rows(ref, shard, rows, tiles):
    return jnp.concatenate([ref[shard, pl.ds(t * rows, rows)] for t in range(tiles)], axis=1)


def pick(ref, rows, tiles, wanted):
    cols = tiles * LANES
    local = lax.broadcasted_iota(jnp.int32, (cols, wanted.shape[1]), 0)
    total = jnp.zeros((3 * rows, wanted.shape[1]), F32)
    for shard in range(ref.shape[0]):
        block = split3(shard_rows(ref, shard, rows, tiles))
        total = total + dot(block, onehot(local == wanted - shard * cols))
    return fold3(total)


def parity():
    return lax.rem(lax.axis_index("sub"), 2)


def pack_kernel(
    residual_ref, agg_ref, lists_ref, counts_ref, coarse_ref,
    out_ref, lists_out, coarse_out,
    residual_buf, agg_buf, lists_buf, counts_buf, packed_buf, sems,
):
    sources = (residual_ref, agg_ref, lists_ref, counts_ref, coarse_ref)
    targets = (residual_buf, agg_buf, lists_buf, counts_buf, coarse_out)
    fetches = [pltpu.make_async_copy(a, b, sems.at[k]) for k, (a, b) in enumerate(zip(sources, targets))]
    for fetch in fetches:
        fetch.start()
    rows, cols = residual_buf.shape
    tiles = cols // LANES
    fetches[0].wait()
    for t in range(tiles):
        packed_buf[t * rows : (t + 1) * rows] = residual_buf[:, t * LANES : (t + 1) * LANES]
    fetches[1].wait()
    codes = [agg_buf[:, t * LANES : (t + 1) * LANES].astype(F32) for t in range(tiles)]
    codes.append(jnp.zeros((packed_buf.shape[0] - rows * tiles - tiles, LANES), F32))
    packed_buf[rows * tiles :] = jnp.concatenate(codes, axis=0)
    sends = []
    for k in range(out_ref.shape[0]):
        sends.append(pltpu.make_async_copy(packed_buf, out_ref.at[k], sems.at[len(fetches) + k]))
        sends[k].start()
    fetches[2].wait()
    fetches[3].wait()
    slots = lax.broadcasted_iota(jnp.int32, (1, lists_buf.shape[1]), 1)
    for side in range(2):
        used = slots < counts_buf[:, side : side + 1]
        lists_out[side : side + 1] = jnp.where(used, lists_buf[side : side + 1], -1)
    fetches[4].wait()
    for send in sends:
        send.wait()


def coarse_kernel(width, rows, tiles, slots, own_ref, coarse_ref, send_ref, chunk_buf, sems):
    shards = own_ref.shape[0]
    cols = tiles * LANES
    coarse_len = width * shards
    levels = lax.broadcasted_iota(jnp.int32, (coarse_len, cols), 0)
    rhs = jnp.zeros((3 * rows, coarse_len), F32)
    for shard in range(shards):
        block = split3(shard_rows(own_ref, shard, rows, tiles))
        codes = [own_ref[shard, pl.ds(tiles * rows + t, 1)] for t in range(tiles)]
        unknowns = jnp.concatenate(codes, axis=1).astype(jnp.int32)
        rhs = rhs + dot(block, onehot(levels == unknowns), NT)
    rhs = fold3(rhs)
    half = rows // 2
    lane = lax.broadcasted_iota(jnp.int32, (half, LANES), 1)
    stride = coarse_ref.shape[0] // coarse_len
    sends = []
    for tile in range(0, stride, 2):
        parts = [coarse_ref[pl.ds(tile + k, coarse_len, stride=stride), :] for k in range(2)]
        value = dot_halves(rhs, *split2(jnp.concatenate(parts, axis=1)))
        for k in range(2):
            part = value[:, k * LANES : (k + 1) * LANES]
            turned = pltpu.roll(part, width, 1)
            chunk_buf[2 * (tile + k)] = jnp.where(lane < width, part[:half], turned[half:])
            chunk_buf[2 * (tile + k) + 1] = jnp.where(lane < width, turned[:half], part[half:])
        for sub in range(2 * tile, 2 * tile + 4):
            for copy in range(shards):
                send = pltpu.make_async_copy(
                    chunk_buf.at[sub], send_ref.at[slots[sub], copy], sems.at[len(sends)]
                )
                send.start()
                sends.append(send)
    for send in sends:
        send.wait()


def margin_kernel(rows, tiles, own_ref, outer_lists_ref, inner_lists_ref, outer_ref, inner_ref):
    odd = parity()
    wanted = jnp.where(odd == 1, outer_lists_ref[0:1], outer_lists_ref[1:2])
    outer_ref[...] = pick(own_ref, rows, tiles, wanted)
    wanted = jnp.where(odd == 1, inner_lists_ref[1:2], inner_lists_ref[0:1])
    inner_ref[...] = pick(own_ref, rows, tiles, wanted)


def own_kernel(
    rows, tiles, margin, own_ref, agg_ref, fine_ref, out_ref, hi_ref, low_ref, hot_ref, agg_buf, fine_buf, sems
):
    shards = own_ref.shape[0]
    ext = fine_ref.shape[1]
    step = 2 * LANES
    starts = list(range(margin, ext - margin, step)) + [0, ext - margin]
    sizes = [step] * (len(starts) - 2) + [margin] * 2
    fetch = pltpu.make_async_copy(agg_ref, agg_buf, sems.at[len(starts)])
    fetch.start()
    copies = []
    for k, (start, size) in enumerate(zip(starts, sizes)):
        copies.append(
            pltpu.make_async_copy(
                fine_ref.at[0, pl.ds(start, size)], fine_buf.at[pl.ds(start, size)], sems.at[k]
            )
        )
        copies[k].start()
    fetch.wait()
    levels = lax.broadcasted_iota(jnp.int32, hot_ref.shape, 0)
    hot_ref[...] = onehot(levels == agg_buf[...])
    total = jnp.zeros(out_ref.shape, F32)
    for k, start in enumerate(starts[:-2]):
        shard, tile = divmod(2 * k, tiles)
        block = jnp.concatenate([own_ref[shard, pl.ds((tile + t) * rows, rows)] for t in range(2)], axis=1)
        copies[k].wait()
        total = total + dot_halves(block, *split2(fine_buf[start : start + step]))
    out_ref[...] = total
    for side in range(2):
        start = starts[side - 2]
        copies[side - 2].wait()
        hi_ref[side], low_ref[side] = split2(fine_buf[start : start + margin])


def tail_kernel(width, got_ref, outer_ref, inner_ref, hi_ref, low_ref, hot_ref, total_ref, out_ref):
    subs, shards, half, _ = got_ref.shape
    odd = parity()
    outer, inner = outer_ref[...], inner_ref[...]
    total = total_ref[...]
    total = total + dot_halves(jnp.where(odd == 1, inner, outer), hi_ref[0], low_ref[0])
    total = total + dot_halves(jnp.where(odd == 1, outer, inner), hi_ref[1], low_ref[1])
    sums = [got_ref[0, shard] for shard in range(shards)]
    for sub in range(1, subs):
        for shard in range(shards):
            sums[shard] = sums[shard] + got_ref[sub, shard]
    lane = lax.broadcasted_iota(jnp.int32, (half, LANES), 1)
    top, bottom = [], []
    for pair in range(shards // 2):
        left, right = sums[2 * pair], sums[2 * pair + 1]
        top.append(jnp.where(lane < width, left, pltpu.roll(right, width, 1)))
        bottom.append(jnp.where(lane < width, pltpu.roll(left, width, 1), right))
    coarse = jnp.concatenate([jnp.concatenate(top, axis=1), jnp.concatenate(bottom, axis=1)], axis=0)
    out_ref[...] = total + fold3(dot(split3(coarse), hot_ref[...]))


def whole(space=pltpu.VMEM):
    return pl.BlockSpec(memory_space=space)


def limit(mib):
    return pltpu.CompilerParams(vmem_limit_bytes=mib * MIB)


def in_hbm(x):
    return pltpu.with_memory_space_constraint(x, pltpu.HBM)


def weight(flops):
    return pl.CostEstimate(flops=flops, bytes_accessed=0, transcendentals=0)


def on_device(residual, fine_inverse, coarse_inverse, wanted_rows, wanted_count, aggregate):
    subs = lax.axis_size("sub")
    shards = lax.axis_size("blk")
    rows, cols = residual.shape
    tiles = cols // LANES
    margin = wanted_rows.shape[2]
    coarse_len = coarse_inverse.shape[0]
    width = coarse_len // shards
    packed_rows = -(-(rows * tiles + tiles) // 8) * 8
    inner = [(i, i + 1) for i in range(0, subs, 2)] + [(i + 1, i) for i in range(0, subs, 2)]
    outer = [(i, i + 1) for i in range(1, subs - 1, 2)] + [(i + 1, i) for i in range(1, subs - 1, 2)]
    receivers = [sub for k in range(subs // 2) for sub in (k, subs - 1 - k)]
    slots = [receivers.index(sub) for sub in range(subs)]
    codes = aggregate[None]
    lists = wanted_rows[0]
    table = coarse_inverse.reshape(-1, LANES)
    packed_shape = (packed_rows, LANES)

    packed, lists, table = pl.pallas_call(
        pack_kernel,
        out_shape=(
            jax.ShapeDtypeStruct((shards,) + packed_shape, F32),
            jax.ShapeDtypeStruct(lists.shape, jnp.int32),
            jax.ShapeDtypeStruct(table.shape, F32),
        ),
        in_specs=[whole(pl.ANY)] * 5,
        out_specs=(whole(pl.ANY), whole(), whole()),
        scratch_shapes=[
            pltpu.VMEM(residual.shape, F32),
            pltpu.VMEM(codes.shape, jnp.int32),
            pltpu.VMEM(lists.shape, jnp.int32),
            pltpu.VMEM(wanted_count.shape, jnp.int32),
            pltpu.VMEM(packed_shape, F32),
            pltpu.SemaphoreType.DMA((5 + shards,)),
        ],
        compiler_params=limit(4),
        name="pack",
    )(in_hbm(residual), in_hbm(codes), in_hbm(lists), in_hbm(wanted_count), in_hbm(table))
    own = lax.all_to_all(packed, "blk", 0, 0, tiled=True)
    outer_lists = lax.ppermute(lists, "sub", outer)
    inner_lists = lax.ppermute(lists, "sub", inner)

    send = pl.pallas_call(
        functools.partial(coarse_kernel, width, rows, tiles, slots),
        out_shape=jax.ShapeDtypeStruct((subs, shards, rows // 2, LANES), F32),
        in_specs=[whole()] * 2,
        out_specs=whole(pl.ANY),
        scratch_shapes=[
            pltpu.VMEM((subs, rows // 2, LANES), F32),
            pltpu.SemaphoreType.DMA((shards * subs,)),
        ],
        compiler_params=limit(12),
        cost_estimate=weight(8 * 10**9),
        name="coarse",
    )(own, table)
    flat = send.reshape((subs * shards,) + send.shape[2:])
    members = [sub * shards + shard for sub in receivers for shard in range(shards)]
    got = lax.all_to_all(flat, ("sub", "blk"), 0, 0, axis_index_groups=[members], tiled=True)
    got = got.reshape(send.shape)

    outgoing, ingoing = pl.pallas_call(
        functools.partial(margin_kernel, rows, tiles),
        out_shape=(jax.ShapeDtypeStruct((rows, margin), F32),) * 2,
        in_specs=[whole()] * 3,
        out_specs=(whole(), whole()),
        compiler_params=limit(8),
        cost_estimate=weight(4 * 10**9),
        name="margins",
    )(own, outer_lists, inner_lists)
    outer_halo = lax.ppermute(outgoing, "sub", outer)
    inner_halo = lax.ppermute(ingoing, "sub", inner)

    owned, w_hi, w_low, hot = pl.pallas_call(
        functools.partial(own_kernel, rows, tiles, margin),
        out_shape=(
            jax.ShapeDtypeStruct((rows, cols), F32),
            jax.ShapeDtypeStruct((2, margin, cols), BF16),
            jax.ShapeDtypeStruct((2, margin, cols), BF16),
            jax.ShapeDtypeStruct((coarse_len, cols), BF16),
        ),
        in_specs=[whole(), whole(pl.ANY), whole(pl.ANY)],
        out_specs=(whole(),) * 4,
        scratch_shapes=[
            pltpu.VMEM(codes.shape, jnp.int32),
            pltpu.VMEM(fine_inverse.shape[1:], F32),
            pltpu.SemaphoreType.DMA((shards * tiles // 2 + 3,)),
        ],
        compiler_params=limit(16),
        cost_estimate=weight(40 * 10**9),
        name="owned",
    )(own, in_hbm(codes), in_hbm(fine_inverse))

    return pl.pallas_call(
        functools.partial(tail_kernel, width),
        out_shape=jax.ShapeDtypeStruct((rows, cols), F32),
        in_specs=[whole()] * 7,
        out_specs=whole(),
        compiler_params=limit(12),
        name="tail",
    )(got, outer_halo, inner_halo, w_hi, w_low, hot, owned)


def solution(mesh):
    in_specs = (
        P(None, ("sub", "blk")),
        P("sub", None, "blk"),
        P("sub", "blk", None),
        P("sub", None, None),
        P("sub", None),
        P(("sub", "blk")),
    )
    out_specs = P(None, ("sub", "blk"))
    return jax.shard_map(
        on_device, mesh=mesh, in_specs=in_specs, out_specs=out_specs, check_vma=False
    )
```

```python
import functools

import jax
import jax.numpy as jnp
from jax import lax
from jax.experimental import pallas as pl
from jax.experimental.pallas import tpu as pltpu
from jax.sharding import PartitionSpec as P

BF16 = jnp.bfloat16
F32 = jnp.float32
NN = (((1,), (0,)), ((), ()))
NT = (((1,), (1,)), ((), ()))
LANES = 128
MIB = 1 << 20


def split3(x):
    hi = x.astype(BF16)
    rest = x - hi.astype(F32)
    mid = rest.astype(BF16)
    low = (rest - mid.astype(F32)).astype(BF16)
    return jnp.concatenate([hi, mid, low], axis=0)


def split2(x):
    hi = x.astype(BF16)
    low = (x - hi.astype(F32)).astype(BF16)
    return hi, low


def dot(a, b, dims=NN):
    return lax.dot_general(a, b, dims, preferred_element_type=F32)


def dot_halves(x, w_hi, w_low):
    rows = x.shape[0]
    x_hi, x_low = split2(x)
    both = dot(jnp.concatenate([x_hi, x_low], axis=0), w_hi)
    return both[:rows] + both[rows:] + dot(x_hi, w_low)


def fold3(acc):
    rows = acc.shape[0] // 3
    return acc[:rows] + acc[rows : 2 * rows] + acc[2 * rows :]


def onehot(condition):
    return condition.astype(F32).astype(BF16)


def shard_rows(ref, shard, rows, tiles):
    return jnp.concatenate([ref[shard, pl.ds(t * rows, rows)] for t in range(tiles)], axis=1)


def pick(ref, rows, tiles, wanted):
    cols = tiles * LANES
    local = lax.broadcasted_iota(jnp.int32, (cols, wanted.shape[1]), 0)
    total = jnp.zeros((3 * rows, wanted.shape[1]), F32)
    for shard in range(ref.shape[0]):
        block = split3(shard_rows(ref, shard, rows, tiles))
        total = total + dot(block, onehot(local == wanted - shard * cols))
    return fold3(total)


def parity():
    return lax.rem(lax.axis_index("sub"), 2)


def pack_kernel(
    residual_ref, agg_ref, lists_ref, counts_ref, coarse_ref,
    out_ref, lists_out, coarse_out,
    residual_buf, agg_buf, lists_buf, counts_buf, sems,
):
    sources = (residual_ref, agg_ref, lists_ref, counts_ref, coarse_ref)
    targets = (residual_buf, agg_buf, lists_buf, counts_buf, coarse_out)
    fetches = [pltpu.make_async_copy(a, b, sems.at[k]) for k, (a, b) in enumerate(zip(sources, targets))]
    for fetch in fetches:
        fetch.start()
    rows, cols = residual_buf.shape
    tiles = cols // LANES
    fetches[0].wait()
    fetches[1].wait()
    codes = [agg_buf[:, t * LANES : (t + 1) * LANES].astype(F32) for t in range(tiles)]
    codes.append(jnp.zeros((out_ref.shape[1] - rows * tiles - tiles, LANES), F32))
    last = jnp.concatenate(codes, axis=0)
    for k in range(out_ref.shape[0]):
        for t in range(tiles):
            out_ref[k, t * rows : (t + 1) * rows] = residual_buf[:, t * LANES : (t + 1) * LANES]
        out_ref[k, rows * tiles :] = last
    fetches[2].wait()
    fetches[3].wait()
    slots = lax.broadcasted_iota(jnp.int32, (1, lists_buf.shape[1]), 1)
    for side in range(2):
        used = slots < counts_buf[:, side : side + 1]
        lists_out[side : side + 1] = jnp.where(used, lists_buf[side : side + 1], -1)
    fetches[4].wait()


def coarse_kernel(width, rows, tiles, own_ref, coarse_ref, send_ref):
    shards = own_ref.shape[0]
    cols = tiles * LANES
    coarse_len = width * shards
    levels = lax.broadcasted_iota(jnp.int32, (coarse_len, cols), 0)
    rhs = jnp.zeros((3 * rows, coarse_len), F32)
    for shard in range(shards):
        block = split3(shard_rows(own_ref, shard, rows, tiles))
        codes = [own_ref[shard, pl.ds(tiles * rows + t, 1)] for t in range(tiles)]
        unknowns = jnp.concatenate(codes, axis=1).astype(jnp.int32)
        rhs = rhs + dot(block, onehot(levels == unknowns), NT)
    rhs = fold3(rhs)
    half = rows // 2
    lane = lax.broadcasted_iota(jnp.int32, (half, LANES), 1)
    stride = coarse_ref.shape[0] // coarse_len
    for tile in range(0, stride, 2):
        parts = [coarse_ref[pl.ds(tile + k, coarse_len, stride=stride), :] for k in range(2)]
        value = dot_halves(rhs, *split2(jnp.concatenate(parts, axis=1)))
        for k in range(2):
            part = value[:, k * LANES : (k + 1) * LANES]
            turned = pltpu.roll(part, width, 1)
            left = jnp.where(lane < width, part[:half], turned[half:])
            right = jnp.where(lane < width, turned[:half], part[half:])
            for copy in range(shards):
                send_ref[2 * (tile + k), copy] = left
                send_ref[2 * (tile + k) + 1, copy] = right


def margin_kernel(rows, tiles, own_ref, outer_lists_ref, inner_lists_ref, outer_ref, inner_ref):
    odd = parity()
    wanted = jnp.where(odd == 1, outer_lists_ref[0:1], outer_lists_ref[1:2])
    outer_ref[...] = pick(own_ref, rows, tiles, wanted)
    wanted = jnp.where(odd == 1, inner_lists_ref[1:2], inner_lists_ref[0:1])
    inner_ref[...] = pick(own_ref, rows, tiles, wanted)


def own_kernel(
    rows, tiles, margin, own_ref, agg_ref, fine_ref, out_ref, hi_ref, low_ref, hot_ref, agg_buf, fine_buf, sems
):
    shards = own_ref.shape[0]
    ext = fine_ref.shape[1]
    step = 2 * LANES
    starts = list(range(margin, ext - margin, step)) + [0, ext - margin]
    sizes = [step] * (len(starts) - 2) + [margin] * 2
    fetch = pltpu.make_async_copy(agg_ref, agg_buf, sems.at[len(starts)])
    fetch.start()
    copies = []
    for k, (start, size) in enumerate(zip(starts, sizes)):
        copies.append(
            pltpu.make_async_copy(
                fine_ref.at[0, pl.ds(start, size)], fine_buf.at[pl.ds(start, size)], sems.at[k]
            )
        )
        copies[k].start()
    fetch.wait()
    levels = lax.broadcasted_iota(jnp.int32, hot_ref.shape, 0)
    hot_ref[...] = onehot(levels == agg_buf[...])
    total = jnp.zeros(out_ref.shape, F32)
    for k, start in enumerate(starts[:-2]):
        shard, tile = divmod(2 * k, tiles)
        block = jnp.concatenate([own_ref[shard, pl.ds((tile + t) * rows, rows)] for t in range(2)], axis=1)
        copies[k].wait()
        total = total + dot_halves(block, *split2(fine_buf[start : start + step]))
    out_ref[...] = total
    for side in range(2):
        start = starts[side - 2]
        copies[side - 2].wait()
        hi_ref[side], low_ref[side] = split2(fine_buf[start : start + margin])


def halo_kernel(outer_ref, inner_ref, hi_ref, low_ref, total_ref, out_ref):
    odd = parity()
    outer, inner = outer_ref[...], inner_ref[...]
    total = total_ref[...]
    total = total + dot_halves(jnp.where(odd == 1, inner, outer), hi_ref[0], low_ref[0])
    total = total + dot_halves(jnp.where(odd == 1, outer, inner), hi_ref[1], low_ref[1])
    out_ref[...] = total


def tail_kernel(width, got_ref, hot_ref, total_ref, out_ref):
    subs, shards, half, _ = got_ref.shape
    sums = [got_ref[0, shard] for shard in range(shards)]
    for sub in range(1, subs):
        for shard in range(shards):
            sums[shard] = sums[shard] + got_ref[sub, shard]
    lane = lax.broadcasted_iota(jnp.int32, (half, LANES), 1)
    top, bottom = [], []
    for pair in range(shards // 2):
        left, right = sums[2 * pair], sums[2 * pair + 1]
        top.append(jnp.where(lane < width, left, pltpu.roll(right, width, 1)))
        bottom.append(jnp.where(lane < width, pltpu.roll(left, width, 1), right))
    coarse = jnp.concatenate([jnp.concatenate(top, axis=1), jnp.concatenate(bottom, axis=1)], axis=0)
    out_ref[...] = total_ref[...] + fold3(dot(split3(coarse), hot_ref[...]))


def whole(space=pltpu.VMEM):
    return pl.BlockSpec(memory_space=space)


def limit(mib):
    return pltpu.CompilerParams(vmem_limit_bytes=mib * MIB)


def in_hbm(x):
    return pltpu.with_memory_space_constraint(x, pltpu.HBM)


def weight(flops):
    return pl.CostEstimate(flops=flops, bytes_accessed=0, transcendentals=0)


def on_device(residual, fine_inverse, coarse_inverse, wanted_rows, wanted_count, aggregate):
    subs = lax.axis_size("sub")
    shards = lax.axis_size("blk")
    rows, cols = residual.shape
    tiles = cols // LANES
    margin = wanted_rows.shape[2]
    coarse_len = coarse_inverse.shape[0]
    width = coarse_len // shards
    packed_rows = -(-(rows * tiles + tiles) // 8) * 8
    inner = [(i, i + 1) for i in range(0, subs, 2)] + [(i + 1, i) for i in range(0, subs, 2)]
    outer = [(i, i + 1) for i in range(1, subs - 1, 2)] + [(i + 1, i) for i in range(1, subs - 1, 2)]
    codes = aggregate[None]
    lists = wanted_rows[0]
    table = coarse_inverse.reshape(-1, LANES)
    packed_shape = (packed_rows, LANES)

    packed, lists, table = pl.pallas_call(
        pack_kernel,
        out_shape=(
            pltpu.VMEM((shards,) + packed_shape, F32),
            jax.ShapeDtypeStruct(lists.shape, jnp.int32),
            jax.ShapeDtypeStruct(table.shape, F32),
        ),
        in_specs=[whole(pl.ANY)] * 5,
        out_specs=(whole(), whole(), whole()),
        scratch_shapes=[
            pltpu.VMEM(residual.shape, F32),
            pltpu.VMEM(codes.shape, jnp.int32),
            pltpu.VMEM(lists.shape, jnp.int32),
            pltpu.VMEM(wanted_count.shape, jnp.int32),
            pltpu.SemaphoreType.DMA((5,)),
        ],
        compiler_params=limit(4),
        name="pack",
    )(in_hbm(residual), in_hbm(codes), in_hbm(lists), in_hbm(wanted_count), in_hbm(table))
    own = lax.all_to_all(packed, "blk", 0, 0, tiled=True)
    outer_lists = lax.ppermute(lists, "sub", outer)
    inner_lists = lax.ppermute(lists, "sub", inner)

    send = pl.pallas_call(
        functools.partial(coarse_kernel, width, rows, tiles),
        out_shape=pltpu.VMEM((subs, shards, rows // 2, LANES), F32),
        in_specs=[whole()] * 2,
        out_specs=whole(),
        compiler_params=limit(12),
        cost_estimate=weight(8 * 10**9),
        name="coarse",
    )(own, table)
    flat = send.reshape((subs * shards,) + send.shape[2:])
    got = lax.all_to_all(flat, ("sub", "blk"), 0, 0, tiled=True).reshape(send.shape)

    outgoing, ingoing = pl.pallas_call(
        functools.partial(margin_kernel, rows, tiles),
        out_shape=(jax.ShapeDtypeStruct((rows, margin), F32),) * 2,
        in_specs=[whole()] * 3,
        out_specs=(whole(), whole()),
        compiler_params=limit(8),
        cost_estimate=weight(4 * 10**9),
        name="margins",
    )(own, outer_lists, inner_lists)
    outer_halo = lax.ppermute(outgoing, "sub", outer)
    inner_halo = lax.ppermute(ingoing, "sub", inner)

    owned, w_hi, w_low, hot = pl.pallas_call(
        functools.partial(own_kernel, rows, tiles, margin),
        out_shape=(
            jax.ShapeDtypeStruct((rows, cols), F32),
            jax.ShapeDtypeStruct((2, margin, cols), BF16),
            jax.ShapeDtypeStruct((2, margin, cols), BF16),
            jax.ShapeDtypeStruct((coarse_len, cols), BF16),
        ),
        in_specs=[whole(), whole(pl.ANY), whole(pl.ANY)],
        out_specs=(whole(),) * 4,
        scratch_shapes=[
            pltpu.VMEM(codes.shape, jnp.int32),
            pltpu.VMEM(fine_inverse.shape[1:], F32),
            pltpu.SemaphoreType.DMA((shards * tiles // 2 + 3,)),
        ],
        compiler_params=limit(16),
        cost_estimate=weight(40 * 10**9),
        name="owned",
    )(own, in_hbm(codes), in_hbm(fine_inverse))

    fine = pl.pallas_call(
        halo_kernel,
        out_shape=jax.ShapeDtypeStruct((rows, cols), F32),
        in_specs=[whole()] * 5,
        out_specs=whole(),
        compiler_params=limit(12),
        cost_estimate=weight(4 * 10**9),
        name="halos",
    )(outer_halo, inner_halo, w_hi, w_low, owned)

    return pl.pallas_call(
        functools.partial(tail_kernel, width),
        out_shape=jax.ShapeDtypeStruct((rows, cols), F32),
        in_specs=[whole()] * 3,
        out_specs=whole(),
        compiler_params=limit(12),
        name="tail",
    )(got, hot, fine)


def solution(mesh):
    in_specs = (
        P(None, ("sub", "blk")),
        P("sub", None, "blk"),
        P("sub", "blk", None),
        P("sub", None, None),
        P("sub", None),
        P(("sub", "blk")),
    )
    out_specs = P(None, ("sub", "blk"))
    return jax.shard_map(
        on_device, mesh=mesh, in_specs=in_specs, out_specs=out_specs, check_vma=False
    )
```

```python
import functools

import jax
import jax.numpy as jnp
from jax import lax
from jax.experimental import pallas as pl
from jax.experimental.pallas import tpu as pltpu
from jax.sharding import PartitionSpec as P

BF16 = jnp.bfloat16
F32 = jnp.float32
NN = (((1,), (0,)), ((), ()))
NT = (((1,), (1,)), ((), ()))
LANES = 128
MIB = 1 << 20


def split3(x):
    hi = x.astype(BF16)
    rest = x - hi.astype(F32)
    mid = rest.astype(BF16)
    low = (rest - mid.astype(F32)).astype(BF16)
    return jnp.concatenate([hi, mid, low], axis=0)


def split2(x):
    hi = x.astype(BF16)
    low = (x - hi.astype(F32)).astype(BF16)
    return hi, low


def dot(a, b, dims=NN):
    return lax.dot_general(a, b, dims, preferred_element_type=F32)


def dot_halves(x, w_hi, w_low):
    rows = x.shape[0]
    x_hi, x_low = split2(x)
    both = dot(jnp.concatenate([x_hi, x_low], axis=0), w_hi)
    return both[:rows] + both[rows:] + dot(x_hi, w_low)


def fold3(acc):
    rows = acc.shape[0] // 3
    return acc[:rows] + acc[rows : 2 * rows] + acc[2 * rows :]


def onehot(condition):
    return condition.astype(F32).astype(BF16)


def block_rows(ref, rows, first, count):
    return jnp.concatenate([ref[pl.ds((first + t) * rows, rows)] for t in range(count)], axis=1)


def block_shard(k):
    return lax.axis_index("blk") ^ k


def facing():
    return (lax.axis_index("sub") ^ lax.axis_index("blk")) & 1


def pack_kernel(
    residual_ref, agg_ref, lists_ref, counts_ref, coarse_ref,
    out_ref, lists_out, coarse_out,
    residual_buf, agg_buf, lists_buf, counts_buf, sems,
):
    sources = (residual_ref, agg_ref, lists_ref, counts_ref, coarse_ref)
    targets = (residual_buf, agg_buf, lists_buf, counts_buf, coarse_out)
    fetches = [pltpu.make_async_copy(a, b, sems.at[k]) for k, (a, b) in enumerate(zip(sources, targets))]
    for fetch in fetches:
        fetch.start()
    rows, cols = residual_buf.shape
    tiles = cols // LANES
    fetches[0].wait()
    for t in range(tiles):
        out_ref[t * rows : (t + 1) * rows] = residual_buf[:, t * LANES : (t + 1) * LANES]
    fetches[1].wait()
    codes = [agg_buf[:, t * LANES : (t + 1) * LANES].astype(F32) for t in range(tiles)]
    codes.append(jnp.zeros((out_ref.shape[0] - rows * tiles - tiles, LANES), F32))
    out_ref[rows * tiles :] = jnp.concatenate(codes, axis=0)
    fetches[2].wait()
    fetches[3].wait()
    slots = lax.broadcasted_iota(jnp.int32, (1, lists_buf.shape[1]), 1)
    for side in range(2):
        used = slots < counts_buf[:, side : side + 1]
        lists_out[side : side + 1] = jnp.where(used, lists_buf[side : side + 1], -1)
    fetches[4].wait()


def coarse_kernel(width, rows, tiles, *refs):
    blocks, coarse_ref, send_ref = refs[:-2], refs[-2], refs[-1]
    shards = len(blocks)
    cols = tiles * LANES
    coarse_len = width * shards
    levels = lax.broadcasted_iota(jnp.int32, (coarse_len, cols), 0)
    rhs = jnp.zeros((3 * rows, coarse_len), F32)
    for ref in blocks:
        codes = [ref[pl.ds(tiles * rows + t, 1)] for t in range(tiles)]
        unknowns = jnp.concatenate(codes, axis=1).astype(jnp.int32)
        rhs = rhs + dot(split3(block_rows(ref, rows, 0, tiles)), onehot(levels == unknowns), NT)
    rhs = fold3(rhs)
    half = rows // 2
    lane = lax.broadcasted_iota(jnp.int32, (half, LANES), 1)
    stride = coarse_ref.shape[0] // coarse_len
    for tile in range(0, stride, 2):
        parts = [coarse_ref[pl.ds(tile + k, coarse_len, stride=stride), :] for k in range(2)]
        value = dot_halves(rhs, *split2(jnp.concatenate(parts, axis=1)))
        for k in range(2):
            part = value[:, k * LANES : (k + 1) * LANES]
            turned = pltpu.roll(part, width, 1)
            left = jnp.where(lane < width, part[:half], turned[half:])
            right = jnp.where(lane < width, turned[:half], part[half:])
            for copy in range(shards):
                send_ref[2 * (tile + k), copy] = left
                send_ref[2 * (tile + k) + 1, copy] = right


def margin_kernel(rows, tiles, *refs):
    blocks, lists_ref, out_ref = refs[:-2], refs[-2], refs[-1]
    cols = tiles * LANES
    wanted = jnp.where(facing() == 1, lists_ref[1:2], lists_ref[0:1])
    local = lax.broadcasted_iota(jnp.int32, (cols, wanted.shape[1]), 0)
    total = jnp.zeros((3 * rows, wanted.shape[1]), F32)
    for k, ref in enumerate(blocks):
        chosen = onehot(local == wanted - block_shard(k) * cols)
        total = total + dot(split3(block_rows(ref, rows, 0, tiles)), chosen)
    out_ref[...] = fold3(total)


def own_kernel(rows, tiles, margin, shards, *refs):
    blocks = refs[:shards]
    agg_ref, fine_ref, out_ref, hi_ref, low_ref, hot_ref, agg_buf, fine_buf, sems = refs[shards:]
    ext = fine_ref.shape[1]
    step = 2 * LANES
    per_block = tiles * LANES // step
    starts = [
        pl.multiple_of(margin + block_shard(k) * (tiles * LANES) + part * step, step)
        for k in range(shards)
        for part in range(per_block)
    ]
    starts += [0, ext - margin]
    sizes = [step] * (len(starts) - 2) + [margin] * 2
    fetch = pltpu.make_async_copy(agg_ref, agg_buf, sems.at[len(starts)])
    fetch.start()
    copies = []
    for k, (start, size) in enumerate(zip(starts, sizes)):
        copies.append(
            pltpu.make_async_copy(
                fine_ref.at[0, pl.ds(start, size)], fine_buf.at[pl.ds(start, size)], sems.at[k]
            )
        )
        copies[k].start()
    fetch.wait()
    levels = lax.broadcasted_iota(jnp.int32, hot_ref.shape, 0)
    hot_ref[...] = onehot(levels == agg_buf[...])
    total = jnp.zeros(out_ref.shape, F32)
    for k, start in enumerate(starts[:-2]):
        block = block_rows(blocks[k // per_block], rows, 2 * (k % per_block), 2)
        copies[k].wait()
        total = total + dot_halves(block, *split2(fine_buf[pl.ds(start, step)]))
    out_ref[...] = total
    for side in range(2):
        start = starts[side - 2]
        copies[side - 2].wait()
        hi_ref[side], low_ref[side] = split2(fine_buf[start : start + margin])


def halo_kernel(mine_ref, other_ref, hi_ref, low_ref, total_ref, out_ref):
    mine, other = mine_ref[...], other_ref[...]
    first = facing() == 1
    total = total_ref[...]
    total = total + dot_halves(jnp.where(first, mine, other), hi_ref[0], low_ref[0])
    total = total + dot_halves(jnp.where(first, other, mine), hi_ref[1], low_ref[1])
    out_ref[...] = total


def tail_kernel(width, got_ref, hot_ref, total_ref, out_ref):
    subs, shards, half, _ = got_ref.shape
    sums = [got_ref[0, shard] for shard in range(shards)]
    for sub in range(1, subs):
        for shard in range(shards):
            sums[shard] = sums[shard] + got_ref[sub, shard]
    lane = lax.broadcasted_iota(jnp.int32, (half, LANES), 1)
    top, bottom = [], []
    for pair in range(shards // 2):
        left, right = sums[2 * pair], sums[2 * pair + 1]
        top.append(jnp.where(lane < width, left, pltpu.roll(right, width, 1)))
        bottom.append(jnp.where(lane < width, pltpu.roll(left, width, 1), right))
    coarse = jnp.concatenate([jnp.concatenate(top, axis=1), jnp.concatenate(bottom, axis=1)], axis=0)
    out_ref[...] = total_ref[...] + fold3(dot(split3(coarse), hot_ref[...]))


def whole(space=pltpu.VMEM):
    return pl.BlockSpec(memory_space=space)


def limit(mib):
    return pltpu.CompilerParams(vmem_limit_bytes=mib * MIB)


def in_hbm(x):
    return pltpu.with_memory_space_constraint(x, pltpu.HBM)


def weight(flops):
    return pl.CostEstimate(flops=flops, bytes_accessed=0, transcendentals=0)


def on_device(residual, fine_inverse, coarse_inverse, wanted_rows, wanted_count, aggregate):
    subs = lax.axis_size("sub")
    shards = lax.axis_size("blk")
    rows, cols = residual.shape
    tiles = cols // LANES
    margin = wanted_rows.shape[2]
    coarse_len = coarse_inverse.shape[0]
    width = coarse_len // shards
    packed_rows = -(-(rows * tiles + tiles) // 8) * 8
    core_swap = [(b, b ^ 1) for b in range(shards)]
    far_swap = [(b, b ^ 2) for b in range(shards)]
    neighbours = []
    for sub in range(subs):
        for b in range(shards):
            other = sub ^ 1 if b % 2 == 0 else (sub + 1 if sub % 2 else sub - 1)
            if 0 <= other < subs:
                neighbours.append((sub * shards + b, other * shards + b))
    codes = aggregate[None]
    lists = wanted_rows[0]
    table = coarse_inverse.reshape(-1, LANES)
    packed_shape = (packed_rows, LANES)

    packed, lists, table = pl.pallas_call(
        pack_kernel,
        out_shape=(
            jax.ShapeDtypeStruct(packed_shape, F32),
            jax.ShapeDtypeStruct(lists.shape, jnp.int32),
            jax.ShapeDtypeStruct(table.shape, F32),
        ),
        in_specs=[whole(pl.ANY)] * 5,
        out_specs=(whole(), whole(), whole()),
        scratch_shapes=[
            pltpu.VMEM(residual.shape, F32),
            pltpu.VMEM(codes.shape, jnp.int32),
            pltpu.VMEM(lists.shape, jnp.int32),
            pltpu.VMEM(wanted_count.shape, jnp.int32),
            pltpu.SemaphoreType.DMA((5,)),
        ],
        compiler_params=limit(4),
        name="pack",
    )(in_hbm(residual), in_hbm(codes), in_hbm(lists), in_hbm(wanted_count), in_hbm(table))
    lists = lax.ppermute(lists, ("sub", "blk"), neighbours)
    over_y = lax.ppermute(packed, "blk", far_swap)
    over_core = lax.ppermute(packed, "blk", core_swap)
    over_both = lax.ppermute(over_y, "blk", core_swap)
    blocks = (packed, over_core, over_y, over_both)

    send = pl.pallas_call(
        functools.partial(coarse_kernel, width, rows, tiles),
        out_shape=jax.ShapeDtypeStruct((subs, shards, rows // 2, LANES), F32),
        in_specs=[whole()] * (shards + 1),
        out_specs=whole(),
        compiler_params=limit(12),
        cost_estimate=weight(8 * 10**9),
        name="coarse",
    )(*blocks, table)
    flat = send.reshape((subs * shards,) + send.shape[2:])
    got = lax.all_to_all(flat, ("sub", "blk"), 0, 0, tiled=True).reshape(send.shape)

    outgoing = pl.pallas_call(
        functools.partial(margin_kernel, rows, tiles),
        out_shape=jax.ShapeDtypeStruct((rows, margin), F32),
        in_specs=[whole()] * (shards + 1),
        out_specs=whole(),
        compiler_params=limit(8),
        cost_estimate=weight(4 * 10**9),
        name="margins",
    )(*blocks, lists)
    halo = lax.ppermute(outgoing, ("sub", "blk"), neighbours)
    other_halo = lax.ppermute(halo, "blk", core_swap)

    owned, w_hi, w_low, hot = pl.pallas_call(
        functools.partial(own_kernel, rows, tiles, margin, shards),
        out_shape=(
            jax.ShapeDtypeStruct((rows, cols), F32),
            jax.ShapeDtypeStruct((2, margin, cols), BF16),
            jax.ShapeDtypeStruct((2, margin, cols), BF16),
            jax.ShapeDtypeStruct((coarse_len, cols), BF16),
        ),
        in_specs=[whole()] * shards + [whole(pl.ANY)] * 2,
        out_specs=(whole(),) * 4,
        scratch_shapes=[
            pltpu.VMEM(codes.shape, jnp.int32),
            pltpu.VMEM(fine_inverse.shape[1:], F32),
            pltpu.SemaphoreType.DMA((shards * tiles // 2 + 3,)),
        ],
        compiler_params=limit(16),
        cost_estimate=weight(40 * 10**9),
        name="owned",
    )(*blocks, in_hbm(codes), in_hbm(fine_inverse))

    fine = pl.pallas_call(
        halo_kernel,
        out_shape=jax.ShapeDtypeStruct((rows, cols), F32),
        in_specs=[whole()] * 5,
        out_specs=whole(),
        compiler_params=limit(12),
        cost_estimate=weight(4 * 10**9),
        name="halos",
    )(halo, other_halo, w_hi, w_low, owned)

    return pl.pallas_call(
        functools.partial(tail_kernel, width),
        out_shape=jax.ShapeDtypeStruct((rows, cols), F32),
        in_specs=[whole()] * 3,
        out_specs=whole(),
        compiler_params=limit(12),
        name="tail",
    )(got, hot, fine)


def solution(mesh):
    in_specs = (
        P(None, ("sub", "blk")),
        P("sub", None, "blk"),
        P("sub", "blk", None),
        P("sub", None, None),
        P("sub", None),
        P(("sub", "blk")),
    )
    out_specs = P(None, ("sub", "blk"))
    return jax.shard_map(
        on_device, mesh=mesh, in_specs=in_specs, out_specs=out_specs, check_vma=False
    )
```

```python
import functools

import jax
import jax.numpy as jnp
from jax import lax
from jax.experimental import pallas as pl
from jax.experimental.pallas import tpu as pltpu
from jax.sharding import PartitionSpec as P

BF16 = jnp.bfloat16
F32 = jnp.float32
NN = (((1,), (0,)), ((), ()))
NT = (((1,), (1,)), ((), ()))
LANES = 128
MIB = 1 << 20


def split3(x):
    hi = x.astype(BF16)
    rest = x - hi.astype(F32)
    mid = rest.astype(BF16)
    low = (rest - mid.astype(F32)).astype(BF16)
    return jnp.concatenate([hi, mid, low], axis=0)


def split2(x):
    hi = x.astype(BF16)
    low = (x - hi.astype(F32)).astype(BF16)
    return hi, low


def dot(a, b, dims=NN):
    return lax.dot_general(a, b, dims, preferred_element_type=F32)


def dot_halves(x, w_hi, w_low):
    rows = x.shape[0]
    x_hi, x_low = split2(x)
    both = dot(jnp.concatenate([x_hi, x_low], axis=0), w_hi)
    return both[:rows] + both[rows:] + dot(x_hi, w_low)


def fold3(acc):
    rows = acc.shape[0] // 3
    return acc[:rows] + acc[rows : 2 * rows] + acc[2 * rows :]


def onehot(condition):
    return condition.astype(F32).astype(BF16)


def block_rows(ref, rows, first, count):
    return jnp.concatenate([ref[pl.ds((first + t) * rows, rows)] for t in range(count)], axis=1)


def block_shard(k):
    return lax.axis_index("blk") ^ k


def facing():
    return (lax.axis_index("sub") ^ lax.axis_index("blk")) & 1


def pack_kernel(
    residual_ref, agg_ref, lists_ref, counts_ref, coarse_ref,
    out_ref, lists_out, coarse_out,
    residual_buf, agg_buf, lists_buf, counts_buf, sems,
):
    sources = (residual_ref, agg_ref, lists_ref, counts_ref, coarse_ref)
    targets = (residual_buf, agg_buf, lists_buf, counts_buf, coarse_out)
    fetches = [pltpu.make_async_copy(a, b, sems.at[k]) for k, (a, b) in enumerate(zip(sources, targets))]
    for fetch in fetches:
        fetch.start()
    rows, cols = residual_buf.shape
    tiles = cols // LANES
    fetches[0].wait()
    for t in range(tiles):
        out_ref[t * rows : (t + 1) * rows] = residual_buf[:, t * LANES : (t + 1) * LANES]
    fetches[1].wait()
    codes = [agg_buf[:, t * LANES : (t + 1) * LANES].astype(F32) for t in range(tiles)]
    codes.append(jnp.zeros((out_ref.shape[0] - rows * tiles - tiles, LANES), F32))
    out_ref[rows * tiles :] = jnp.concatenate(codes, axis=0)
    fetches[2].wait()
    fetches[3].wait()
    slots = lax.broadcasted_iota(jnp.int32, (1, lists_buf.shape[1]), 1)
    for side in range(2):
        used = slots < counts_buf[:, side : side + 1]
        lists_out[side : side + 1] = jnp.where(used, lists_buf[side : side + 1], -1)
    fetches[4].wait()


def coarse_kernel(width, rows, tiles, shards, *refs):
    blocks, (coarse_ref, send_ref, parts_ref) = refs[:shards], refs[shards:]
    cols = tiles * LANES
    coarse_len = width * shards
    levels = lax.broadcasted_iota(jnp.int32, (coarse_len, cols), 0)
    rhs = jnp.zeros((3 * rows, coarse_len), F32)
    for k, ref in enumerate(blocks):
        codes = [ref[pl.ds(tiles * rows + t, 1)] for t in range(tiles)]
        unknowns = jnp.concatenate(codes, axis=1).astype(jnp.int32)
        parts = split3(block_rows(ref, rows, 0, tiles))
        parts_ref[k] = parts
        rhs = rhs + dot(parts, onehot(levels == unknowns), NT)
    rhs = fold3(rhs)
    half = rows // 2
    lane = lax.broadcasted_iota(jnp.int32, (half, LANES), 1)
    stride = coarse_ref.shape[0] // coarse_len
    for tile in range(0, stride, 2):
        parts = [coarse_ref[pl.ds(tile + k, coarse_len, stride=stride), :] for k in range(2)]
        value = dot_halves(rhs, *split2(jnp.concatenate(parts, axis=1)))
        for k in range(2):
            part = value[:, k * LANES : (k + 1) * LANES]
            turned = pltpu.roll(part, width, 1)
            left = jnp.where(lane < width, part[:half], turned[half:])
            right = jnp.where(lane < width, turned[:half], part[half:])
            for copy in range(shards):
                send_ref[2 * (tile + k), copy] = left
                send_ref[2 * (tile + k) + 1, copy] = right


def margin_kernel(parts_ref, lists_ref, out_ref):
    shards, rows, cols = parts_ref.shape
    wanted = jnp.where(facing() == 1, lists_ref[1:2], lists_ref[0:1])
    local = lax.broadcasted_iota(jnp.int32, (cols, wanted.shape[1]), 0)
    total = jnp.zeros((rows, wanted.shape[1]), F32)
    for k in range(shards):
        total = total + dot(parts_ref[k], onehot(local == wanted - block_shard(k) * cols))
    out_ref[...] = fold3(total)


def own_kernel(
    margin, parts_ref, agg_ref, fine_ref, out_ref, hi_ref, low_ref, hot_ref, agg_buf, fine_buf, sems
):
    shards, rows, cols = parts_ref.shape
    rows = rows // 3
    tiles = cols // LANES
    ext = fine_ref.shape[1]
    step = 2 * LANES
    per_block = tiles * LANES // step
    starts = [
        pl.multiple_of(margin + block_shard(k) * (tiles * LANES) + part * step, step)
        for k in range(shards)
        for part in range(per_block)
    ]
    starts += [0, ext - margin]
    sizes = [step] * (len(starts) - 2) + [margin] * 2
    fetch = pltpu.make_async_copy(agg_ref, agg_buf, sems.at[len(starts)])
    fetch.start()
    copies = []
    for k, (start, size) in enumerate(zip(starts, sizes)):
        copies.append(
            pltpu.make_async_copy(
                fine_ref.at[0, pl.ds(start, size)], fine_buf.at[pl.ds(start, size)], sems.at[k]
            )
        )
        copies[k].start()
    fetch.wait()
    levels = lax.broadcasted_iota(jnp.int32, hot_ref.shape, 0)
    hot_ref[...] = onehot(levels == agg_buf[...])
    total = jnp.zeros(out_ref.shape, F32)
    for k, start in enumerate(starts[:-2]):
        part = k % per_block
        block = parts_ref[k // per_block, :, part * step : (part + 1) * step]
        copies[k].wait()
        w_hi, w_low = split2(fine_buf[pl.ds(start, step)])
        both = dot(block[: 2 * rows], w_hi)
        total = total + (both[:rows] + both[rows:] + dot(block[:rows], w_low))
    out_ref[...] = total
    for side in range(2):
        start = starts[side - 2]
        copies[side - 2].wait()
        hi_ref[side], low_ref[side] = split2(fine_buf[start : start + margin])


def mine_kernel(halo_ref, hi_ref, low_ref, total_ref, out_ref, copy_ref):
    halo = halo_ref[...]
    copy_ref[...] = halo
    side = 1 - facing()
    out_ref[...] = total_ref[...] + dot_halves(halo, hi_ref[side], low_ref[side])


def other_kernel(halo_ref, hi_ref, low_ref, total_ref, out_ref):
    side = facing()
    out_ref[...] = total_ref[...] + dot_halves(halo_ref[...], hi_ref[side], low_ref[side])


def tail_kernel(width, got_ref, hot_ref, total_ref, out_ref):
    subs, shards, half, _ = got_ref.shape
    sums = [got_ref[0, shard] for shard in range(shards)]
    for sub in range(1, subs):
        for shard in range(shards):
            sums[shard] = sums[shard] + got_ref[sub, shard]
    lane = lax.broadcasted_iota(jnp.int32, (half, LANES), 1)
    top, bottom = [], []
    for pair in range(shards // 2):
        left, right = sums[2 * pair], sums[2 * pair + 1]
        top.append(jnp.where(lane < width, left, pltpu.roll(right, width, 1)))
        bottom.append(jnp.where(lane < width, pltpu.roll(left, width, 1), right))
    coarse = jnp.concatenate([jnp.concatenate(top, axis=1), jnp.concatenate(bottom, axis=1)], axis=0)
    out_ref[...] = total_ref[...] + fold3(dot(split3(coarse), hot_ref[...]))


def whole(space=pltpu.VMEM):
    return pl.BlockSpec(memory_space=space)


def limit(mib):
    return pltpu.CompilerParams(vmem_limit_bytes=mib * MIB)


def in_hbm(x):
    return pltpu.with_memory_space_constraint(x, pltpu.HBM)


def weight(flops):
    return pl.CostEstimate(flops=flops, bytes_accessed=0, transcendentals=0)


def on_device(residual, fine_inverse, coarse_inverse, wanted_rows, wanted_count, aggregate):
    subs = lax.axis_size("sub")
    shards = lax.axis_size("blk")
    rows, cols = residual.shape
    tiles = cols // LANES
    margin = wanted_rows.shape[2]
    coarse_len = coarse_inverse.shape[0]
    width = coarse_len // shards
    packed_rows = -(-(rows * tiles + tiles) // 8) * 8
    core_swap = [(b, b ^ 1) for b in range(shards)]
    far_swap = [(b, b ^ 2) for b in range(shards)]
    both_swap = [(b, b ^ 3) for b in range(shards)]
    neighbours = []
    for sub in range(subs):
        for b in range(shards):
            other = sub ^ 1 if b % 2 == 0 else (sub + 1 if sub % 2 else sub - 1)
            if 0 <= other < subs:
                neighbours.append((sub * shards + b, other * shards + b))
    codes = aggregate[None]
    lists = wanted_rows[0]
    table = coarse_inverse.reshape(-1, LANES)
    packed_shape = (packed_rows, LANES)

    packed, lists, table = pl.pallas_call(
        pack_kernel,
        out_shape=(
            jax.ShapeDtypeStruct(packed_shape, F32),
            jax.ShapeDtypeStruct(lists.shape, jnp.int32),
            jax.ShapeDtypeStruct(table.shape, F32),
        ),
        in_specs=[whole(pl.ANY)] * 5,
        out_specs=(whole(), whole(), whole()),
        scratch_shapes=[
            pltpu.VMEM(residual.shape, F32),
            pltpu.VMEM(codes.shape, jnp.int32),
            pltpu.VMEM(lists.shape, jnp.int32),
            pltpu.VMEM(wanted_count.shape, jnp.int32),
            pltpu.SemaphoreType.DMA((5,)),
        ],
        compiler_params=limit(4),
        name="pack",
    )(in_hbm(residual), in_hbm(codes), in_hbm(lists), in_hbm(wanted_count), in_hbm(table))
    lists = lax.ppermute(lists, ("sub", "blk"), neighbours)
    over_y = lax.ppermute(packed, "blk", far_swap)
    over_core = lax.ppermute(packed, "blk", core_swap)
    over_both = lax.ppermute(packed, "blk", both_swap)
    blocks = (packed, over_core, over_y, over_both)

    send, parts = pl.pallas_call(
        functools.partial(coarse_kernel, width, rows, tiles, shards),
        out_shape=(
            jax.ShapeDtypeStruct((subs, shards, rows // 2, LANES), F32),
            jax.ShapeDtypeStruct((shards, 3 * rows, cols), BF16),
        ),
        in_specs=[whole()] * (shards + 1),
        out_specs=(whole(), whole()),
        compiler_params=limit(12),
        cost_estimate=weight(8 * 10**9),
        name="coarse",
    )(*blocks, table)
    flat = send.reshape((subs * shards,) + send.shape[2:])
    got = lax.all_to_all(flat, ("sub", "blk"), 0, 0, tiled=True).reshape(send.shape)

    outgoing = pl.pallas_call(
        margin_kernel,
        out_shape=jax.ShapeDtypeStruct((rows, margin), F32),
        in_specs=[whole()] * 2,
        out_specs=whole(),
        compiler_params=limit(8),
        cost_estimate=weight(4 * 10**9),
        name="margins",
    )(parts, lists)
    halo = lax.ppermute(outgoing, ("sub", "blk"), neighbours)

    owned, w_hi, w_low, hot = pl.pallas_call(
        functools.partial(own_kernel, margin),
        out_shape=(
            jax.ShapeDtypeStruct((rows, cols), F32),
            jax.ShapeDtypeStruct((2, margin, cols), BF16),
            jax.ShapeDtypeStruct((2, margin, cols), BF16),
            jax.ShapeDtypeStruct((coarse_len, cols), BF16),
        ),
        in_specs=[whole(), whole(pl.ANY), whole(pl.ANY)],
        out_specs=(whole(),) * 4,
        scratch_shapes=[
            pltpu.VMEM(codes.shape, jnp.int32),
            pltpu.VMEM(fine_inverse.shape[1:], F32),
            pltpu.SemaphoreType.DMA((shards * tiles // 2 + 3,)),
        ],
        compiler_params=limit(16),
        cost_estimate=weight(40 * 10**9),
        name="owned",
    )(parts, in_hbm(codes), in_hbm(fine_inverse))

    fine, mine = pl.pallas_call(
        mine_kernel,
        out_shape=(
            jax.ShapeDtypeStruct((rows, cols), F32),
            jax.ShapeDtypeStruct(halo.shape, F32),
        ),
        in_specs=[whole()] * 4,
        out_specs=(whole(), whole()),
        compiler_params=limit(12),
        cost_estimate=weight(4 * 10**9),
        name="mine",
    )(halo, w_hi, w_low, owned)
    other = lax.ppermute(mine, "blk", core_swap)
    fine = pl.pallas_call(
        other_kernel,
        out_shape=jax.ShapeDtypeStruct((rows, cols), F32),
        in_specs=[whole()] * 4,
        out_specs=whole(),
        compiler_params=limit(12),
        cost_estimate=weight(10**9),
        name="other",
    )(other, w_hi, w_low, fine)

    return pl.pallas_call(
        functools.partial(tail_kernel, width),
        out_shape=jax.ShapeDtypeStruct((rows, cols), F32),
        in_specs=[whole()] * 3,
        out_specs=whole(),
        compiler_params=limit(12),
        name="tail",
    )(got, hot, fine)


def solution(mesh):
    in_specs = (
        P(None, ("sub", "blk")),
        P("sub", None, "blk"),
        P("sub", "blk", None),
        P("sub", None, None),
        P("sub", None),
        P(("sub", "blk")),
    )
    out_specs = P(None, ("sub", "blk"))
    return jax.shard_map(
        on_device, mesh=mesh, in_specs=in_specs, out_specs=out_specs, check_vma=False
    )
```

```python
import functools

import jax
import jax.numpy as jnp
from jax import lax
from jax.experimental import pallas as pl
from jax.experimental.pallas import tpu as pltpu
from jax.sharding import PartitionSpec as P

BF16 = jnp.bfloat16
F32 = jnp.float32
NN = (((1,), (0,)), ((), ()))
NT = (((1,), (1,)), ((), ()))
LANES = 128
MIB = 1 << 20


def split3(x):
    hi = x.astype(BF16)
    rest = x - hi.astype(F32)
    mid = rest.astype(BF16)
    low = (rest - mid.astype(F32)).astype(BF16)
    return jnp.concatenate([hi, mid, low], axis=0)


def split2(x):
    hi = x.astype(BF16)
    low = (x - hi.astype(F32)).astype(BF16)
    return hi, low


def dot(a, b, dims=NN):
    return lax.dot_general(a, b, dims, preferred_element_type=F32)


def dot_halves(x, w_hi, w_low):
    rows = x.shape[0]
    x_hi, x_low = split2(x)
    both = dot(jnp.concatenate([x_hi, x_low], axis=0), w_hi)
    return both[:rows] + both[rows:] + dot(x_hi, w_low)


def fold3(acc):
    rows = acc.shape[0] // 3
    return acc[:rows] + acc[rows : 2 * rows] + acc[2 * rows :]


def onehot(condition):
    return condition.astype(F32).astype(BF16)


def block_rows(ref, rows, first, count):
    return jnp.concatenate([ref[pl.ds((first + t) * rows, rows)] for t in range(count)], axis=1)


def block_shard(k):
    return lax.axis_index("blk") ^ k


def facing():
    return (lax.axis_index("sub") ^ lax.axis_index("blk")) & 1


def pack_kernel(
    residual_ref, agg_ref, lists_ref, counts_ref, coarse_ref,
    out_ref, lists_out, coarse_out,
    residual_buf, agg_buf, lists_buf, counts_buf, sems,
):
    sources = (residual_ref, agg_ref, lists_ref, counts_ref, coarse_ref)
    targets = (residual_buf, agg_buf, lists_buf, counts_buf, coarse_out)
    fetches = [pltpu.make_async_copy(a, b, sems.at[k]) for k, (a, b) in enumerate(zip(sources, targets))]
    for fetch in fetches:
        fetch.start()
    rows, cols = residual_buf.shape
    tiles = cols // LANES
    fetches[0].wait()
    for t in range(tiles):
        out_ref[t * rows : (t + 1) * rows] = residual_buf[:, t * LANES : (t + 1) * LANES]
    fetches[1].wait()
    codes = [agg_buf[:, t * LANES : (t + 1) * LANES].astype(F32) for t in range(tiles)]
    codes.append(jnp.zeros((out_ref.shape[0] - rows * tiles - tiles, LANES), F32))
    out_ref[rows * tiles :] = jnp.concatenate(codes, axis=0)
    fetches[2].wait()
    fetches[3].wait()
    slots = lax.broadcasted_iota(jnp.int32, (1, lists_buf.shape[1]), 1)
    for side in range(2):
        used = slots < counts_buf[:, side : side + 1]
        lists_out[side : side + 1] = jnp.where(used, lists_buf[side : side + 1], -1)
    fetches[4].wait()


def coarse_kernel(width, rows, tiles, shards, *refs):
    blocks = refs[:shards]
    coarse_ref, fine_ref, send_ref, parts_ref, early_ref, sems = refs[shards:]
    cols = tiles * LANES
    margin = (fine_ref.shape[1] - shards * cols) // 2
    fetches = []
    for k in range(early_ref.shape[0]):
        rows_at = pl.ds(pl.multiple_of(margin + block_shard(k) * cols, LANES), cols)
        fetches.append(pltpu.make_async_copy(fine_ref.at[0, rows_at], early_ref.at[k], sems.at[k]))
        fetches[k].start()
    coarse_len = width * shards
    levels = lax.broadcasted_iota(jnp.int32, (coarse_len, cols), 0)
    rhs = jnp.zeros((3 * rows, coarse_len), F32)
    for k, ref in enumerate(blocks):
        codes = [ref[pl.ds(tiles * rows + t, 1)] for t in range(tiles)]
        unknowns = jnp.concatenate(codes, axis=1).astype(jnp.int32)
        parts = split3(block_rows(ref, rows, 0, tiles))
        parts_ref[k] = parts
        rhs = rhs + dot(parts, onehot(levels == unknowns), NT)
    rhs = fold3(rhs)
    half = rows // 2
    lane = lax.broadcasted_iota(jnp.int32, (half, LANES), 1)
    stride = coarse_ref.shape[0] // coarse_len
    for tile in range(0, stride, 2):
        parts = [coarse_ref[pl.ds(tile + k, coarse_len, stride=stride), :] for k in range(2)]
        value = dot_halves(rhs, *split2(jnp.concatenate(parts, axis=1)))
        for k in range(2):
            part = value[:, k * LANES : (k + 1) * LANES]
            turned = pltpu.roll(part, width, 1)
            left = jnp.where(lane < width, part[:half], turned[half:])
            right = jnp.where(lane < width, turned[:half], part[half:])
            for copy in range(send_ref.shape[1]):
                send_ref[2 * (tile + k), copy] = left
                send_ref[2 * (tile + k) + 1, copy] = right
    for fetch in fetches:
        fetch.wait()


def margin_kernel(parts_ref, lists_ref, out_ref):
    shards, rows, cols = parts_ref.shape
    wanted = jnp.where(facing() == 1, lists_ref[1:2], lists_ref[0:1])
    local = lax.broadcasted_iota(jnp.int32, (cols, wanted.shape[1]), 0)
    total = jnp.zeros((rows, wanted.shape[1]), F32)
    for k in range(shards):
        total = total + dot(parts_ref[k], onehot(local == wanted - block_shard(k) * cols))
    out_ref[...] = fold3(total)


def own_kernel(
    margin, parts_ref, early_ref, agg_ref, fine_ref, out_ref, hi_ref, low_ref, hot_ref, agg_buf, fine_buf, sems
):
    shards, rows, cols = parts_ref.shape
    rows = rows // 3
    ext = fine_ref.shape[1]
    early = early_ref.shape[0]
    step = 2 * LANES
    halves = cols // step
    starts = [
        pl.multiple_of(margin + block_shard(k) * cols + part * step, step)
        for k in range(early, shards)
        for part in range(halves)
    ]
    starts += [0, ext - margin]
    sizes = [step] * (len(starts) - 2) + [margin] * 2
    fetch = pltpu.make_async_copy(agg_ref, agg_buf, sems.at[len(starts)])
    fetch.start()
    copies = []
    at = 0
    for k, (start, size) in enumerate(zip(starts, sizes)):
        copies.append(
            pltpu.make_async_copy(fine_ref.at[0, pl.ds(start, size)], fine_buf.at[pl.ds(at, size)], sems.at[k])
        )
        copies[k].start()
        at += size
    total = jnp.zeros(out_ref.shape, F32)
    for k in range(shards):
        for part in range(halves):
            block = parts_ref[k, :, part * step : (part + 1) * step]
            if k < early:
                weights = early_ref[k, part * step : (part + 1) * step]
            else:
                piece = (k - early) * halves + part
                copies[piece].wait()
                weights = fine_buf[piece * step : (piece + 1) * step]
            w_hi, w_low = split2(weights)
            both = dot(block[: 2 * rows], w_hi)
            total = total + (both[:rows] + both[rows:] + dot(block[:rows], w_low))
    out_ref[...] = total
    fetch.wait()
    levels = lax.broadcasted_iota(jnp.int32, hot_ref.shape, 0)
    hot_ref[...] = onehot(levels == agg_buf[...])
    for side in range(2):
        copies[side - 2].wait()
        at = (shards - early) * cols + side * margin
        hi_ref[side], low_ref[side] = split2(fine_buf[at : at + margin])


def mine_kernel(halo_ref, hi_ref, low_ref, total_ref, out_ref, copy_ref):
    halo = halo_ref[...]
    copy_ref[...] = halo
    side = 1 - facing()
    out_ref[...] = total_ref[...] + dot_halves(halo, hi_ref[side], low_ref[side])


def other_kernel(halo_ref, hi_ref, low_ref, total_ref, out_ref):
    side = facing()
    out_ref[...] = total_ref[...] + dot_halves(halo_ref[...], hi_ref[side], low_ref[side])


def reduce_kernel(got_ref, out_ref):
    total = got_ref[0]
    for sub in range(1, got_ref.shape[0]):
        total = total + got_ref[sub]
    out_ref[...] = total


def tail_kernel(width, mine_ref, other_ref, hot_ref, total_ref, out_ref):
    chips, half, _ = mine_ref.shape
    odd = lax.axis_index("blk") & 1
    lane = lax.broadcasted_iota(jnp.int32, (half, LANES), 1)
    top, bottom = [], []
    for chip in range(chips):
        mine, other = mine_ref[chip], other_ref[chip]
        left = jnp.where(odd == 1, other, mine)
        right = jnp.where(odd == 1, mine, other)
        top.append(jnp.where(lane < width, left, pltpu.roll(right, width, 1)))
        bottom.append(jnp.where(lane < width, pltpu.roll(left, width, 1), right))
    coarse = jnp.concatenate([jnp.concatenate(top, axis=1), jnp.concatenate(bottom, axis=1)], axis=0)
    out_ref[...] = total_ref[...] + fold3(dot(split3(coarse), hot_ref[...]))


def whole(space=pltpu.VMEM):
    return pl.BlockSpec(memory_space=space)


def limit(mib):
    return pltpu.CompilerParams(vmem_limit_bytes=mib * MIB)


def in_hbm(x):
    return pltpu.with_memory_space_constraint(x, pltpu.HBM)


def weight(flops):
    return pl.CostEstimate(flops=flops, bytes_accessed=0, transcendentals=0)


def on_device(residual, fine_inverse, coarse_inverse, wanted_rows, wanted_count, aggregate):
    subs = lax.axis_size("sub")
    shards = lax.axis_size("blk")
    rows, cols = residual.shape
    tiles = cols // LANES
    margin = wanted_rows.shape[2]
    coarse_len = coarse_inverse.shape[0]
    width = coarse_len // shards
    chips = shards // 2
    packed_rows = -(-(rows * tiles + tiles) // 8) * 8
    core_swap = [(b, b ^ 1) for b in range(shards)]
    far_swap = [(b, b ^ 2) for b in range(shards)]
    both_swap = [(b, b ^ 3) for b in range(shards)]
    neighbours = []
    for sub in range(subs):
        for b in range(shards):
            other = sub ^ 1 if b % 2 == 0 else (sub + 1 if sub % 2 else sub - 1)
            if 0 <= other < subs:
                neighbours.append((sub * shards + b, other * shards + b))
    codes = aggregate[None]
    lists = wanted_rows[0]
    table = coarse_inverse.reshape(-1, LANES)
    packed_shape = (packed_rows, LANES)

    packed, lists, table = pl.pallas_call(
        pack_kernel,
        out_shape=(
            jax.ShapeDtypeStruct(packed_shape, F32),
            jax.ShapeDtypeStruct(lists.shape, jnp.int32),
            jax.ShapeDtypeStruct(table.shape, F32),
        ),
        in_specs=[whole(pl.ANY)] * 5,
        out_specs=(whole(), whole(), whole()),
        scratch_shapes=[
            pltpu.VMEM(residual.shape, F32),
            pltpu.VMEM(codes.shape, jnp.int32),
            pltpu.VMEM(lists.shape, jnp.int32),
            pltpu.VMEM(wanted_count.shape, jnp.int32),
            pltpu.SemaphoreType.DMA((5,)),
        ],
        compiler_params=limit(4),
        name="pack",
    )(in_hbm(residual), in_hbm(codes), in_hbm(lists), in_hbm(wanted_count), in_hbm(table))
    lists = lax.ppermute(lists, ("sub", "blk"), neighbours)
    over_y = lax.ppermute(packed, "blk", far_swap)
    over_core = lax.ppermute(packed, "blk", core_swap)
    over_both = lax.ppermute(packed, "blk", both_swap)
    blocks = (packed, over_core, over_y, over_both)

    send, parts, early = pl.pallas_call(
        functools.partial(coarse_kernel, width, rows, tiles, shards),
        out_shape=(
            jax.ShapeDtypeStruct((subs, chips, rows // 2, LANES), F32),
            jax.ShapeDtypeStruct((shards, 3 * rows, cols), BF16),
            jax.ShapeDtypeStruct((2, cols, cols), F32),
        ),
        in_specs=[whole()] * (shards + 1) + [whole(pl.ANY)],
        out_specs=(whole(), whole(), whole()),
        scratch_shapes=[pltpu.SemaphoreType.DMA((2,))],
        compiler_params=limit(12),
        cost_estimate=weight(8 * 10**9),
        name="coarse",
    )(*blocks, table, in_hbm(fine_inverse))
    flat = send.reshape((subs * chips,) + send.shape[2:])
    same_core = [[k for k in range(subs * shards) if k % 2 == core] for core in range(2)]
    got = lax.all_to_all(flat, ("sub", "blk"), 0, 0, axis_index_groups=same_core, tiled=True)
    got = got.reshape(send.shape)

    outgoing = pl.pallas_call(
        margin_kernel,
        out_shape=jax.ShapeDtypeStruct((rows, margin), F32),
        in_specs=[whole()] * 2,
        out_specs=whole(),
        compiler_params=limit(8),
        cost_estimate=weight(4 * 10**9),
        name="margins",
    )(parts, lists)
    halo = lax.ppermute(outgoing, ("sub", "blk"), neighbours)

    owned, w_hi, w_low, hot = pl.pallas_call(
        functools.partial(own_kernel, margin),
        out_shape=(
            jax.ShapeDtypeStruct((rows, cols), F32),
            jax.ShapeDtypeStruct((2, margin, cols), BF16),
            jax.ShapeDtypeStruct((2, margin, cols), BF16),
            jax.ShapeDtypeStruct((coarse_len, cols), BF16),
        ),
        in_specs=[whole(), whole(), whole(pl.ANY), whole(pl.ANY)],
        out_specs=(whole(),) * 4,
        scratch_shapes=[
            pltpu.VMEM(codes.shape, jnp.int32),
            pltpu.VMEM((fine_inverse.shape[1] - 2 * cols, cols), F32),
            pltpu.SemaphoreType.DMA((shards * tiles // 2 + 3,)),
        ],
        compiler_params=limit(16),
        cost_estimate=weight(40 * 10**9),
        name="owned",
    )(parts, early, in_hbm(codes), in_hbm(fine_inverse))

    fine, mine = pl.pallas_call(
        mine_kernel,
        out_shape=(
            jax.ShapeDtypeStruct((rows, cols), F32),
            jax.ShapeDtypeStruct(halo.shape, F32),
        ),
        in_specs=[whole()] * 4,
        out_specs=(whole(), whole()),
        compiler_params=limit(12),
        cost_estimate=weight(4 * 10**9),
        name="mine",
    )(halo, w_hi, w_low, owned)
    other = lax.ppermute(mine, "blk", core_swap)
    fine = pl.pallas_call(
        other_kernel,
        out_shape=jax.ShapeDtypeStruct((rows, cols), F32),
        in_specs=[whole()] * 4,
        out_specs=whole(),
        compiler_params=limit(12),
        cost_estimate=weight(10**9),
        name="other",
    )(other, w_hi, w_low, fine)

    sums = pl.pallas_call(
        reduce_kernel,
        out_shape=jax.ShapeDtypeStruct(got.shape[1:], F32),
        in_specs=[whole()],
        out_specs=whole(),
        compiler_params=limit(8),
        cost_estimate=weight(10**8),
        name="reduce",
    )(got)
    other_sums = lax.ppermute(sums, "blk", core_swap)

    return pl.pallas_call(
        functools.partial(tail_kernel, width),
        out_shape=jax.ShapeDtypeStruct((rows, cols), F32),
        in_specs=[whole()] * 4,
        out_specs=whole(),
        compiler_params=limit(12),
        name="tail",
    )(sums, other_sums, hot, fine)


def solution(mesh):
    in_specs = (
        P(None, ("sub", "blk")),
        P("sub", None, "blk"),
        P("sub", "blk", None),
        P("sub", None, None),
        P("sub", None),
        P(("sub", "blk")),
    )
    out_specs = P(None, ("sub", "blk"))
    return jax.shard_map(
        on_device, mesh=mesh, in_specs=in_specs, out_specs=out_specs, check_vma=False
    )
```

```python
import functools

import jax
import jax.numpy as jnp
from jax import lax
from jax.experimental import pallas as pl
from jax.experimental.pallas import tpu as pltpu
from jax.sharding import PartitionSpec as P

BF16 = jnp.bfloat16
F32 = jnp.float32
NN = (((1,), (0,)), ((), ()))
NT = (((1,), (1,)), ((), ()))
LANES = 128
MIB = 1 << 20


def split3(x):
    hi = x.astype(BF16)
    rest = x - hi.astype(F32)
    mid = rest.astype(BF16)
    low = (rest - mid.astype(F32)).astype(BF16)
    return jnp.concatenate([hi, mid, low], axis=0)


def split2(x):
    hi = x.astype(BF16)
    low = (x - hi.astype(F32)).astype(BF16)
    return hi, low


def dot(a, b, dims=NN):
    return lax.dot_general(a, b, dims, preferred_element_type=F32)


def dot_halves(x, w_hi, w_low):
    rows = x.shape[0]
    x_hi, x_low = split2(x)
    both = dot(jnp.concatenate([x_hi, x_low], axis=0), w_hi)
    return both[:rows] + both[rows:] + dot(x_hi, w_low)


def fold3(acc):
    rows = acc.shape[0] // 3
    return acc[:rows] + acc[rows : 2 * rows] + acc[2 * rows :]


def onehot(condition):
    return condition.astype(F32).astype(BF16)


def block_rows(ref, rows, first, count):
    return jnp.concatenate([ref[pl.ds((first + t) * rows, rows)] for t in range(count)], axis=1)


def block_shard(k):
    return lax.axis_index("blk") ^ k


def facing():
    return (lax.axis_index("sub") ^ lax.axis_index("blk")) & 1


def pack_kernel(
    residual_ref, agg_ref, lists_ref, counts_ref,
    out_ref, lists_out,
    residual_buf, agg_buf, lists_buf, counts_buf, sems,
):
    sources = (residual_ref, agg_ref, lists_ref, counts_ref)
    targets = (residual_buf, agg_buf, lists_buf, counts_buf)
    fetches = [pltpu.make_async_copy(a, b, sems.at[k]) for k, (a, b) in enumerate(zip(sources, targets))]
    for fetch in fetches:
        fetch.start()
    rows, cols = residual_buf.shape
    tiles = cols // LANES
    fetches[0].wait()
    for t in range(tiles):
        out_ref[t * rows : (t + 1) * rows] = residual_buf[:, t * LANES : (t + 1) * LANES]
    fetches[1].wait()
    codes = [agg_buf[:, t * LANES : (t + 1) * LANES].astype(F32) for t in range(tiles)]
    codes.append(jnp.zeros((out_ref.shape[0] - rows * tiles - tiles, LANES), F32))
    out_ref[rows * tiles :] = jnp.concatenate(codes, axis=0)
    fetches[2].wait()
    fetches[3].wait()
    slots = lax.broadcasted_iota(jnp.int32, (1, lists_buf.shape[1]), 1)
    for side in range(2):
        used = slots < counts_buf[:, side : side + 1]
        lists_out[side : side + 1] = jnp.where(used, lists_buf[side : side + 1], -1)


def right_hand_side(rows, tiles, coarse_len, blocks, parts_ref):
    levels = lax.broadcasted_iota(jnp.int32, (coarse_len, tiles * LANES), 0)
    rhs = jnp.zeros((3 * rows, coarse_len), F32)
    for k, ref in enumerate(blocks):
        codes = [ref[pl.ds(tiles * rows + t, 1)] for t in range(tiles)]
        unknowns = jnp.concatenate(codes, axis=1).astype(jnp.int32)
        parts = split3(block_rows(ref, rows, 0, tiles))
        parts_ref[k] = parts
        rhs = rhs + dot(parts, onehot(levels == unknowns), NT)
    return fold3(rhs)


def near_kernel(
    rows, tiles, packed_ref, core_ref, coarse_ref, rhs_ref, parts_ref, hi_ref, low_ref, coarse_buf, sem
):
    fetch = pltpu.make_async_copy(coarse_ref, coarse_buf, sem)
    fetch.start()
    coarse_len = hi_ref.shape[0]
    rhs_ref[...] = right_hand_side(rows, tiles, coarse_len, (packed_ref, core_ref), parts_ref)
    stride = coarse_buf.shape[0] // coarse_len
    fetch.wait()
    for tile in range(stride):
        at = slice(tile * LANES, (tile + 1) * LANES)
        hi_ref[:, at], low_ref[:, at] = split2(coarse_buf[pl.ds(tile, coarse_len, stride=stride), :])


def coarse_kernel(
    width, rows, tiles, y_ref, both_ref, rhs_ref, hi_ref, low_ref, send_ref, parts_ref
):
    coarse_len = hi_ref.shape[0]
    rhs = rhs_ref[...] + right_hand_side(rows, tiles, coarse_len, (y_ref, both_ref), parts_ref)
    half = rows // 2
    lane = lax.broadcasted_iota(jnp.int32, (half, LANES), 1)
    step = 2 * LANES
    for first in range(0, hi_ref.shape[1], step):
        at = slice(first, first + step)
        value = dot_halves(rhs, hi_ref[:, at], low_ref[:, at])
        for k in range(2):
            to = 2 * (first // LANES + k)
            part = value[:, k * LANES : (k + 1) * LANES]
            turned = pltpu.roll(part, width, 1)
            left = jnp.where(lane < width, part[:half], turned[half:])
            right = jnp.where(lane < width, turned[:half], part[half:])
            for copy in range(send_ref.shape[1]):
                send_ref[to, copy] = left
                send_ref[to + 1, copy] = right


def margin_kernel(near_ref, far_ref, lists_ref, out_ref):
    half, rows, cols = near_ref.shape
    wanted = jnp.where(facing() == 1, lists_ref[1:2], lists_ref[0:1])
    local = lax.broadcasted_iota(jnp.int32, (cols, wanted.shape[1]), 0)
    total = jnp.zeros((rows, wanted.shape[1]), F32)
    for k in range(2 * half):
        part = near_ref[k] if k < half else far_ref[k - half]
        total = total + dot(part, onehot(local == wanted - block_shard(k) * cols))
    out_ref[...] = fold3(total)


def own_kernel(
    margin, near_ref, far_ref, agg_ref, fine_ref, out_ref, hi_ref, low_ref, hot_ref, agg_buf, fine_buf, sems
):
    half, rows, cols = near_ref.shape
    shards = 2 * half
    rows = rows // 3
    tiles = cols // LANES
    ext = fine_ref.shape[1]
    step = 2 * LANES
    per_block = tiles * LANES // step
    starts = [
        pl.multiple_of(margin + block_shard(k) * (tiles * LANES) + part * step, step)
        for k in range(shards)
        for part in range(per_block)
    ]
    starts += [0, ext - margin]
    sizes = [step] * (len(starts) - 2) + [margin] * 2
    fetch = pltpu.make_async_copy(agg_ref, agg_buf, sems.at[len(starts)])
    fetch.start()
    copies = []
    for k, (start, size) in enumerate(zip(starts, sizes)):
        copies.append(
            pltpu.make_async_copy(
                fine_ref.at[0, pl.ds(start, size)], fine_buf.at[pl.ds(start, size)], sems.at[k]
            )
        )
        copies[k].start()
    fetch.wait()
    levels = lax.broadcasted_iota(jnp.int32, hot_ref.shape, 0)
    hot_ref[...] = onehot(levels == agg_buf[...])
    total = jnp.zeros(out_ref.shape, F32)
    for k, start in enumerate(starts[:-2]):
        part = k % per_block
        at = k // per_block
        ref = near_ref if at < half else far_ref
        block = ref[at % half, :, part * step : (part + 1) * step]
        copies[k].wait()
        w_hi, w_low = split2(fine_buf[pl.ds(start, step)])
        both = dot(block[: 2 * rows], w_hi)
        total = total + (both[:rows] + both[rows:] + dot(block[:rows], w_low))
    out_ref[...] = total
    for side in range(2):
        start = starts[side - 2]
        copies[side - 2].wait()
        hi_ref[side], low_ref[side] = split2(fine_buf[start : start + margin])


def mine_kernel(halo_ref, hi_ref, low_ref, total_ref, out_ref, copy_ref):
    halo = halo_ref[...]
    copy_ref[...] = halo
    side = 1 - facing()
    out_ref[...] = total_ref[...] + dot_halves(halo, hi_ref[side], low_ref[side])


def other_kernel(halo_ref, hi_ref, low_ref, total_ref, out_ref):
    side = facing()
    out_ref[...] = total_ref[...] + dot_halves(halo_ref[...], hi_ref[side], low_ref[side])


def reduce_kernel(got_ref, out_ref):
    total = got_ref[0]
    for sub in range(1, got_ref.shape[0]):
        total = total + got_ref[sub]
    out_ref[...] = total


def tail_kernel(width, mine_ref, other_ref, hot_ref, total_ref, out_ref):
    chips, half, _ = mine_ref.shape
    odd = lax.axis_index("blk") & 1
    lane = lax.broadcasted_iota(jnp.int32, (half, LANES), 1)
    top, bottom = [], []
    for chip in range(chips):
        mine, other = mine_ref[chip], other_ref[chip]
        left = jnp.where(odd == 1, other, mine)
        right = jnp.where(odd == 1, mine, other)
        top.append(jnp.where(lane < width, left, pltpu.roll(right, width, 1)))
        bottom.append(jnp.where(lane < width, pltpu.roll(left, width, 1), right))
    coarse = jnp.concatenate([jnp.concatenate(top, axis=1), jnp.concatenate(bottom, axis=1)], axis=0)
    out_ref[...] = total_ref[...] + fold3(dot(split3(coarse), hot_ref[...]))


def whole(space=pltpu.VMEM):
    return pl.BlockSpec(memory_space=space)


def limit(mib):
    return pltpu.CompilerParams(vmem_limit_bytes=mib * MIB)


def in_hbm(x):
    return pltpu.with_memory_space_constraint(x, pltpu.HBM)


def weight(flops):
    return pl.CostEstimate(flops=flops, bytes_accessed=0, transcendentals=0)


def on_device(residual, fine_inverse, coarse_inverse, wanted_rows, wanted_count, aggregate):
    subs = lax.axis_size("sub")
    shards = lax.axis_size("blk")
    rows, cols = residual.shape
    tiles = cols // LANES
    margin = wanted_rows.shape[2]
    coarse_len = coarse_inverse.shape[0]
    width = coarse_len // shards
    chips = shards // 2
    packed_rows = -(-(rows * tiles + tiles) // 8) * 8
    core_swap = [(b, b ^ 1) for b in range(shards)]
    far_swap = [(b, b ^ 2) for b in range(shards)]
    both_swap = [(b, b ^ 3) for b in range(shards)]
    neighbours = []
    for sub in range(subs):
        for b in range(shards):
            other = sub ^ 1 if b % 2 == 0 else (sub + 1 if sub % 2 else sub - 1)
            if 0 <= other < subs:
                neighbours.append((sub * shards + b, other * shards + b))
    codes = aggregate[None]
    lists = wanted_rows[0]
    table = coarse_inverse.reshape(-1, LANES)
    packed_shape = (packed_rows, LANES)

    packed, lists = pl.pallas_call(
        pack_kernel,
        out_shape=(
            jax.ShapeDtypeStruct(packed_shape, F32),
            jax.ShapeDtypeStruct(lists.shape, jnp.int32),
        ),
        in_specs=[whole(pl.ANY)] * 4,
        out_specs=(whole(), whole()),
        scratch_shapes=[
            pltpu.VMEM(residual.shape, F32),
            pltpu.VMEM(codes.shape, jnp.int32),
            pltpu.VMEM(lists.shape, jnp.int32),
            pltpu.VMEM(wanted_count.shape, jnp.int32),
            pltpu.SemaphoreType.DMA((4,)),
        ],
        compiler_params=limit(4),
        name="pack",
    )(in_hbm(residual), in_hbm(codes), in_hbm(lists), in_hbm(wanted_count))
    lists = lax.ppermute(lists, ("sub", "blk"), neighbours)
    over_y = lax.ppermute(packed, "blk", far_swap)
    over_core = lax.ppermute(packed, "blk", core_swap)
    over_both = lax.ppermute(packed, "blk", both_swap)

    rhs, near, m_hi, m_low = pl.pallas_call(
        functools.partial(near_kernel, rows, tiles),
        out_shape=(
            jax.ShapeDtypeStruct((rows, coarse_len), F32),
            jax.ShapeDtypeStruct((2, 3 * rows, cols), BF16),
            jax.ShapeDtypeStruct((coarse_len, subs * width), BF16),
            jax.ShapeDtypeStruct((coarse_len, subs * width), BF16),
        ),
        in_specs=[whole(), whole(), whole(pl.ANY)],
        out_specs=(whole(),) * 4,
        scratch_shapes=[pltpu.VMEM(table.shape, F32), pltpu.SemaphoreType.DMA],
        compiler_params=limit(12),
        cost_estimate=weight(2 * 10**9),
        name="near",
    )(packed, over_core, in_hbm(table))
    send, far = pl.pallas_call(
        functools.partial(coarse_kernel, width, rows, tiles),
        out_shape=(
            jax.ShapeDtypeStruct((subs, chips, rows // 2, LANES), F32),
            jax.ShapeDtypeStruct((shards - 2, 3 * rows, cols), BF16),
        ),
        in_specs=[whole()] * 5,
        out_specs=(whole(), whole()),
        compiler_params=limit(12),
        cost_estimate=weight(8 * 10**9),
        name="coarse",
    )(over_y, over_both, rhs, m_hi, m_low)
    flat = send.reshape((subs * chips,) + send.shape[2:])
    same_core = [[k for k in range(subs * shards) if k % 2 == core] for core in range(2)]
    got = lax.all_to_all(flat, ("sub", "blk"), 0, 0, axis_index_groups=same_core, tiled=True)
    got = got.reshape(send.shape)

    outgoing = pl.pallas_call(
        margin_kernel,
        out_shape=jax.ShapeDtypeStruct((rows, margin), F32),
        in_specs=[whole()] * 3,
        out_specs=whole(),
        compiler_params=limit(8),
        cost_estimate=weight(4 * 10**9),
        name="margins",
    )(near, far, lists)
    halo = lax.ppermute(outgoing, ("sub", "blk"), neighbours)

    owned, w_hi, w_low, hot = pl.pallas_call(
        functools.partial(own_kernel, margin),
        out_shape=(
            jax.ShapeDtypeStruct((rows, cols), F32),
            jax.ShapeDtypeStruct((2, margin, cols), BF16),
            jax.ShapeDtypeStruct((2, margin, cols), BF16),
            jax.ShapeDtypeStruct((coarse_len, cols), BF16),
        ),
        in_specs=[whole(), whole(), whole(pl.ANY), whole(pl.ANY)],
        out_specs=(whole(),) * 4,
        scratch_shapes=[
            pltpu.VMEM(codes.shape, jnp.int32),
            pltpu.VMEM(fine_inverse.shape[1:], F32),
            pltpu.SemaphoreType.DMA((shards * tiles // 2 + 3,)),
        ],
        compiler_params=limit(16),
        cost_estimate=weight(40 * 10**9),
        name="owned",
    )(near, far, in_hbm(codes), in_hbm(fine_inverse))

    fine, mine = pl.pallas_call(
        mine_kernel,
        out_shape=(
            jax.ShapeDtypeStruct((rows, cols), F32),
            jax.ShapeDtypeStruct(halo.shape, F32),
        ),
        in_specs=[whole()] * 4,
        out_specs=(whole(), whole()),
        compiler_params=limit(12),
        cost_estimate=weight(4 * 10**9),
        name="mine",
    )(halo, w_hi, w_low, owned)
    other = lax.ppermute(mine, "blk", core_swap)
    fine = pl.pallas_call(
        other_kernel,
        out_shape=jax.ShapeDtypeStruct((rows, cols), F32),
        in_specs=[whole()] * 4,
        out_specs=whole(),
        compiler_params=limit(12),
        cost_estimate=weight(10**9),
        name="other",
    )(other, w_hi, w_low, fine)

    sums = pl.pallas_call(
        reduce_kernel,
        out_shape=jax.ShapeDtypeStruct(got.shape[1:], F32),
        in_specs=[whole()],
        out_specs=whole(),
        compiler_params=limit(8),
        cost_estimate=weight(10**8),
        name="reduce",
    )(got)
    other_sums = lax.ppermute(sums, "blk", core_swap)

    return pl.pallas_call(
        functools.partial(tail_kernel, width),
        out_shape=jax.ShapeDtypeStruct((rows, cols), F32),
        in_specs=[whole()] * 4,
        out_specs=whole(),
        compiler_params=limit(12),
        name="tail",
    )(sums, other_sums, hot, fine)


def solution(mesh):
    in_specs = (
        P(None, ("sub", "blk")),
        P("sub", None, "blk"),
        P("sub", "blk", None),
        P("sub", None, None),
        P("sub", None),
        P(("sub", "blk")),
    )
    out_specs = P(None, ("sub", "blk"))
    return jax.shard_map(
        on_device, mesh=mesh, in_specs=in_specs, out_specs=out_specs, check_vma=False
    )
```

```python
import functools

import jax
import jax.numpy as jnp
from jax import lax
from jax.experimental import pallas as pl
from jax.experimental.pallas import tpu as pltpu
from jax.sharding import PartitionSpec as P

BF16 = jnp.bfloat16
F32 = jnp.float32
NN = (((1,), (0,)), ((), ()))
NT = (((1,), (1,)), ((), ()))
LANES = 128
MIB = 1 << 20


def split3(x):
    hi = x.astype(BF16)
    rest = x - hi.astype(F32)
    mid = rest.astype(BF16)
    low = (rest - mid.astype(F32)).astype(BF16)
    return jnp.concatenate([hi, mid, low], axis=0)


def split2(x):
    hi = x.astype(BF16)
    low = (x - hi.astype(F32)).astype(BF16)
    return hi, low


def dot(a, b, dims=NN):
    return lax.dot_general(a, b, dims, preferred_element_type=F32)


def dot_halves(x, w_hi, w_low):
    rows = x.shape[0]
    x_hi, x_low = split2(x)
    both = dot(jnp.concatenate([x_hi, x_low], axis=0), w_hi)
    return both[:rows] + both[rows:] + dot(x_hi, w_low)


def fold3(acc):
    rows = acc.shape[0] // 3
    return acc[:rows] + acc[rows : 2 * rows] + acc[2 * rows :]


def onehot(condition):
    return condition.astype(F32).astype(BF16)


def block_rows(ref, rows, first, count):
    return jnp.concatenate([ref[pl.ds((first + t) * rows, rows)] for t in range(count)], axis=1)


def block_shard(k):
    return lax.axis_index("blk") ^ k


def facing():
    return (lax.axis_index("sub") ^ lax.axis_index("blk")) & 1


def pack_kernel(
    residual_ref, agg_ref, lists_ref, counts_ref, coarse_ref,
    out_ref, lists_out, coarse_out,
    residual_buf, agg_buf, lists_buf, counts_buf, sems,
):
    sources = (residual_ref, agg_ref, lists_ref, counts_ref, coarse_ref)
    targets = (residual_buf, agg_buf, lists_buf, counts_buf, coarse_out)
    fetches = [pltpu.make_async_copy(a, b, sems.at[k]) for k, (a, b) in enumerate(zip(sources, targets))]
    for fetch in fetches:
        fetch.start()
    rows, cols = residual_buf.shape
    tiles = cols // LANES
    fetches[0].wait()
    for t in range(tiles):
        out_ref[t * rows : (t + 1) * rows] = residual_buf[:, t * LANES : (t + 1) * LANES]
    fetches[1].wait()
    codes = [agg_buf[:, t * LANES : (t + 1) * LANES].astype(F32) for t in range(tiles)]
    codes.append(jnp.zeros((out_ref.shape[0] - rows * tiles - tiles, LANES), F32))
    out_ref[rows * tiles :] = jnp.concatenate(codes, axis=0)
    fetches[2].wait()
    fetches[3].wait()
    slots = lax.broadcasted_iota(jnp.int32, (1, lists_buf.shape[1]), 1)
    for side in range(2):
        used = slots < counts_buf[:, side : side + 1]
        lists_out[side : side + 1] = jnp.where(used, lists_buf[side : side + 1], -1)
    fetches[4].wait()


def right_hand_side(rows, tiles, coarse_len, blocks, parts_ref):
    levels = lax.broadcasted_iota(jnp.int32, (coarse_len, tiles * LANES), 0)
    rhs = jnp.zeros((3 * rows, coarse_len), F32)
    for k, ref in enumerate(blocks):
        codes = [ref[pl.ds(tiles * rows + t, 1)] for t in range(tiles)]
        unknowns = jnp.concatenate(codes, axis=1).astype(jnp.int32)
        parts = split3(block_rows(ref, rows, 0, tiles))
        parts_ref[k] = parts
        rhs = rhs + dot(parts, onehot(levels == unknowns), NT)
    return fold3(rhs)


def near_kernel(
    rows, tiles, packed_ref, core_ref, coarse_ref, rhs_ref, parts_ref, hi_ref, low_ref
):
    coarse_len = hi_ref.shape[0]
    rhs_ref[...] = right_hand_side(rows, tiles, coarse_len, (packed_ref, core_ref), parts_ref)
    stride = coarse_ref.shape[0] // coarse_len
    for tile in range(stride):
        at = slice(tile * LANES, (tile + 1) * LANES)
        hi_ref[:, at], low_ref[:, at] = split2(coarse_ref[pl.ds(tile, coarse_len, stride=stride), :])


def coarse_kernel(
    width, rows, tiles, y_ref, both_ref, rhs_ref, hi_ref, low_ref, send_ref, parts_ref
):
    coarse_len = hi_ref.shape[0]
    rhs = rhs_ref[...] + right_hand_side(rows, tiles, coarse_len, (y_ref, both_ref), parts_ref)
    half = rows // 2
    lane = lax.broadcasted_iota(jnp.int32, (half, LANES), 1)
    step = 2 * LANES
    for first in range(0, hi_ref.shape[1], step):
        at = slice(first, first + step)
        value = dot_halves(rhs, hi_ref[:, at], low_ref[:, at])
        for k in range(2):
            to = 2 * (first // LANES + k)
            part = value[:, k * LANES : (k + 1) * LANES]
            turned = pltpu.roll(part, width, 1)
            left = jnp.where(lane < width, part[:half], turned[half:])
            right = jnp.where(lane < width, turned[:half], part[half:])
            send_ref[to] = left
            send_ref[to + 1] = right


def margin_kernel(near_ref, far_ref, lists_ref, out_ref):
    half, rows, cols = near_ref.shape
    wanted = jnp.where(facing() == 1, lists_ref[1:2], lists_ref[0:1])
    local = lax.broadcasted_iota(jnp.int32, (cols, wanted.shape[1]), 0)
    total = jnp.zeros((rows, wanted.shape[1]), F32)
    for k in range(2 * half):
        part = near_ref[k] if k < half else far_ref[k - half]
        total = total + dot(part, onehot(local == wanted - block_shard(k) * cols))
    out_ref[...] = fold3(total)


def own_kernel(
    margin, near_ref, far_ref, agg_ref, fine_ref, out_ref, hi_ref, low_ref, hot_ref, agg_buf, fine_buf, sems
):
    half, rows, cols = near_ref.shape
    shards = 2 * half
    rows = rows // 3
    tiles = cols // LANES
    ext = fine_ref.shape[1]
    step = 2 * LANES
    per_block = tiles * LANES // step
    starts = [
        pl.multiple_of(margin + block_shard(k) * (tiles * LANES) + part * step, step)
        for k in range(shards)
        for part in range(per_block)
    ]
    starts += [0, ext - margin]
    sizes = [step] * (len(starts) - 2) + [margin] * 2
    fetch = pltpu.make_async_copy(agg_ref, agg_buf, sems.at[len(starts)])
    fetch.start()
    copies = []
    for k, (start, size) in enumerate(zip(starts, sizes)):
        copies.append(
            pltpu.make_async_copy(
                fine_ref.at[0, pl.ds(start, size)], fine_buf.at[pl.ds(start, size)], sems.at[k]
            )
        )
        copies[k].start()
    fetch.wait()
    levels = lax.broadcasted_iota(jnp.int32, hot_ref.shape, 0)
    hot_ref[...] = onehot(levels == agg_buf[...])
    total = jnp.zeros(out_ref.shape, F32)
    for k, start in enumerate(starts[:-2]):
        part = k % per_block
        at = k // per_block
        ref = near_ref if at < half else far_ref
        block = ref[at % half, :, part * step : (part + 1) * step]
        copies[k].wait()
        w_hi, w_low = split2(fine_buf[pl.ds(start, step)])
        both = dot(block[: 2 * rows], w_hi)
        total = total + (both[:rows] + both[rows:] + dot(block[:rows], w_low))
    out_ref[...] = total
    for side in range(2):
        start = starts[side - 2]
        copies[side - 2].wait()
        hi_ref[side], low_ref[side] = split2(fine_buf[start : start + margin])


def mine_kernel(halo_ref, hi_ref, low_ref, total_ref, out_ref, copy_ref):
    halo = halo_ref[...]
    copy_ref[...] = halo
    side = 1 - facing()
    out_ref[...] = total_ref[...] + dot_halves(halo, hi_ref[side], low_ref[side])


def other_kernel(halo_ref, hi_ref, low_ref, total_ref, out_ref):
    side = facing()
    out_ref[...] = total_ref[...] + dot_halves(halo_ref[...], hi_ref[side], low_ref[side])


def reduce_kernel(got_ref, out_ref):
    total = got_ref[0]
    for sub in range(1, got_ref.shape[0]):
        total = total + got_ref[sub]
    out_ref[...] = total


def tail_kernel(width, mine_ref, core_ref, y_ref, both_ref, hot_ref, total_ref, out_ref):
    half = mine_ref.shape[0]
    place = lax.axis_index("blk")
    odd, upper = (place & 1) == 1, place >= 2
    lane = lax.broadcasted_iota(jnp.int32, (half, LANES), 1)
    tiles = []
    for even_ref, odd_ref in ((mine_ref, core_ref), (y_ref, both_ref)):
        this, that = even_ref[...], odd_ref[...]
        left, right = jnp.where(odd, that, this), jnp.where(odd, this, that)
        top = jnp.where(lane < width, left, pltpu.roll(right, width, 1))
        bottom = jnp.where(lane < width, pltpu.roll(left, width, 1), right)
        tiles.append(jnp.concatenate([top, bottom], axis=0))
    first, second = jnp.where(upper, tiles[1], tiles[0]), jnp.where(upper, tiles[0], tiles[1])
    coarse = jnp.concatenate([first, second], axis=1)
    out_ref[...] = total_ref[...] + fold3(dot(split3(coarse), hot_ref[...]))


def whole(space=pltpu.VMEM):
    return pl.BlockSpec(memory_space=space)


def limit(mib):
    return pltpu.CompilerParams(vmem_limit_bytes=mib * MIB)


def in_hbm(x):
    return pltpu.with_memory_space_constraint(x, pltpu.HBM)


def weight(flops):
    return pl.CostEstimate(flops=flops, bytes_accessed=0, transcendentals=0)


def on_device(residual, fine_inverse, coarse_inverse, wanted_rows, wanted_count, aggregate):
    subs = lax.axis_size("sub")
    shards = lax.axis_size("blk")
    rows, cols = residual.shape
    tiles = cols // LANES
    margin = wanted_rows.shape[2]
    coarse_len = coarse_inverse.shape[0]
    width = coarse_len // shards
    packed_rows = -(-(rows * tiles + tiles) // 8) * 8
    core_swap = [(b, b ^ 1) for b in range(shards)]
    far_swap = [(b, b ^ 2) for b in range(shards)]
    both_swap = [(b, b ^ 3) for b in range(shards)]
    neighbours = []
    for sub in range(subs):
        for b in range(shards):
            other = sub ^ 1 if b % 2 == 0 else (sub + 1 if sub % 2 else sub - 1)
            if 0 <= other < subs:
                neighbours.append((sub * shards + b, other * shards + b))
    codes = aggregate[None]
    lists = wanted_rows[0]
    table = coarse_inverse.reshape(-1, LANES)
    packed_shape = (packed_rows, LANES)

    packed, lists, table = pl.pallas_call(
        pack_kernel,
        out_shape=(
            jax.ShapeDtypeStruct(packed_shape, F32),
            jax.ShapeDtypeStruct(lists.shape, jnp.int32),
            jax.ShapeDtypeStruct(table.shape, F32),
        ),
        in_specs=[whole(pl.ANY)] * 5,
        out_specs=(whole(),) * 3,
        scratch_shapes=[
            pltpu.VMEM(residual.shape, F32),
            pltpu.VMEM(codes.shape, jnp.int32),
            pltpu.VMEM(lists.shape, jnp.int32),
            pltpu.VMEM(wanted_count.shape, jnp.int32),
            pltpu.SemaphoreType.DMA((5,)),
        ],
        compiler_params=limit(4),
        name="pack",
    )(in_hbm(residual), in_hbm(codes), in_hbm(lists), in_hbm(wanted_count), in_hbm(table))
    lists = lax.ppermute(lists, ("sub", "blk"), neighbours)
    over_y = lax.ppermute(packed, "blk", far_swap)
    over_core = lax.ppermute(packed, "blk", core_swap)
    over_both = lax.ppermute(packed, "blk", both_swap)

    rhs, near, m_hi, m_low = pl.pallas_call(
        functools.partial(near_kernel, rows, tiles),
        out_shape=(
            jax.ShapeDtypeStruct((rows, coarse_len), F32),
            jax.ShapeDtypeStruct((2, 3 * rows, cols), BF16),
            jax.ShapeDtypeStruct((coarse_len, subs * width), BF16),
            jax.ShapeDtypeStruct((coarse_len, subs * width), BF16),
        ),
        in_specs=[whole()] * 3,
        out_specs=(whole(),) * 4,
        compiler_params=limit(12),
        cost_estimate=weight(2 * 10**9),
        name="near",
    )(packed, over_core, table)
    send, far = pl.pallas_call(
        functools.partial(coarse_kernel, width, rows, tiles),
        out_shape=(
            jax.ShapeDtypeStruct((subs, rows // 2, LANES), F32),
            jax.ShapeDtypeStruct((shards - 2, 3 * rows, cols), BF16),
        ),
        in_specs=[whole()] * 5,
        out_specs=(whole(), whole()),
        compiler_params=limit(12),
        cost_estimate=weight(8 * 10**9),
        name="coarse",
    )(over_y, over_both, rhs, m_hi, m_low)
    got = lax.all_to_all(send, "sub", 0, 0, tiled=True)

    outgoing = pl.pallas_call(
        margin_kernel,
        out_shape=jax.ShapeDtypeStruct((rows, margin), F32),
        in_specs=[whole()] * 3,
        out_specs=whole(),
        compiler_params=limit(8),
        cost_estimate=weight(4 * 10**9),
        name="margins",
    )(near, far, lists)
    halo = lax.ppermute(outgoing, ("sub", "blk"), neighbours)

    owned, w_hi, w_low, hot = pl.pallas_call(
        functools.partial(own_kernel, margin),
        out_shape=(
            jax.ShapeDtypeStruct((rows, cols), F32),
            jax.ShapeDtypeStruct((2, margin, cols), BF16),
            jax.ShapeDtypeStruct((2, margin, cols), BF16),
            jax.ShapeDtypeStruct((coarse_len, cols), BF16),
        ),
        in_specs=[whole(), whole(), whole(pl.ANY), whole(pl.ANY)],
        out_specs=(whole(),) * 4,
        scratch_shapes=[
            pltpu.VMEM(codes.shape, jnp.int32),
            pltpu.VMEM(fine_inverse.shape[1:], F32),
            pltpu.SemaphoreType.DMA((shards * tiles // 2 + 3,)),
        ],
        compiler_params=limit(16),
        cost_estimate=weight(40 * 10**9),
        name="owned",
    )(near, far, in_hbm(codes), in_hbm(fine_inverse))

    fine, mine = pl.pallas_call(
        mine_kernel,
        out_shape=(
            jax.ShapeDtypeStruct((rows, cols), F32),
            jax.ShapeDtypeStruct(halo.shape, F32),
        ),
        in_specs=[whole()] * 4,
        out_specs=(whole(), whole()),
        compiler_params=limit(12),
        cost_estimate=weight(4 * 10**9),
        name="mine",
    )(halo, w_hi, w_low, owned)
    other = lax.ppermute(mine, "blk", core_swap)
    fine = pl.pallas_call(
        other_kernel,
        out_shape=jax.ShapeDtypeStruct((rows, cols), F32),
        in_specs=[whole()] * 4,
        out_specs=whole(),
        compiler_params=limit(12),
        cost_estimate=weight(10**9),
        name="other",
    )(other, w_hi, w_low, fine)

    sums = pl.pallas_call(
        reduce_kernel,
        out_shape=jax.ShapeDtypeStruct(got.shape[1:], F32),
        in_specs=[whole()],
        out_specs=whole(),
        compiler_params=limit(8),
        cost_estimate=weight(10**8),
        name="reduce",
    )(got)
    sums_over = [lax.ppermute(sums, "blk", swap) for swap in (core_swap, far_swap, both_swap)]

    return pl.pallas_call(
        functools.partial(tail_kernel, width),
        out_shape=jax.ShapeDtypeStruct((rows, cols), F32),
        in_specs=[whole()] * 6,
        out_specs=whole(),
        compiler_params=limit(12),
        name="tail",
    )(sums, *sums_over, hot, fine)


def solution(mesh):
    in_specs = (
        P(None, ("sub", "blk")),
        P("sub", None, "blk"),
        P("sub", "blk", None),
        P("sub", None, None),
        P("sub", None),
        P(("sub", "blk")),
    )
    out_specs = P(None, ("sub", "blk"))
    return jax.shard_map(
        on_device, mesh=mesh, in_specs=in_specs, out_specs=out_specs, check_vma=False
    )
```

```python
import functools

import jax
import jax.numpy as jnp
from jax import lax
from jax.experimental import pallas as pl
from jax.experimental.pallas import tpu as pltpu
from jax.sharding import PartitionSpec as P

BF16 = jnp.bfloat16
F32 = jnp.float32
NN = (((1,), (0,)), ((), ()))
NT = (((1,), (1,)), ((), ()))
LANES = 128
MIB = 1 << 20


def split3(x):
    hi = x.astype(BF16)
    rest = x - hi.astype(F32)
    mid = rest.astype(BF16)
    low = (rest - mid.astype(F32)).astype(BF16)
    return jnp.concatenate([hi, mid, low], axis=0)


def split2(x):
    hi = x.astype(BF16)
    low = (x - hi.astype(F32)).astype(BF16)
    return hi, low


def dot(a, b, dims=NN):
    return lax.dot_general(a, b, dims, preferred_element_type=F32)


def dot_halves(x, w_hi, w_low):
    rows = x.shape[0]
    x_hi, x_low = split2(x)
    both = dot(jnp.concatenate([x_hi, x_low], axis=0), w_hi)
    return both[:rows] + both[rows:] + dot(x_hi, w_low)


def fold3(acc):
    rows = acc.shape[0] // 3
    return acc[:rows] + acc[rows : 2 * rows] + acc[2 * rows :]


def onehot(condition):
    return condition.astype(F32).astype(BF16)


def block_rows(ref, rows, first, count):
    return jnp.concatenate([ref[pl.ds((first + t) * rows, rows)] for t in range(count)], axis=1)


def block_shard(k):
    return lax.axis_index("blk") ^ k


def facing():
    return (lax.axis_index("sub") ^ lax.axis_index("blk")) & 1


def pack_kernel(
    residual_ref, agg_ref, lists_ref, counts_ref, coarse_ref,
    out_ref, lists_out, coarse_out,
    residual_buf, agg_buf, lists_buf, counts_buf, sems,
):
    sources = (residual_ref, agg_ref, lists_ref, counts_ref, coarse_ref)
    targets = (residual_buf, agg_buf, lists_buf, counts_buf, coarse_out)
    fetches = [pltpu.make_async_copy(a, b, sems.at[k]) for k, (a, b) in enumerate(zip(sources, targets))]
    for fetch in fetches:
        fetch.start()
    rows, cols = residual_buf.shape
    tiles = cols // LANES
    fetches[0].wait()
    for t in range(tiles):
        out_ref[t * rows : (t + 1) * rows] = residual_buf[:, t * LANES : (t + 1) * LANES]
    fetches[1].wait()
    codes = [agg_buf[:, t * LANES : (t + 1) * LANES].astype(F32) for t in range(tiles)]
    codes.append(jnp.zeros((out_ref.shape[0] - rows * tiles - tiles, LANES), F32))
    out_ref[rows * tiles :] = jnp.concatenate(codes, axis=0)
    fetches[2].wait()
    fetches[3].wait()
    slots = lax.broadcasted_iota(jnp.int32, (1, lists_buf.shape[1]), 1)
    for side in range(2):
        used = slots < counts_buf[:, side : side + 1]
        lists_out[side : side + 1] = jnp.where(used, lists_buf[side : side + 1], -1)
    fetches[4].wait()


def right_hand_side(rows, tiles, coarse_len, blocks, parts_ref):
    levels = lax.broadcasted_iota(jnp.int32, (coarse_len, tiles * LANES), 0)
    rhs = jnp.zeros((3 * rows, coarse_len), F32)
    for k, ref in enumerate(blocks):
        codes = [ref[pl.ds(tiles * rows + t, 1)] for t in range(tiles)]
        unknowns = jnp.concatenate(codes, axis=1).astype(jnp.int32)
        parts = split3(block_rows(ref, rows, 0, tiles))
        parts_ref[k] = parts
        rhs = rhs + dot(parts, onehot(levels == unknowns), NT)
    return fold3(rhs)


def near_kernel(
    rows, tiles, packed_ref, core_ref, coarse_ref, rhs_ref, parts_ref, hi_ref, low_ref
):
    coarse_len = hi_ref.shape[0]
    rhs_ref[...] = right_hand_side(rows, tiles, coarse_len, (packed_ref, core_ref), parts_ref)
    stride = coarse_ref.shape[0] // coarse_len
    for tile in range(stride):
        at = slice(tile * LANES, (tile + 1) * LANES)
        hi_ref[:, at], low_ref[:, at] = split2(coarse_ref[pl.ds(tile, coarse_len, stride=stride), :])


def coarse_kernel(
    width, rows, tiles, y_ref, both_ref, rhs_ref, hi_ref, low_ref, send_ref, parts_ref
):
    coarse_len = hi_ref.shape[0]
    rhs = rhs_ref[...] + right_hand_side(rows, tiles, coarse_len, (y_ref, both_ref), parts_ref)
    half = rows // 2
    lane = lax.broadcasted_iota(jnp.int32, (half, LANES), 1)
    step = 2 * LANES
    for first in range(0, hi_ref.shape[1], step):
        at = slice(first, first + step)
        value = dot_halves(rhs, hi_ref[:, at], low_ref[:, at])
        for k in range(2):
            to = 2 * (first // LANES + k)
            part = value[:, k * LANES : (k + 1) * LANES]
            turned = pltpu.roll(part, width, 1)
            left = jnp.where(lane < width, part[:half], turned[half:])
            right = jnp.where(lane < width, turned[:half], part[half:])
            for copy in range(send_ref.shape[1]):
                send_ref[to, copy] = left
                send_ref[to + 1, copy] = right


def margin_kernel(near_ref, far_ref, lists_ref, out_ref):
    half, rows, cols = near_ref.shape
    wanted = jnp.where(facing() == 1, lists_ref[1:2], lists_ref[0:1])
    local = lax.broadcasted_iota(jnp.int32, (cols, wanted.shape[1]), 0)
    total = jnp.zeros((rows, wanted.shape[1]), F32)
    for k in range(2 * half):
        part = near_ref[k] if k < half else far_ref[k - half]
        total = total + dot(part, onehot(local == wanted - block_shard(k) * cols))
    out_ref[...] = fold3(total)


def own_kernel(
    margin, near_ref, far_ref, agg_ref, fine_ref, out_ref, hi_ref, low_ref, hot_ref, agg_buf, fine_buf, sems
):
    half, rows, cols = near_ref.shape
    shards = 2 * half
    rows = rows // 3
    tiles = cols // LANES
    ext = fine_ref.shape[1]
    step = 2 * LANES
    per_block = tiles * LANES // step
    starts = [
        pl.multiple_of(margin + block_shard(k) * (tiles * LANES) + part * step, step)
        for k in range(shards)
        for part in range(per_block)
    ]
    starts += [0, ext - margin]
    sizes = [step] * (len(starts) - 2) + [margin] * 2
    fetch = pltpu.make_async_copy(agg_ref, agg_buf, sems.at[len(starts)])
    fetch.start()
    copies = []
    for k, (start, size) in enumerate(zip(starts, sizes)):
        copies.append(
            pltpu.make_async_copy(
                fine_ref.at[0, pl.ds(start, size)], fine_buf.at[pl.ds(start, size)], sems.at[k]
            )
        )
        copies[k].start()
    fetch.wait()
    levels = lax.broadcasted_iota(jnp.int32, hot_ref.shape, 0)
    hot_ref[...] = onehot(levels == agg_buf[...])
    total = jnp.zeros(out_ref.shape, F32)
    for k, start in enumerate(starts[:-2]):
        part = k % per_block
        at = k // per_block
        ref = near_ref if at < half else far_ref
        block = ref[at % half, :, part * step : (part + 1) * step]
        copies[k].wait()
        w_hi, w_low = split2(fine_buf[pl.ds(start, step)])
        both = dot(block[: 2 * rows], w_hi)
        total = total + (both[:rows] + both[rows:] + dot(block[:rows], w_low))
    out_ref[...] = total
    for side in range(2):
        start = starts[side - 2]
        copies[side - 2].wait()
        hi_ref[side], low_ref[side] = split2(fine_buf[start : start + margin])


def mine_kernel(halo_ref, hi_ref, low_ref, total_ref, out_ref, copy_ref):
    halo = halo_ref[...]
    copy_ref[...] = halo
    side = 1 - facing()
    out_ref[...] = total_ref[...] + dot_halves(halo, hi_ref[side], low_ref[side])


def other_kernel(halo_ref, hi_ref, low_ref, total_ref, out_ref):
    side = facing()
    out_ref[...] = total_ref[...] + dot_halves(halo_ref[...], hi_ref[side], low_ref[side])


def reduce_kernel(got_ref, out_ref):
    total = got_ref[0]
    for sub in range(1, got_ref.shape[0]):
        total = total + got_ref[sub]
    out_ref[...] = total


def tail_kernel(width, mine_ref, other_ref, hot_ref, total_ref, out_ref):
    chips, half, _ = mine_ref.shape
    odd = lax.axis_index("blk") & 1
    lane = lax.broadcasted_iota(jnp.int32, (half, LANES), 1)
    top, bottom = [], []
    for chip in range(chips):
        mine, other = mine_ref[chip], other_ref[chip]
        left = jnp.where(odd == 1, other, mine)
        right = jnp.where(odd == 1, mine, other)
        top.append(jnp.where(lane < width, left, pltpu.roll(right, width, 1)))
        bottom.append(jnp.where(lane < width, pltpu.roll(left, width, 1), right))
    coarse = jnp.concatenate([jnp.concatenate(top, axis=1), jnp.concatenate(bottom, axis=1)], axis=0)
    out_ref[...] = total_ref[...] + fold3(dot(split3(coarse), hot_ref[...]))


def whole(space=pltpu.VMEM):
    return pl.BlockSpec(memory_space=space)


def limit(mib):
    return pltpu.CompilerParams(vmem_limit_bytes=mib * MIB)


def in_hbm(x):
    return pltpu.with_memory_space_constraint(x, pltpu.HBM)


def weight(flops):
    return pl.CostEstimate(flops=flops, bytes_accessed=0, transcendentals=0)


def on_device(residual, fine_inverse, coarse_inverse, wanted_rows, wanted_count, aggregate):
    subs = lax.axis_size("sub")
    shards = lax.axis_size("blk")
    rows, cols = residual.shape
    tiles = cols // LANES
    margin = wanted_rows.shape[2]
    coarse_len = coarse_inverse.shape[0]
    width = coarse_len // shards
    chips = shards // 2
    packed_rows = -(-(rows * tiles + tiles) // 8) * 8
    core_swap = [(b, b ^ 1) for b in range(shards)]
    far_swap = [(b, b ^ 2) for b in range(shards)]
    both_swap = [(b, b ^ 3) for b in range(shards)]
    neighbours = []
    for sub in range(subs):
        for b in range(shards):
            other = sub ^ 1 if b % 2 == 0 else (sub + 1 if sub % 2 else sub - 1)
            if 0 <= other < subs:
                neighbours.append((sub * shards + b, other * shards + b))
    codes = aggregate[None]
    lists = wanted_rows[0]
    table = coarse_inverse.reshape(-1, LANES)
    packed_shape = (packed_rows, LANES)

    packed, lists, table = pl.pallas_call(
        pack_kernel,
        out_shape=(
            jax.ShapeDtypeStruct(packed_shape, F32),
            jax.ShapeDtypeStruct(lists.shape, jnp.int32),
            jax.ShapeDtypeStruct(table.shape, F32),
        ),
        in_specs=[whole(pl.ANY)] * 5,
        out_specs=(whole(),) * 3,
        scratch_shapes=[
            pltpu.VMEM(residual.shape, F32),
            pltpu.VMEM(codes.shape, jnp.int32),
            pltpu.VMEM(lists.shape, jnp.int32),
            pltpu.VMEM(wanted_count.shape, jnp.int32),
            pltpu.SemaphoreType.DMA((5,)),
        ],
        compiler_params=limit(4),
        name="pack",
    )(in_hbm(residual), in_hbm(codes), in_hbm(lists), in_hbm(wanted_count), in_hbm(table))
    lists = lax.ppermute(lists, ("sub", "blk"), neighbours)
    over_y = lax.ppermute(packed, "blk", far_swap)
    over_core = lax.ppermute(packed, "blk", core_swap)
    over_both = lax.ppermute(packed, "blk", both_swap)

    rhs, near, m_hi, m_low = pl.pallas_call(
        functools.partial(near_kernel, rows, tiles),
        out_shape=(
            jax.ShapeDtypeStruct((rows, coarse_len), F32),
            jax.ShapeDtypeStruct((2, 3 * rows, cols), BF16),
            jax.ShapeDtypeStruct((coarse_len, subs * width), BF16),
            jax.ShapeDtypeStruct((coarse_len, subs * width), BF16),
        ),
        in_specs=[whole()] * 3,
        out_specs=(whole(),) * 4,
        compiler_params=limit(12),
        cost_estimate=weight(2 * 10**9),
        name="near",
    )(packed, over_core, table)
    send, far = pl.pallas_call(
        functools.partial(coarse_kernel, width, rows, tiles),
        out_shape=(
            jax.ShapeDtypeStruct((subs, chips, rows // 2, LANES), F32),
            jax.ShapeDtypeStruct((shards - 2, 3 * rows, cols), BF16),
        ),
        in_specs=[whole()] * 5,
        out_specs=(whole(), whole()),
        compiler_params=limit(12),
        cost_estimate=weight(8 * 10**9),
        name="coarse",
    )(over_y, over_both, rhs, m_hi, m_low)
    flat = send.reshape((subs * chips,) + send.shape[2:])
    same_core = [[k for k in range(subs * shards) if k % 2 == core] for core in range(2)]
    got = lax.all_to_all(flat, ("sub", "blk"), 0, 0, axis_index_groups=same_core, tiled=True)
    got = got.reshape(send.shape)

    outgoing = pl.pallas_call(
        margin_kernel,
        out_shape=jax.ShapeDtypeStruct((rows, margin), F32),
        in_specs=[whole()] * 3,
        out_specs=whole(),
        compiler_params=limit(8),
        cost_estimate=weight(4 * 10**9),
        name="margins",
    )(near, far, lists)
    halo = lax.ppermute(outgoing, ("sub", "blk"), neighbours)

    owned, w_hi, w_low, hot = pl.pallas_call(
        functools.partial(own_kernel, margin),
        out_shape=(
            jax.ShapeDtypeStruct((rows, cols), F32),
            jax.ShapeDtypeStruct((2, margin, cols), BF16),
            jax.ShapeDtypeStruct((2, margin, cols), BF16),
            jax.ShapeDtypeStruct((coarse_len, cols), BF16),
        ),
        in_specs=[whole(), whole(), whole(pl.ANY), whole(pl.ANY)],
        out_specs=(whole(),) * 4,
        scratch_shapes=[
            pltpu.VMEM(codes.shape, jnp.int32),
            pltpu.VMEM(fine_inverse.shape[1:], F32),
            pltpu.SemaphoreType.DMA((shards * tiles // 2 + 3,)),
        ],
        compiler_params=limit(16),
        cost_estimate=weight(40 * 10**9),
        name="owned",
    )(near, far, in_hbm(codes), in_hbm(fine_inverse))

    fine, mine = pl.pallas_call(
        mine_kernel,
        out_shape=(
            jax.ShapeDtypeStruct((rows, cols), F32),
            jax.ShapeDtypeStruct(halo.shape, F32),
        ),
        in_specs=[whole()] * 4,
        out_specs=(whole(), whole()),
        compiler_params=limit(12),
        cost_estimate=weight(4 * 10**9),
        name="mine",
    )(halo, w_hi, w_low, owned)
    other = lax.ppermute(mine, "blk", core_swap)
    fine = pl.pallas_call(
        other_kernel,
        out_shape=jax.ShapeDtypeStruct((rows, cols), F32),
        in_specs=[whole()] * 4,
        out_specs=whole(),
        compiler_params=limit(12),
        cost_estimate=weight(10**9),
        name="other",
    )(other, w_hi, w_low, fine)

    sums = pl.pallas_call(
        reduce_kernel,
        out_shape=jax.ShapeDtypeStruct(got.shape[1:], F32),
        in_specs=[whole()],
        out_specs=whole(),
        compiler_params=limit(8),
        cost_estimate=weight(10**8),
        name="reduce",
    )(got)
    other_sums = lax.ppermute(sums, "blk", core_swap)

    return pl.pallas_call(
        functools.partial(tail_kernel, width),
        out_shape=jax.ShapeDtypeStruct((rows, cols), F32),
        in_specs=[whole()] * 4,
        out_specs=whole(),
        compiler_params=limit(12),
        name="tail",
    )(sums, other_sums, hot, fine)


def solution(mesh):
    in_specs = (
        P(None, ("sub", "blk")),
        P("sub", None, "blk"),
        P("sub", "blk", None),
        P("sub", None, None),
        P("sub", None),
        P(("sub", "blk")),
    )
    out_specs = P(None, ("sub", "blk"))
    return jax.shard_map(
        on_device, mesh=mesh, in_specs=in_specs, out_specs=out_specs, check_vma=False
    )
```

```python
import functools

import jax
import jax.numpy as jnp
from jax import lax
from jax.experimental import pallas as pl
from jax.experimental.pallas import tpu as pltpu
from jax.sharding import PartitionSpec as P

BF16 = jnp.bfloat16
F32 = jnp.float32
NN = (((1,), (0,)), ((), ()))
NT = (((1,), (1,)), ((), ()))
LANES = 128
MIB = 1 << 20


def split3(x):
    hi = x.astype(BF16)
    rest = x - hi.astype(F32)
    mid = rest.astype(BF16)
    low = (rest - mid.astype(F32)).astype(BF16)
    return jnp.concatenate([hi, mid, low], axis=0)


def split2(x):
    hi = x.astype(BF16)
    low = (x - hi.astype(F32)).astype(BF16)
    return hi, low


def dot(a, b, dims=NN):
    return lax.dot_general(a, b, dims, preferred_element_type=F32)


def dot_halves(x, w_hi, w_low):
    rows = x.shape[0]
    x_hi, x_low = split2(x)
    both = dot(jnp.concatenate([x_hi, x_low], axis=0), w_hi)
    return both[:rows] + both[rows:] + dot(x_hi, w_low)


def fold3(acc):
    rows = acc.shape[0] // 3
    return acc[:rows] + acc[rows : 2 * rows] + acc[2 * rows :]


def onehot(condition):
    return condition.astype(F32).astype(BF16)


def block_rows(ref, rows, first, count):
    return jnp.concatenate([ref[pl.ds((first + t) * rows, rows)] for t in range(count)], axis=1)


def block_shard(k):
    return lax.axis_index("blk") ^ k


def facing():
    return (lax.axis_index("sub") ^ lax.axis_index("blk")) & 1


def pack_kernel(
    residual_ref, agg_ref, lists_ref, counts_ref, coarse_ref,
    out_ref, lists_out, coarse_out,
    residual_buf, agg_buf, lists_buf, counts_buf, sems,
):
    sources = (residual_ref, agg_ref, lists_ref, counts_ref, coarse_ref)
    targets = (residual_buf, agg_buf, lists_buf, counts_buf, coarse_out)
    fetches = [pltpu.make_async_copy(a, b, sems.at[k]) for k, (a, b) in enumerate(zip(sources, targets))]
    for fetch in fetches:
        fetch.start()
    rows, cols = residual_buf.shape
    tiles = cols // LANES
    fetches[0].wait()
    for t in range(tiles):
        out_ref[t * rows : (t + 1) * rows] = residual_buf[:, t * LANES : (t + 1) * LANES]
    fetches[1].wait()
    codes = [agg_buf[:, t * LANES : (t + 1) * LANES].astype(F32) for t in range(tiles)]
    codes.append(jnp.zeros((out_ref.shape[0] - rows * tiles - tiles, LANES), F32))
    out_ref[rows * tiles :] = jnp.concatenate(codes, axis=0)
    fetches[2].wait()
    fetches[3].wait()
    slots = lax.broadcasted_iota(jnp.int32, (1, lists_buf.shape[1]), 1)
    for side in range(2):
        used = slots < counts_buf[:, side : side + 1]
        lists_out[side : side + 1] = jnp.where(used, lists_buf[side : side + 1], -1)
    fetches[4].wait()


def right_hand_side(rows, tiles, coarse_len, blocks, parts_ref):
    levels = lax.broadcasted_iota(jnp.int32, (coarse_len, tiles * LANES), 0)
    rhs = jnp.zeros((3 * rows, coarse_len), F32)
    for k, ref in enumerate(blocks):
        codes = [ref[pl.ds(tiles * rows + t, 1)] for t in range(tiles)]
        unknowns = jnp.concatenate(codes, axis=1).astype(jnp.int32)
        parts = split3(block_rows(ref, rows, 0, tiles))
        parts_ref[k] = parts
        rhs = rhs + dot(parts, onehot(levels == unknowns), NT)
    return fold3(rhs)


def near_kernel(
    rows, tiles, packed_ref, core_ref, coarse_ref, rhs_ref, parts_ref, hi_ref, low_ref
):
    coarse_len = hi_ref.shape[0]
    rhs_ref[...] = right_hand_side(rows, tiles, coarse_len, (packed_ref, core_ref), parts_ref)
    stride = coarse_ref.shape[0] // coarse_len
    for tile in range(stride):
        at = slice(tile * LANES, (tile + 1) * LANES)
        hi_ref[:, at], low_ref[:, at] = split2(coarse_ref[pl.ds(tile, coarse_len, stride=stride), :])


def coarse_kernel(
    width, rows, tiles, y_ref, both_ref, rhs_ref, hi_ref, low_ref, send_ref, parts_ref
):
    coarse_len = hi_ref.shape[0]
    rhs = rhs_ref[...] + right_hand_side(rows, tiles, coarse_len, (y_ref, both_ref), parts_ref)
    half = rows // 2
    lane = lax.broadcasted_iota(jnp.int32, (half, LANES), 1)
    step = 2 * LANES
    for first in range(0, hi_ref.shape[1], step):
        at = slice(first, first + step)
        value = dot_halves(rhs, hi_ref[:, at], low_ref[:, at])
        for k in range(2):
            to = 2 * (first // LANES + k)
            part = value[:, k * LANES : (k + 1) * LANES]
            turned = pltpu.roll(part, width, 1)
            left = jnp.where(lane < width, part[:half], turned[half:])
            right = jnp.where(lane < width, turned[:half], part[half:])
            for copy in range(send_ref.shape[1]):
                for core in range(2):
                    piece = slice(core * half // 2, (core + 1) * half // 2)
                    send_ref[to, copy, core] = left[piece]
                    send_ref[to + 1, copy, core] = right[piece]


def margin_kernel(near_ref, far_ref, lists_ref, out_ref):
    half, rows, cols = near_ref.shape
    wanted = jnp.where(facing() == 1, lists_ref[1:2], lists_ref[0:1])
    local = lax.broadcasted_iota(jnp.int32, (cols, wanted.shape[1]), 0)
    total = jnp.zeros((rows, wanted.shape[1]), F32)
    for k in range(2 * half):
        part = near_ref[k] if k < half else far_ref[k - half]
        total = total + dot(part, onehot(local == wanted - block_shard(k) * cols))
    out_ref[...] = fold3(total)


def own_kernel(
    margin, near_ref, far_ref, agg_ref, fine_ref, out_ref, hi_ref, low_ref, hot_ref, agg_buf, fine_buf, sems
):
    half, rows, cols = near_ref.shape
    shards = 2 * half
    rows = rows // 3
    tiles = cols // LANES
    ext = fine_ref.shape[1]
    step = 2 * LANES
    per_block = tiles * LANES // step
    starts = [
        pl.multiple_of(margin + block_shard(k) * (tiles * LANES) + part * step, step)
        for k in range(shards)
        for part in range(per_block)
    ]
    starts += [0, ext - margin]
    sizes = [step] * (len(starts) - 2) + [margin] * 2
    fetch = pltpu.make_async_copy(agg_ref, agg_buf, sems.at[len(starts)])
    fetch.start()
    copies = []
    for k, (start, size) in enumerate(zip(starts, sizes)):
        copies.append(
            pltpu.make_async_copy(
                fine_ref.at[0, pl.ds(start, size)], fine_buf.at[pl.ds(start, size)], sems.at[k]
            )
        )
        copies[k].start()
    fetch.wait()
    levels = lax.broadcasted_iota(jnp.int32, hot_ref.shape, 0)
    hot_ref[...] = onehot(levels == agg_buf[...])
    total = jnp.zeros(out_ref.shape, F32)
    for k, start in enumerate(starts[:-2]):
        part = k % per_block
        at = k // per_block
        ref = near_ref if at < half else far_ref
        block = ref[at % half, :, part * step : (part + 1) * step]
        copies[k].wait()
        w_hi, w_low = split2(fine_buf[pl.ds(start, step)])
        both = dot(block[: 2 * rows], w_hi)
        total = total + (both[:rows] + both[rows:] + dot(block[:rows], w_low))
    out_ref[...] = total
    for side in range(2):
        start = starts[side - 2]
        copies[side - 2].wait()
        hi_ref[side], low_ref[side] = split2(fine_buf[start : start + margin])


def mine_kernel(halo_ref, hi_ref, low_ref, total_ref, out_ref, copy_ref):
    halo = halo_ref[...]
    copy_ref[...] = halo
    side = 1 - facing()
    out_ref[...] = total_ref[...] + dot_halves(halo, hi_ref[side], low_ref[side])


def other_kernel(halo_ref, hi_ref, low_ref, total_ref, out_ref):
    side = facing()
    out_ref[...] = total_ref[...] + dot_halves(halo_ref[...], hi_ref[side], low_ref[side])


def reduce_kernel(got_ref, out_ref):
    total = got_ref[0]
    for sub in range(1, got_ref.shape[0]):
        total = total + got_ref[sub]
    out_ref[...] = total


def tail_kernel(width, mine_ref, other_ref, hot_ref, total_ref, out_ref):
    odd = (lax.axis_index("blk") & 1) == 1
    chunks = []
    for k in range(mine_ref.shape[0]):
        mine, other = mine_ref[k], other_ref[k]
        pieces = [jnp.where(odd, other, mine), jnp.where(odd, mine, other)]
        chunks.append(jnp.concatenate(pieces, axis=0))
    lane = lax.broadcasted_iota(jnp.int32, chunks[0].shape, 1)
    top, bottom = [], []
    for left, right in zip(chunks[::2], chunks[1::2]):
        top.append(jnp.where(lane < width, left, pltpu.roll(right, width, 1)))
        bottom.append(jnp.where(lane < width, pltpu.roll(left, width, 1), right))
    coarse = jnp.concatenate([jnp.concatenate(top, axis=1), jnp.concatenate(bottom, axis=1)], axis=0)
    out_ref[...] = total_ref[...] + fold3(dot(split3(coarse), hot_ref[...]))


def whole(space=pltpu.VMEM):
    return pl.BlockSpec(memory_space=space)


def limit(mib):
    return pltpu.CompilerParams(vmem_limit_bytes=mib * MIB)


def in_hbm(x):
    return pltpu.with_memory_space_constraint(x, pltpu.HBM)


def weight(flops):
    return pl.CostEstimate(flops=flops, bytes_accessed=0, transcendentals=0)


def on_device(residual, fine_inverse, coarse_inverse, wanted_rows, wanted_count, aggregate):
    subs = lax.axis_size("sub")
    shards = lax.axis_size("blk")
    rows, cols = residual.shape
    tiles = cols // LANES
    margin = wanted_rows.shape[2]
    coarse_len = coarse_inverse.shape[0]
    width = coarse_len // shards
    chips = shards // 2
    packed_rows = -(-(rows * tiles + tiles) // 8) * 8
    core_swap = [(b, b ^ 1) for b in range(shards)]
    far_swap = [(b, b ^ 2) for b in range(shards)]
    both_swap = [(b, b ^ 3) for b in range(shards)]
    neighbours = []
    for sub in range(subs):
        for b in range(shards):
            other = sub ^ 1 if b % 2 == 0 else (sub + 1 if sub % 2 else sub - 1)
            if 0 <= other < subs:
                neighbours.append((sub * shards + b, other * shards + b))
    codes = aggregate[None]
    lists = wanted_rows[0]
    table = coarse_inverse.reshape(-1, LANES)
    packed_shape = (packed_rows, LANES)

    packed, lists, table = pl.pallas_call(
        pack_kernel,
        out_shape=(
            jax.ShapeDtypeStruct(packed_shape, F32),
            jax.ShapeDtypeStruct(lists.shape, jnp.int32),
            jax.ShapeDtypeStruct(table.shape, F32),
        ),
        in_specs=[whole(pl.ANY)] * 5,
        out_specs=(whole(),) * 3,
        scratch_shapes=[
            pltpu.VMEM(residual.shape, F32),
            pltpu.VMEM(codes.shape, jnp.int32),
            pltpu.VMEM(lists.shape, jnp.int32),
            pltpu.VMEM(wanted_count.shape, jnp.int32),
            pltpu.SemaphoreType.DMA((5,)),
        ],
        compiler_params=limit(4),
        name="pack",
    )(in_hbm(residual), in_hbm(codes), in_hbm(lists), in_hbm(wanted_count), in_hbm(table))
    lists = lax.ppermute(lists, ("sub", "blk"), neighbours)
    over_y = lax.ppermute(packed, "blk", far_swap)
    over_core = lax.ppermute(packed, "blk", core_swap)
    over_both = lax.ppermute(packed, "blk", both_swap)

    rhs, near, m_hi, m_low = pl.pallas_call(
        functools.partial(near_kernel, rows, tiles),
        out_shape=(
            jax.ShapeDtypeStruct((rows, coarse_len), F32),
            jax.ShapeDtypeStruct((2, 3 * rows, cols), BF16),
            jax.ShapeDtypeStruct((coarse_len, subs * width), BF16),
            jax.ShapeDtypeStruct((coarse_len, subs * width), BF16),
        ),
        in_specs=[whole()] * 3,
        out_specs=(whole(),) * 4,
        compiler_params=limit(12),
        cost_estimate=weight(2 * 10**9),
        name="near",
    )(packed, over_core, table)
    send, far = pl.pallas_call(
        functools.partial(coarse_kernel, width, rows, tiles),
        out_shape=(
            jax.ShapeDtypeStruct((subs, chips, 2, rows // 4, LANES), F32),
            jax.ShapeDtypeStruct((shards - 2, 3 * rows, cols), BF16),
        ),
        in_specs=[whole()] * 5,
        out_specs=(whole(), whole()),
        compiler_params=limit(12),
        cost_estimate=weight(8 * 10**9),
        name="coarse",
    )(over_y, over_both, rhs, m_hi, m_low)
    flat = send.reshape((subs * shards,) + send.shape[3:])
    got = lax.all_to_all(flat, ("sub", "blk"), 0, 0, tiled=True)
    got = got.reshape((subs, shards) + flat.shape[1:])

    outgoing = pl.pallas_call(
        margin_kernel,
        out_shape=jax.ShapeDtypeStruct((rows, margin), F32),
        in_specs=[whole()] * 3,
        out_specs=whole(),
        compiler_params=limit(8),
        cost_estimate=weight(4 * 10**9),
        name="margins",
    )(near, far, lists)
    halo = lax.ppermute(outgoing, ("sub", "blk"), neighbours)

    owned, w_hi, w_low, hot = pl.pallas_call(
        functools.partial(own_kernel, margin),
        out_shape=(
            jax.ShapeDtypeStruct((rows, cols), F32),
            jax.ShapeDtypeStruct((2, margin, cols), BF16),
            jax.ShapeDtypeStruct((2, margin, cols), BF16),
            jax.ShapeDtypeStruct((coarse_len, cols), BF16),
        ),
        in_specs=[whole(), whole(), whole(pl.ANY), whole(pl.ANY)],
        out_specs=(whole(),) * 4,
        scratch_shapes=[
            pltpu.VMEM(codes.shape, jnp.int32),
            pltpu.VMEM(fine_inverse.shape[1:], F32),
            pltpu.SemaphoreType.DMA((shards * tiles // 2 + 3,)),
        ],
        compiler_params=limit(16),
        cost_estimate=weight(40 * 10**9),
        name="owned",
    )(near, far, in_hbm(codes), in_hbm(fine_inverse))

    fine, mine = pl.pallas_call(
        mine_kernel,
        out_shape=(
            jax.ShapeDtypeStruct((rows, cols), F32),
            jax.ShapeDtypeStruct(halo.shape, F32),
        ),
        in_specs=[whole()] * 4,
        out_specs=(whole(), whole()),
        compiler_params=limit(12),
        cost_estimate=weight(4 * 10**9),
        name="mine",
    )(halo, w_hi, w_low, owned)
    other = lax.ppermute(mine, "blk", core_swap)
    fine = pl.pallas_call(
        other_kernel,
        out_shape=jax.ShapeDtypeStruct((rows, cols), F32),
        in_specs=[whole()] * 4,
        out_specs=whole(),
        compiler_params=limit(12),
        cost_estimate=weight(10**9),
        name="other",
    )(other, w_hi, w_low, fine)

    sums = pl.pallas_call(
        reduce_kernel,
        out_shape=jax.ShapeDtypeStruct(got.shape[1:], F32),
        in_specs=[whole()],
        out_specs=whole(),
        compiler_params=limit(8),
        cost_estimate=weight(10**8),
        name="reduce",
    )(got)
    other_sums = lax.ppermute(sums, "blk", core_swap)

    return pl.pallas_call(
        functools.partial(tail_kernel, width),
        out_shape=jax.ShapeDtypeStruct((rows, cols), F32),
        in_specs=[whole()] * 4,
        out_specs=whole(),
        compiler_params=limit(12),
        name="tail",
    )(sums, other_sums, hot, fine)


def solution(mesh):
    in_specs = (
        P(None, ("sub", "blk")),
        P("sub", None, "blk"),
        P("sub", "blk", None),
        P("sub", None, None),
        P("sub", None),
        P(("sub", "blk")),
    )
    out_specs = P(None, ("sub", "blk"))
    return jax.shard_map(
        on_device, mesh=mesh, in_specs=in_specs, out_specs=out_specs, check_vma=False
    )
```

```python
import functools

import jax
import jax.numpy as jnp
from jax import lax
from jax.experimental import pallas as pl
from jax.experimental.pallas import tpu as pltpu
from jax.sharding import PartitionSpec as P

BF16 = jnp.bfloat16
F32 = jnp.float32
NN = (((1,), (0,)), ((), ()))
NT = (((1,), (1,)), ((), ()))
LANES = 128
MIB = 1 << 20


def split3(x):
    hi = x.astype(BF16)
    rest = x - hi.astype(F32)
    mid = rest.astype(BF16)
    low = (rest - mid.astype(F32)).astype(BF16)
    return jnp.concatenate([hi, mid, low], axis=0)


def split2(x):
    hi = x.astype(BF16)
    low = (x - hi.astype(F32)).astype(BF16)
    return hi, low


def dot(a, b, dims=NN):
    return lax.dot_general(a, b, dims, preferred_element_type=F32)


def dot_halves(x, w_hi, w_low):
    rows = x.shape[0]
    x_hi, x_low = split2(x)
    both = dot(jnp.concatenate([x_hi, x_low], axis=0), w_hi)
    return both[:rows] + both[rows:] + dot(x_hi, w_low)


def fold3(acc):
    rows = acc.shape[0] // 3
    return acc[:rows] + acc[rows : 2 * rows] + acc[2 * rows :]


def onehot(condition):
    return condition.astype(F32).astype(BF16)


def block_rows(ref, rows, first, count):
    return jnp.concatenate([ref[pl.ds((first + t) * rows, rows)] for t in range(count)], axis=1)


def block_shard(k):
    return lax.axis_index("blk") ^ k


def facing():
    return (lax.axis_index("sub") ^ lax.axis_index("blk")) & 1


def pack_kernel(
    residual_ref, agg_ref, lists_ref, counts_ref, coarse_ref,
    out_ref, lists_out, coarse_out,
    residual_buf, agg_buf, lists_buf, counts_buf, sems,
):
    sources = (residual_ref, agg_ref, lists_ref, counts_ref, coarse_ref)
    targets = (residual_buf, agg_buf, lists_buf, counts_buf, coarse_out)
    fetches = [pltpu.make_async_copy(a, b, sems.at[k]) for k, (a, b) in enumerate(zip(sources, targets))]
    for fetch in fetches:
        fetch.start()
    rows, cols = residual_buf.shape
    tiles = cols // LANES
    fetches[0].wait()
    for t in range(tiles):
        out_ref[t * rows : (t + 1) * rows] = residual_buf[:, t * LANES : (t + 1) * LANES]
    fetches[1].wait()
    codes = [agg_buf[:, t * LANES : (t + 1) * LANES].astype(F32) for t in range(tiles)]
    codes.append(jnp.zeros((out_ref.shape[0] - rows * tiles - tiles, LANES), F32))
    out_ref[rows * tiles :] = jnp.concatenate(codes, axis=0)
    fetches[2].wait()
    fetches[3].wait()
    slots = lax.broadcasted_iota(jnp.int32, (1, lists_buf.shape[1]), 1)
    for side in range(2):
        used = slots < counts_buf[:, side : side + 1]
        lists_out[side : side + 1] = jnp.where(used, lists_buf[side : side + 1], -1)
    fetches[4].wait()


def near_kernel(rows, tiles, packed_ref, core_ref, coarse_ref, rhs_ref, hi_ref, low_ref):
    coarse_len = hi_ref.shape[0]
    levels = lax.broadcasted_iota(jnp.int32, (coarse_len, tiles * LANES), 0)
    rhs = jnp.zeros((3 * rows, coarse_len), F32)
    for ref in (packed_ref, core_ref):
        codes = [ref[pl.ds(tiles * rows + t, 1)] for t in range(tiles)]
        unknowns = jnp.concatenate(codes, axis=1).astype(jnp.int32)
        rhs = rhs + dot(split3(block_rows(ref, rows, 0, tiles)), onehot(levels == unknowns), NT)
    rhs_ref[...] = fold3(rhs)
    stride = coarse_ref.shape[0] // coarse_len
    for tile in range(stride):
        at = slice(tile * LANES, (tile + 1) * LANES)
        hi_ref[:, at], low_ref[:, at] = split2(coarse_ref[pl.ds(tile, coarse_len, stride=stride), :])


def coarse_kernel(
    width, rows, tiles, packed_ref, core_ref, rhs_ref, far_ref, hi_ref, low_ref, send_ref, parts_ref
):
    for k, ref in enumerate((packed_ref, core_ref)):
        parts_ref[k] = split3(block_rows(ref, rows, 0, tiles))
    rhs = rhs_ref[...] + far_ref[...]
    half = rows // 2
    lane = lax.broadcasted_iota(jnp.int32, (half, LANES), 1)
    step = 2 * LANES
    for first in range(0, hi_ref.shape[1], step):
        at = slice(first, first + step)
        value = dot_halves(rhs, hi_ref[:, at], low_ref[:, at])
        for k in range(2):
            to = 2 * (first // LANES + k)
            part = value[:, k * LANES : (k + 1) * LANES]
            turned = pltpu.roll(part, width, 1)
            left = jnp.where(lane < width, part[:half], turned[half:])
            right = jnp.where(lane < width, turned[:half], part[half:])
            for copy in range(send_ref.shape[1]):
                for core in range(2):
                    piece = slice(core * half // 2, (core + 1) * half // 2)
                    send_ref[to, copy, core] = left[piece]
                    send_ref[to + 1, copy, core] = right[piece]


def margin_kernel(tiles, near_ref, y_ref, both_ref, lists_ref, out_ref, far_ref):
    half, rows, cols = near_ref.shape
    wanted = jnp.where(facing() == 1, lists_ref[1:2], lists_ref[0:1])
    local = lax.broadcasted_iota(jnp.int32, (cols, wanted.shape[1]), 0)
    for k, ref in enumerate((y_ref, both_ref)):
        far_ref[k] = split3(block_rows(ref, rows // 3, 0, tiles))
    total = jnp.zeros((rows, wanted.shape[1]), F32)
    for k in range(2 * half):
        part = near_ref[k] if k < half else far_ref[k - half]
        total = total + dot(part, onehot(local == wanted - block_shard(k) * cols))
    out_ref[...] = fold3(total)


def own_kernel(
    margin, near_ref, far_ref, agg_ref, fine_ref, out_ref, hi_ref, low_ref, hot_ref, agg_buf, fine_buf, sems
):
    half, rows, cols = near_ref.shape
    shards = 2 * half
    rows = rows // 3
    tiles = cols // LANES
    ext = fine_ref.shape[1]
    step = 2 * LANES
    per_block = tiles * LANES // step
    starts = [
        pl.multiple_of(margin + block_shard(k) * (tiles * LANES) + part * step, step)
        for k in range(shards)
        for part in range(per_block)
    ]
    starts += [0, ext - margin]
    sizes = [step] * (len(starts) - 2) + [margin] * 2
    fetch = pltpu.make_async_copy(agg_ref, agg_buf, sems.at[len(starts)])
    fetch.start()
    copies = []
    for k, (start, size) in enumerate(zip(starts, sizes)):
        copies.append(
            pltpu.make_async_copy(
                fine_ref.at[0, pl.ds(start, size)], fine_buf.at[pl.ds(start, size)], sems.at[k]
            )
        )
        copies[k].start()
    fetch.wait()
    levels = lax.broadcasted_iota(jnp.int32, hot_ref.shape, 0)
    hot_ref[...] = onehot(levels == agg_buf[...])
    total = jnp.zeros(out_ref.shape, F32)
    for k, start in enumerate(starts[:-2]):
        part = k % per_block
        at = k // per_block
        ref = near_ref if at < half else far_ref
        block = ref[at % half, :, part * step : (part + 1) * step]
        copies[k].wait()
        w_hi, w_low = split2(fine_buf[pl.ds(start, step)])
        both = dot(block[: 2 * rows], w_hi)
        total = total + (both[:rows] + both[rows:] + dot(block[:rows], w_low))
    out_ref[...] = total
    for side in range(2):
        start = starts[side - 2]
        copies[side - 2].wait()
        hi_ref[side], low_ref[side] = split2(fine_buf[start : start + margin])


def mine_kernel(halo_ref, hi_ref, low_ref, total_ref, out_ref, copy_ref):
    halo = halo_ref[...]
    copy_ref[...] = halo
    side = 1 - facing()
    out_ref[...] = total_ref[...] + dot_halves(halo, hi_ref[side], low_ref[side])


def other_kernel(halo_ref, hi_ref, low_ref, total_ref, out_ref):
    side = facing()
    out_ref[...] = total_ref[...] + dot_halves(halo_ref[...], hi_ref[side], low_ref[side])


def reduce_kernel(got_ref, out_ref):
    total = got_ref[0]
    for sub in range(1, got_ref.shape[0]):
        total = total + got_ref[sub]
    out_ref[...] = total


def tail_kernel(width, mine_ref, other_ref, hot_ref, total_ref, out_ref):
    odd = (lax.axis_index("blk") & 1) == 1
    chunks = []
    for k in range(mine_ref.shape[0]):
        mine, other = mine_ref[k], other_ref[k]
        pieces = [jnp.where(odd, other, mine), jnp.where(odd, mine, other)]
        chunks.append(jnp.concatenate(pieces, axis=0))
    lane = lax.broadcasted_iota(jnp.int32, chunks[0].shape, 1)
    top, bottom = [], []
    for left, right in zip(chunks[::2], chunks[1::2]):
        top.append(jnp.where(lane < width, left, pltpu.roll(right, width, 1)))
        bottom.append(jnp.where(lane < width, pltpu.roll(left, width, 1), right))
    coarse = jnp.concatenate([jnp.concatenate(top, axis=1), jnp.concatenate(bottom, axis=1)], axis=0)
    out_ref[...] = total_ref[...] + fold3(dot(split3(coarse), hot_ref[...]))


def whole(space=pltpu.VMEM):
    return pl.BlockSpec(memory_space=space)


def limit(mib):
    return pltpu.CompilerParams(vmem_limit_bytes=mib * MIB)


def in_hbm(x):
    return pltpu.with_memory_space_constraint(x, pltpu.HBM)


def weight(flops):
    return pl.CostEstimate(flops=flops, bytes_accessed=0, transcendentals=0)


def on_device(residual, fine_inverse, coarse_inverse, wanted_rows, wanted_count, aggregate):
    subs = lax.axis_size("sub")
    shards = lax.axis_size("blk")
    rows, cols = residual.shape
    tiles = cols // LANES
    margin = wanted_rows.shape[2]
    coarse_len = coarse_inverse.shape[0]
    width = coarse_len // shards
    chips = shards // 2
    packed_rows = -(-(rows * tiles + tiles) // 8) * 8
    core_swap = [(b, b ^ 1) for b in range(shards)]
    far_swap = [(b, b ^ 2) for b in range(shards)]
    both_swap = [(b, b ^ 3) for b in range(shards)]
    neighbours = []
    for sub in range(subs):
        for b in range(shards):
            other = sub ^ 1 if b % 2 == 0 else (sub + 1 if sub % 2 else sub - 1)
            if 0 <= other < subs:
                neighbours.append((sub * shards + b, other * shards + b))
    codes = aggregate[None]
    lists = wanted_rows[0]
    table = coarse_inverse.reshape(-1, LANES)
    packed_shape = (packed_rows, LANES)

    packed, lists, table = pl.pallas_call(
        pack_kernel,
        out_shape=(
            jax.ShapeDtypeStruct(packed_shape, F32),
            jax.ShapeDtypeStruct(lists.shape, jnp.int32),
            jax.ShapeDtypeStruct(table.shape, F32),
        ),
        in_specs=[whole(pl.ANY)] * 5,
        out_specs=(whole(),) * 3,
        scratch_shapes=[
            pltpu.VMEM(residual.shape, F32),
            pltpu.VMEM(codes.shape, jnp.int32),
            pltpu.VMEM(lists.shape, jnp.int32),
            pltpu.VMEM(wanted_count.shape, jnp.int32),
            pltpu.SemaphoreType.DMA((5,)),
        ],
        compiler_params=limit(4),
        name="pack",
    )(in_hbm(residual), in_hbm(codes), in_hbm(lists), in_hbm(wanted_count), in_hbm(table))
    lists = lax.ppermute(lists, ("sub", "blk"), neighbours)
    over_core = lax.ppermute(packed, "blk", core_swap)

    rhs, m_hi, m_low = pl.pallas_call(
        functools.partial(near_kernel, rows, tiles),
        out_shape=(
            jax.ShapeDtypeStruct((rows, coarse_len), F32),
            jax.ShapeDtypeStruct((coarse_len, subs * width), BF16),
            jax.ShapeDtypeStruct((coarse_len, subs * width), BF16),
        ),
        in_specs=[whole()] * 3,
        out_specs=(whole(),) * 3,
        compiler_params=limit(12),
        cost_estimate=weight(2 * 10**9),
        name="near",
    )(packed, over_core, table)
    far_rhs = lax.ppermute(rhs, "blk", far_swap)
    over_y = lax.ppermute(packed, "blk", far_swap)
    over_both = lax.ppermute(packed, "blk", both_swap)
    send, near = pl.pallas_call(
        functools.partial(coarse_kernel, width, rows, tiles),
        out_shape=(
            jax.ShapeDtypeStruct((subs, chips, 2, rows // 4, LANES), F32),
            jax.ShapeDtypeStruct((2, 3 * rows, cols), BF16),
        ),
        in_specs=[whole()] * 6,
        out_specs=(whole(), whole()),
        compiler_params=limit(12),
        cost_estimate=weight(8 * 10**9),
        name="coarse",
    )(packed, over_core, rhs, far_rhs, m_hi, m_low)
    flat = send.reshape((subs * shards,) + send.shape[3:])
    got = lax.all_to_all(flat, ("sub", "blk"), 0, 0, tiled=True)
    got = got.reshape((subs, shards) + flat.shape[1:])

    outgoing, far = pl.pallas_call(
        functools.partial(margin_kernel, tiles),
        out_shape=(
            jax.ShapeDtypeStruct((rows, margin), F32),
            jax.ShapeDtypeStruct((shards - 2, 3 * rows, cols), BF16),
        ),
        in_specs=[whole()] * 4,
        out_specs=(whole(), whole()),
        compiler_params=limit(8),
        cost_estimate=weight(4 * 10**9),
        name="margins",
    )(near, over_y, over_both, lists)
    halo = lax.ppermute(outgoing, ("sub", "blk"), neighbours)

    owned, w_hi, w_low, hot = pl.pallas_call(
        functools.partial(own_kernel, margin),
        out_shape=(
            jax.ShapeDtypeStruct((rows, cols), F32),
            jax.ShapeDtypeStruct((2, margin, cols), BF16),
            jax.ShapeDtypeStruct((2, margin, cols), BF16),
            jax.ShapeDtypeStruct((coarse_len, cols), BF16),
        ),
        in_specs=[whole(), whole(), whole(pl.ANY), whole(pl.ANY)],
        out_specs=(whole(),) * 4,
        scratch_shapes=[
            pltpu.VMEM(codes.shape, jnp.int32),
            pltpu.VMEM(fine_inverse.shape[1:], F32),
            pltpu.SemaphoreType.DMA((shards * tiles // 2 + 3,)),
        ],
        compiler_params=limit(16),
        cost_estimate=weight(40 * 10**9),
        name="owned",
    )(near, far, in_hbm(codes), in_hbm(fine_inverse))

    fine, mine = pl.pallas_call(
        mine_kernel,
        out_shape=(
            jax.ShapeDtypeStruct((rows, cols), F32),
            jax.ShapeDtypeStruct(halo.shape, F32),
        ),
        in_specs=[whole()] * 4,
        out_specs=(whole(), whole()),
        compiler_params=limit(12),
        cost_estimate=weight(4 * 10**9),
        name="mine",
    )(halo, w_hi, w_low, owned)
    other = lax.ppermute(mine, "blk", core_swap)
    fine = pl.pallas_call(
        other_kernel,
        out_shape=jax.ShapeDtypeStruct((rows, cols), F32),
        in_specs=[whole()] * 4,
        out_specs=whole(),
        compiler_params=limit(12),
        cost_estimate=weight(10**9),
        name="other",
    )(other, w_hi, w_low, fine)

    sums = pl.pallas_call(
        reduce_kernel,
        out_shape=jax.ShapeDtypeStruct(got.shape[1:], F32),
        in_specs=[whole()],
        out_specs=whole(),
        compiler_params=limit(8),
        cost_estimate=weight(10**8),
        name="reduce",
    )(got)
    other_sums = lax.ppermute(sums, "blk", core_swap)

    return pl.pallas_call(
        functools.partial(tail_kernel, width),
        out_shape=jax.ShapeDtypeStruct((rows, cols), F32),
        in_specs=[whole()] * 4,
        out_specs=whole(),
        compiler_params=limit(12),
        name="tail",
    )(sums, other_sums, hot, fine)


def solution(mesh):
    in_specs = (
        P(None, ("sub", "blk")),
        P("sub", None, "blk"),
        P("sub", "blk", None),
        P("sub", None, None),
        P("sub", None),
        P(("sub", "blk")),
    )
    out_specs = P(None, ("sub", "blk"))
    return jax.shard_map(
        on_device, mesh=mesh, in_specs=in_specs, out_specs=out_specs, check_vma=False
    )
```

```python
import functools

import jax
import jax.numpy as jnp
from jax import lax
from jax.experimental import pallas as pl
from jax.experimental.pallas import tpu as pltpu
from jax.sharding import PartitionSpec as P

BF16 = jnp.bfloat16
F32 = jnp.float32
NN = (((1,), (0,)), ((), ()))
NT = (((1,), (1,)), ((), ()))
LANES = 128
MIB = 1 << 20


def split3(x):
    hi = x.astype(BF16)
    rest = x - hi.astype(F32)
    mid = rest.astype(BF16)
    low = (rest - mid.astype(F32)).astype(BF16)
    return jnp.concatenate([hi, mid, low], axis=0)


def split2(x):
    hi = x.astype(BF16)
    low = (x - hi.astype(F32)).astype(BF16)
    return hi, low


def dot(a, b, dims=NN):
    return lax.dot_general(a, b, dims, preferred_element_type=F32)


def dot_halves(x, w_hi, w_low):
    rows = x.shape[0]
    x_hi, x_low = split2(x)
    both = dot(jnp.concatenate([x_hi, x_low], axis=0), w_hi)
    return both[:rows] + both[rows:] + dot(x_hi, w_low)


def fold3(acc):
    rows = acc.shape[0] // 3
    return acc[:rows] + acc[rows : 2 * rows] + acc[2 * rows :]


def onehot(condition):
    return condition.astype(F32).astype(BF16)


def block_rows(ref, rows, first, count):
    return jnp.concatenate([ref[pl.ds((first + t) * rows, rows)] for t in range(count)], axis=1)


def block_shard(k):
    return lax.axis_index("blk") ^ k


def facing():
    return (lax.axis_index("sub") ^ lax.axis_index("blk")) & 1


def pack_kernel(
    residual_ref, agg_ref, lists_ref, counts_ref, coarse_ref,
    out_ref, lists_out, coarse_out,
    residual_buf, agg_buf, lists_buf, counts_buf, sems,
):
    sources = (residual_ref, agg_ref, lists_ref, counts_ref, coarse_ref)
    targets = (residual_buf, agg_buf, lists_buf, counts_buf, coarse_out)
    fetches = [pltpu.make_async_copy(a, b, sems.at[k]) for k, (a, b) in enumerate(zip(sources, targets))]
    for fetch in fetches:
        fetch.start()
    rows, cols = residual_buf.shape
    tiles = cols // LANES
    fetches[0].wait()
    for t in range(tiles):
        out_ref[t * rows : (t + 1) * rows] = residual_buf[:, t * LANES : (t + 1) * LANES]
    fetches[1].wait()
    codes = [agg_buf[:, t * LANES : (t + 1) * LANES].astype(F32) for t in range(tiles)]
    codes.append(jnp.zeros((out_ref.shape[0] - rows * tiles - tiles, LANES), F32))
    out_ref[rows * tiles :] = jnp.concatenate(codes, axis=0)
    fetches[2].wait()
    fetches[3].wait()
    slots = lax.broadcasted_iota(jnp.int32, (1, lists_buf.shape[1]), 1)
    for side in range(2):
        used = slots < counts_buf[:, side : side + 1]
        lists_out[side : side + 1] = jnp.where(used, lists_buf[side : side + 1], -1)
    fetches[4].wait()


def near_kernel(
    rows, tiles, packed_ref, core_ref, core_agg_ref, coarse_ref, rhs_ref, hi_ref, low_ref
):
    coarse_len = hi_ref.shape[0]
    levels = lax.broadcasted_iota(jnp.int32, (coarse_len, tiles * LANES), 0)
    codes = [packed_ref[pl.ds(tiles * rows + t, 1)] for t in range(tiles)]
    unknowns = jnp.concatenate(codes, axis=1).astype(jnp.int32)
    rhs = dot(split3(block_rows(packed_ref, rows, 0, tiles)), onehot(levels == unknowns), NT)
    rhs = rhs + dot(split3(core_ref[...]), onehot(levels == core_agg_ref[...]), NT)
    rhs_ref[...] = fold3(rhs)
    stride = coarse_ref.shape[0] // coarse_len
    for tile in range(stride):
        at = slice(tile * LANES, (tile + 1) * LANES)
        hi_ref[:, at], low_ref[:, at] = split2(coarse_ref[pl.ds(tile, coarse_len, stride=stride), :])


def coarse_kernel(
    width, rows, tiles, packed_ref, core_ref, rhs_ref, far_ref, hi_ref, low_ref, send_ref, parts_ref
):
    parts_ref[0] = split3(block_rows(packed_ref, rows, 0, tiles))
    parts_ref[1] = split3(core_ref[...])
    rhs = rhs_ref[...] + far_ref[...]
    half = rows // 2
    lane = lax.broadcasted_iota(jnp.int32, (half, LANES), 1)
    step = 2 * LANES
    for first in range(0, hi_ref.shape[1], step):
        at = slice(first, first + step)
        value = dot_halves(rhs, hi_ref[:, at], low_ref[:, at])
        for k in range(2):
            to = 2 * (first // LANES + k)
            part = value[:, k * LANES : (k + 1) * LANES]
            turned = pltpu.roll(part, width, 1)
            left = jnp.where(lane < width, part[:half], turned[half:])
            right = jnp.where(lane < width, turned[:half], part[half:])
            for copy in range(send_ref.shape[1]):
                for core in range(2):
                    piece = slice(core * half // 2, (core + 1) * half // 2)
                    send_ref[to, copy, core] = left[piece]
                    send_ref[to + 1, copy, core] = right[piece]


def margin_kernel(tiles, near_ref, y_ref, both_ref, lists_ref, out_ref, far_ref):
    half, rows, cols = near_ref.shape
    wanted = jnp.where(facing() == 1, lists_ref[1:2], lists_ref[0:1])
    local = lax.broadcasted_iota(jnp.int32, (cols, wanted.shape[1]), 0)
    for k, ref in enumerate((y_ref, both_ref)):
        far_ref[k] = split3(block_rows(ref, rows // 3, 0, tiles))
    total = jnp.zeros((rows, wanted.shape[1]), F32)
    for k in range(2 * half):
        part = near_ref[k] if k < half else far_ref[k - half]
        total = total + dot(part, onehot(local == wanted - block_shard(k) * cols))
    out_ref[...] = fold3(total)


def own_kernel(
    margin, near_ref, far_ref, agg_ref, fine_ref, out_ref, hi_ref, low_ref, hot_ref, agg_buf, fine_buf, sems
):
    half, rows, cols = near_ref.shape
    shards = 2 * half
    rows = rows // 3
    tiles = cols // LANES
    ext = fine_ref.shape[1]
    step = 2 * LANES
    per_block = tiles * LANES // step
    starts = [
        pl.multiple_of(margin + block_shard(k) * (tiles * LANES) + part * step, step)
        for k in range(shards)
        for part in range(per_block)
    ]
    starts += [0, ext - margin]
    sizes = [step] * (len(starts) - 2) + [margin] * 2
    fetch = pltpu.make_async_copy(agg_ref, agg_buf, sems.at[len(starts)])
    fetch.start()
    copies = []
    for k, (start, size) in enumerate(zip(starts, sizes)):
        copies.append(
            pltpu.make_async_copy(
                fine_ref.at[0, pl.ds(start, size)], fine_buf.at[pl.ds(start, size)], sems.at[k]
            )
        )
        copies[k].start()
    fetch.wait()
    levels = lax.broadcasted_iota(jnp.int32, hot_ref.shape, 0)
    hot_ref[...] = onehot(levels == agg_buf[...])
    total = jnp.zeros(out_ref.shape, F32)
    for k, start in enumerate(starts[:-2]):
        part = k % per_block
        at = k // per_block
        ref = near_ref if at < half else far_ref
        block = ref[at % half, :, part * step : (part + 1) * step]
        copies[k].wait()
        w_hi, w_low = split2(fine_buf[pl.ds(start, step)])
        both = dot(block[: 2 * rows], w_hi)
        total = total + (both[:rows] + both[rows:] + dot(block[:rows], w_low))
    out_ref[...] = total
    for side in range(2):
        start = starts[side - 2]
        copies[side - 2].wait()
        hi_ref[side], low_ref[side] = split2(fine_buf[start : start + margin])


def mine_kernel(halo_ref, hi_ref, low_ref, total_ref, out_ref, copy_ref):
    halo = halo_ref[...]
    copy_ref[...] = halo
    side = 1 - facing()
    out_ref[...] = total_ref[...] + dot_halves(halo, hi_ref[side], low_ref[side])


def other_kernel(halo_ref, hi_ref, low_ref, total_ref, out_ref):
    side = facing()
    out_ref[...] = total_ref[...] + dot_halves(halo_ref[...], hi_ref[side], low_ref[side])


def reduce_kernel(got_ref, out_ref):
    total = got_ref[0]
    for sub in range(1, got_ref.shape[0]):
        total = total + got_ref[sub]
    out_ref[...] = total


def tail_kernel(width, mine_ref, other_ref, hot_ref, total_ref, out_ref):
    odd = (lax.axis_index("blk") & 1) == 1
    chunks = []
    for k in range(mine_ref.shape[0]):
        mine, other = mine_ref[k], other_ref[k]
        pieces = [jnp.where(odd, other, mine), jnp.where(odd, mine, other)]
        chunks.append(jnp.concatenate(pieces, axis=0))
    lane = lax.broadcasted_iota(jnp.int32, chunks[0].shape, 1)
    top, bottom = [], []
    for left, right in zip(chunks[::2], chunks[1::2]):
        top.append(jnp.where(lane < width, left, pltpu.roll(right, width, 1)))
        bottom.append(jnp.where(lane < width, pltpu.roll(left, width, 1), right))
    coarse = jnp.concatenate([jnp.concatenate(top, axis=1), jnp.concatenate(bottom, axis=1)], axis=0)
    out_ref[...] = total_ref[...] + fold3(dot(split3(coarse), hot_ref[...]))


def whole(space=pltpu.VMEM):
    return pl.BlockSpec(memory_space=space)


def limit(mib):
    return pltpu.CompilerParams(vmem_limit_bytes=mib * MIB)


def in_hbm(x):
    return pltpu.with_memory_space_constraint(x, pltpu.HBM)


def weight(flops):
    return pl.CostEstimate(flops=flops, bytes_accessed=0, transcendentals=0)


def on_device(residual, fine_inverse, coarse_inverse, wanted_rows, wanted_count, aggregate):
    subs = lax.axis_size("sub")
    shards = lax.axis_size("blk")
    rows, cols = residual.shape
    tiles = cols // LANES
    margin = wanted_rows.shape[2]
    coarse_len = coarse_inverse.shape[0]
    width = coarse_len // shards
    chips = shards // 2
    packed_rows = -(-(rows * tiles + tiles) // 8) * 8
    core_swap = [(b, b ^ 1) for b in range(shards)]
    far_swap = [(b, b ^ 2) for b in range(shards)]
    both_swap = [(b, b ^ 3) for b in range(shards)]
    neighbours = []
    for sub in range(subs):
        for b in range(shards):
            other = sub ^ 1 if b % 2 == 0 else (sub + 1 if sub % 2 else sub - 1)
            if 0 <= other < subs:
                neighbours.append((sub * shards + b, other * shards + b))
    codes = aggregate[None]
    lists = wanted_rows[0]
    table = coarse_inverse.reshape(-1, LANES)
    packed_shape = (packed_rows, LANES)

    packed, lists, table = pl.pallas_call(
        pack_kernel,
        out_shape=(
            jax.ShapeDtypeStruct(packed_shape, F32),
            jax.ShapeDtypeStruct(lists.shape, jnp.int32),
            jax.ShapeDtypeStruct(table.shape, F32),
        ),
        in_specs=[whole(pl.ANY)] * 5,
        out_specs=(whole(),) * 3,
        scratch_shapes=[
            pltpu.VMEM(residual.shape, F32),
            pltpu.VMEM(codes.shape, jnp.int32),
            pltpu.VMEM(lists.shape, jnp.int32),
            pltpu.VMEM(wanted_count.shape, jnp.int32),
            pltpu.SemaphoreType.DMA((5,)),
        ],
        compiler_params=limit(4),
        cost_estimate=weight(8 * 10**9),
        name="pack",
    )(in_hbm(residual), in_hbm(codes), in_hbm(lists), in_hbm(wanted_count), in_hbm(table))
    lists = lax.ppermute(lists, ("sub", "blk"), neighbours)
    over_core = lax.ppermute(residual, "blk", core_swap)
    core_codes = lax.ppermute(aggregate, "blk", core_swap)[None]

    rhs, m_hi, m_low = pl.pallas_call(
        functools.partial(near_kernel, rows, tiles),
        out_shape=(
            jax.ShapeDtypeStruct((rows, coarse_len), F32),
            jax.ShapeDtypeStruct((coarse_len, subs * width), BF16),
            jax.ShapeDtypeStruct((coarse_len, subs * width), BF16),
        ),
        in_specs=[whole()] * 4,
        out_specs=(whole(),) * 3,
        compiler_params=limit(12),
        cost_estimate=weight(2 * 10**9),
        name="near",
    )(packed, over_core, core_codes, table)
    far_rhs = lax.ppermute(rhs, "blk", far_swap)
    over_y = lax.ppermute(packed, "blk", far_swap)
    over_both = lax.ppermute(packed, "blk", both_swap)
    send, near = pl.pallas_call(
        functools.partial(coarse_kernel, width, rows, tiles),
        out_shape=(
            jax.ShapeDtypeStruct((subs, chips, 2, rows // 4, LANES), F32),
            jax.ShapeDtypeStruct((2, 3 * rows, cols), BF16),
        ),
        in_specs=[whole()] * 6,
        out_specs=(whole(), whole()),
        compiler_params=limit(12),
        cost_estimate=weight(8 * 10**9),
        name="coarse",
    )(packed, over_core, rhs, far_rhs, m_hi, m_low)
    flat = send.reshape((subs * shards,) + send.shape[3:])
    got = lax.all_to_all(flat, ("sub", "blk"), 0, 0, tiled=True)
    got = got.reshape((subs, shards) + flat.shape[1:])

    outgoing, far = pl.pallas_call(
        functools.partial(margin_kernel, tiles),
        out_shape=(
            jax.ShapeDtypeStruct((rows, margin), F32),
            jax.ShapeDtypeStruct((shards - 2, 3 * rows, cols), BF16),
        ),
        in_specs=[whole()] * 4,
        out_specs=(whole(), whole()),
        compiler_params=limit(8),
        cost_estimate=weight(4 * 10**9),
        name="margins",
    )(near, over_y, over_both, lists)
    halo = lax.ppermute(outgoing, ("sub", "blk"), neighbours)

    owned, w_hi, w_low, hot = pl.pallas_call(
        functools.partial(own_kernel, margin),
        out_shape=(
            jax.ShapeDtypeStruct((rows, cols), F32),
            jax.ShapeDtypeStruct((2, margin, cols), BF16),
            jax.ShapeDtypeStruct((2, margin, cols), BF16),
            jax.ShapeDtypeStruct((coarse_len, cols), BF16),
        ),
        in_specs=[whole(), whole(), whole(pl.ANY), whole(pl.ANY)],
        out_specs=(whole(),) * 4,
        scratch_shapes=[
            pltpu.VMEM(codes.shape, jnp.int32),
            pltpu.VMEM(fine_inverse.shape[1:], F32),
            pltpu.SemaphoreType.DMA((shards * tiles // 2 + 3,)),
        ],
        compiler_params=limit(16),
        cost_estimate=weight(40 * 10**9),
        name="owned",
    )(near, far, in_hbm(codes), in_hbm(fine_inverse))

    fine, mine = pl.pallas_call(
        mine_kernel,
        out_shape=(
            jax.ShapeDtypeStruct((rows, cols), F32),
            jax.ShapeDtypeStruct(halo.shape, F32),
        ),
        in_specs=[whole()] * 4,
        out_specs=(whole(), whole()),
        compiler_params=limit(12),
        cost_estimate=weight(4 * 10**9),
        name="mine",
    )(halo, w_hi, w_low, owned)
    other = lax.ppermute(mine, "blk", core_swap)
    fine = pl.pallas_call(
        other_kernel,
        out_shape=jax.ShapeDtypeStruct((rows, cols), F32),
        in_specs=[whole()] * 4,
        out_specs=whole(),
        compiler_params=limit(12),
        cost_estimate=weight(10**9),
        name="other",
    )(other, w_hi, w_low, fine)

    sums = pl.pallas_call(
        reduce_kernel,
        out_shape=jax.ShapeDtypeStruct(got.shape[1:], F32),
        in_specs=[whole()],
        out_specs=whole(),
        compiler_params=limit(8),
        cost_estimate=weight(10**8),
        name="reduce",
    )(got)
    other_sums = lax.ppermute(sums, "blk", core_swap)

    return pl.pallas_call(
        functools.partial(tail_kernel, width),
        out_shape=jax.ShapeDtypeStruct((rows, cols), F32),
        in_specs=[whole()] * 4,
        out_specs=whole(),
        compiler_params=limit(12),
        name="tail",
    )(sums, other_sums, hot, fine)


def solution(mesh):
    in_specs = (
        P(None, ("sub", "blk")),
        P("sub", None, "blk"),
        P("sub", "blk", None),
        P("sub", None, None),
        P("sub", None),
        P(("sub", "blk")),
    )
    out_specs = P(None, ("sub", "blk"))
    return jax.shard_map(
        on_device, mesh=mesh, in_specs=in_specs, out_specs=out_specs, check_vma=False
    )
```

```python
import functools

import jax
import jax.numpy as jnp
from jax import lax
from jax.experimental import pallas as pl
from jax.experimental.pallas import tpu as pltpu
from jax.sharding import PartitionSpec as P

BF16 = jnp.bfloat16
F32 = jnp.float32
NN = (((1,), (0,)), ((), ()))
NT = (((1,), (1,)), ((), ()))
LANES = 128
MIB = 1 << 20


def split3(x):
    hi = x.astype(BF16)
    rest = x - hi.astype(F32)
    mid = rest.astype(BF16)
    low = (rest - mid.astype(F32)).astype(BF16)
    return jnp.concatenate([hi, mid, low], axis=0)


def split2(x):
    hi = x.astype(BF16)
    low = (x - hi.astype(F32)).astype(BF16)
    return hi, low


def dot(a, b, dims=NN):
    return lax.dot_general(a, b, dims, preferred_element_type=F32)


def dot_halves(x, w_hi, w_low):
    rows = x.shape[0]
    x_hi, x_low = split2(x)
    both = dot(jnp.concatenate([x_hi, x_low], axis=0), w_hi)
    return both[:rows] + both[rows:] + dot(x_hi, w_low)


def fold3(acc):
    rows = acc.shape[0] // 3
    return acc[:rows] + acc[rows : 2 * rows] + acc[2 * rows :]


def onehot(condition):
    return condition.astype(F32).astype(BF16)


def block_rows(ref, rows, first, count):
    return jnp.concatenate([ref[pl.ds((first + t) * rows, rows)] for t in range(count)], axis=1)


def block_shard(k):
    return lax.axis_index("blk") ^ k


def facing():
    return (lax.axis_index("sub") ^ lax.axis_index("blk")) & 1


def pack_kernel(
    residual_ref, agg_ref, lists_ref, counts_ref, coarse_ref,
    out_ref, lists_out, coarse_out,
    residual_buf, agg_buf, lists_buf, counts_buf, sems,
):
    sources = (residual_ref, agg_ref, lists_ref, counts_ref, coarse_ref)
    targets = (residual_buf, agg_buf, lists_buf, counts_buf, coarse_out)
    fetches = [pltpu.make_async_copy(a, b, sems.at[k]) for k, (a, b) in enumerate(zip(sources, targets))]
    for fetch in fetches:
        fetch.start()
    rows, cols = residual_buf.shape
    tiles = cols // LANES
    fetches[0].wait()
    for t in range(tiles):
        out_ref[t * rows : (t + 1) * rows] = residual_buf[:, t * LANES : (t + 1) * LANES]
    fetches[1].wait()
    codes = [agg_buf[:, t * LANES : (t + 1) * LANES].astype(F32) for t in range(tiles)]
    codes.append(jnp.zeros((out_ref.shape[0] - rows * tiles - tiles, LANES), F32))
    out_ref[rows * tiles :] = jnp.concatenate(codes, axis=0)
    fetches[2].wait()
    fetches[3].wait()
    slots = lax.broadcasted_iota(jnp.int32, (1, lists_buf.shape[1]), 1)
    for side in range(2):
        used = slots < counts_buf[:, side : side + 1]
        lists_out[side : side + 1] = jnp.where(used, lists_buf[side : side + 1], -1)
    fetches[4].wait()


def near_kernel(
    rows, tiles, packed_ref, core_ref, core_agg_ref, coarse_ref, joint_ref, hi_ref, low_ref
):
    coarse_len = hi_ref.shape[0]
    levels = lax.broadcasted_iota(jnp.int32, (coarse_len, tiles * LANES), 0)
    codes = [packed_ref[pl.ds(tiles * rows + t, 1)] for t in range(tiles)]
    unknowns = jnp.concatenate(codes, axis=1).astype(jnp.int32)
    block = block_rows(packed_ref, rows, 0, tiles)
    rhs = dot(split3(block), onehot(levels == unknowns), NT)
    rhs = rhs + dot(split3(core_ref[...]), onehot(levels == core_agg_ref[...]), NT)
    joint_ref[:, :coarse_len] = fold3(rhs)
    joint_ref[:, coarse_len:] = block
    stride = coarse_ref.shape[0] // coarse_len
    for tile in range(stride):
        at = slice(tile * LANES, (tile + 1) * LANES)
        hi_ref[:, at], low_ref[:, at] = split2(coarse_ref[pl.ds(tile, coarse_len, stride=stride), :])


def coarse_kernel(
    width, rows, tiles, packed_ref, core_ref, joint_ref, far_ref, hi_ref, low_ref, send_ref, parts_ref
):
    parts_ref[0] = split3(block_rows(packed_ref, rows, 0, tiles))
    parts_ref[1] = split3(core_ref[...])
    coarse_len = hi_ref.shape[0]
    rhs = joint_ref[:, :coarse_len] + far_ref[:, :coarse_len]
    half = rows // 2
    lane = lax.broadcasted_iota(jnp.int32, (half, LANES), 1)
    step = 2 * LANES
    for first in range(0, hi_ref.shape[1], step):
        at = slice(first, first + step)
        value = dot_halves(rhs, hi_ref[:, at], low_ref[:, at])
        for k in range(2):
            to = 2 * (first // LANES + k)
            part = value[:, k * LANES : (k + 1) * LANES]
            turned = pltpu.roll(part, width, 1)
            left = jnp.where(lane < width, part[:half], turned[half:])
            right = jnp.where(lane < width, turned[:half], part[half:])
            for copy in range(send_ref.shape[1]):
                for core in range(2):
                    piece = slice(core * half // 2, (core + 1) * half // 2)
                    send_ref[to, copy, core] = left[piece]
                    send_ref[to + 1, copy, core] = right[piece]


def margin_kernel(near_ref, y_ref, both_ref, lists_ref, out_ref, far_ref):
    half, rows, cols = near_ref.shape
    wanted = jnp.where(facing() == 1, lists_ref[1:2], lists_ref[0:1])
    local = lax.broadcasted_iota(jnp.int32, (cols, wanted.shape[1]), 0)
    far_ref[0] = split3(y_ref[:, y_ref.shape[1] - cols :])
    far_ref[1] = split3(both_ref[...])
    total = jnp.zeros((rows, wanted.shape[1]), F32)
    for k in range(2 * half):
        part = near_ref[k] if k < half else far_ref[k - half]
        total = total + dot(part, onehot(local == wanted - block_shard(k) * cols))
    out_ref[...] = fold3(total)


def own_kernel(
    margin, near_ref, far_ref, agg_ref, fine_ref, out_ref, hi_ref, low_ref, hot_ref, agg_buf, fine_buf, sems
):
    half, rows, cols = near_ref.shape
    shards = 2 * half
    rows = rows // 3
    tiles = cols // LANES
    ext = fine_ref.shape[1]
    step = 2 * LANES
    per_block = tiles * LANES // step
    starts = [
        pl.multiple_of(margin + block_shard(k) * (tiles * LANES) + part * step, step)
        for k in range(shards)
        for part in range(per_block)
    ]
    starts += [0, ext - margin]
    sizes = [step] * (len(starts) - 2) + [margin] * 2
    fetch = pltpu.make_async_copy(agg_ref, agg_buf, sems.at[len(starts)])
    fetch.start()
    copies = []
    for k, (start, size) in enumerate(zip(starts, sizes)):
        copies.append(
            pltpu.make_async_copy(
                fine_ref.at[0, pl.ds(start, size)], fine_buf.at[pl.ds(start, size)], sems.at[k]
            )
        )
        copies[k].start()
    fetch.wait()
    levels = lax.broadcasted_iota(jnp.int32, hot_ref.shape, 0)
    hot_ref[...] = onehot(levels == agg_buf[...])
    total = jnp.zeros(out_ref.shape, F32)
    for k, start in enumerate(starts[:-2]):
        part = k % per_block
        at = k // per_block
        ref = near_ref if at < half else far_ref
        block = ref[at % half, :, part * step : (part + 1) * step]
        copies[k].wait()
        w_hi, w_low = split2(fine_buf[pl.ds(start, step)])
        both = dot(block[: 2 * rows], w_hi)
        total = total + (both[:rows] + both[rows:] + dot(block[:rows], w_low))
    out_ref[...] = total
    for side in range(2):
        start = starts[side - 2]
        copies[side - 2].wait()
        hi_ref[side], low_ref[side] = split2(fine_buf[start : start + margin])


def mine_kernel(halo_ref, hi_ref, low_ref, total_ref, out_ref, copy_ref):
    halo = halo_ref[...]
    copy_ref[...] = halo
    side = 1 - facing()
    out_ref[...] = total_ref[...] + dot_halves(halo, hi_ref[side], low_ref[side])


def other_kernel(halo_ref, hi_ref, low_ref, total_ref, out_ref):
    side = facing()
    out_ref[...] = total_ref[...] + dot_halves(halo_ref[...], hi_ref[side], low_ref[side])


def reduce_kernel(got_ref, out_ref):
    total = got_ref[0]
    for sub in range(1, got_ref.shape[0]):
        total = total + got_ref[sub]
    out_ref[...] = total


def tail_kernel(width, mine_ref, other_ref, hot_ref, total_ref, out_ref):
    odd = (lax.axis_index("blk") & 1) == 1
    chunks = []
    for k in range(mine_ref.shape[0]):
        mine, other = mine_ref[k], other_ref[k]
        pieces = [jnp.where(odd, other, mine), jnp.where(odd, mine, other)]
        chunks.append(jnp.concatenate(pieces, axis=0))
    lane = lax.broadcasted_iota(jnp.int32, chunks[0].shape, 1)
    top, bottom = [], []
    for left, right in zip(chunks[::2], chunks[1::2]):
        top.append(jnp.where(lane < width, left, pltpu.roll(right, width, 1)))
        bottom.append(jnp.where(lane < width, pltpu.roll(left, width, 1), right))
    coarse = jnp.concatenate([jnp.concatenate(top, axis=1), jnp.concatenate(bottom, axis=1)], axis=0)
    out_ref[...] = total_ref[...] + fold3(dot(split3(coarse), hot_ref[...]))


def whole(space=pltpu.VMEM):
    return pl.BlockSpec(memory_space=space)


def limit(mib):
    return pltpu.CompilerParams(vmem_limit_bytes=mib * MIB)


def in_hbm(x):
    return pltpu.with_memory_space_constraint(x, pltpu.HBM)


def weight(flops):
    return pl.CostEstimate(flops=flops, bytes_accessed=0, transcendentals=0)


def on_device(residual, fine_inverse, coarse_inverse, wanted_rows, wanted_count, aggregate):
    subs = lax.axis_size("sub")
    shards = lax.axis_size("blk")
    rows, cols = residual.shape
    tiles = cols // LANES
    margin = wanted_rows.shape[2]
    coarse_len = coarse_inverse.shape[0]
    width = coarse_len // shards
    chips = shards // 2
    packed_rows = -(-(rows * tiles + tiles) // 8) * 8
    core_swap = [(b, b ^ 1) for b in range(shards)]
    far_swap = [(b, b ^ 2) for b in range(shards)]
    both_swap = [(b, b ^ 3) for b in range(shards)]
    neighbours = []
    for sub in range(subs):
        for b in range(shards):
            other = sub ^ 1 if b % 2 == 0 else (sub + 1 if sub % 2 else sub - 1)
            if 0 <= other < subs:
                neighbours.append((sub * shards + b, other * shards + b))
    codes = aggregate[None]
    lists = wanted_rows[0]
    table = coarse_inverse.reshape(-1, LANES)
    packed_shape = (packed_rows, LANES)

    packed, lists, table = pl.pallas_call(
        pack_kernel,
        out_shape=(
            jax.ShapeDtypeStruct(packed_shape, F32),
            jax.ShapeDtypeStruct(lists.shape, jnp.int32),
            jax.ShapeDtypeStruct(table.shape, F32),
        ),
        in_specs=[whole(pl.ANY)] * 5,
        out_specs=(whole(),) * 3,
        scratch_shapes=[
            pltpu.VMEM(residual.shape, F32),
            pltpu.VMEM(codes.shape, jnp.int32),
            pltpu.VMEM(lists.shape, jnp.int32),
            pltpu.VMEM(wanted_count.shape, jnp.int32),
            pltpu.SemaphoreType.DMA((5,)),
        ],
        compiler_params=limit(4),
        cost_estimate=weight(8 * 10**9),
        name="pack",
    )(in_hbm(residual), in_hbm(codes), in_hbm(lists), in_hbm(wanted_count), in_hbm(table))
    lists = lax.ppermute(lists, ("sub", "blk"), neighbours)
    over_core = lax.ppermute(residual, "blk", core_swap)
    core_codes = lax.ppermute(aggregate, "blk", core_swap)[None]

    joint, m_hi, m_low = pl.pallas_call(
        functools.partial(near_kernel, rows, tiles),
        out_shape=(
            jax.ShapeDtypeStruct((rows, coarse_len + cols), F32),
            jax.ShapeDtypeStruct((coarse_len, subs * width), BF16),
            jax.ShapeDtypeStruct((coarse_len, subs * width), BF16),
        ),
        in_specs=[whole()] * 4,
        out_specs=(whole(),) * 3,
        compiler_params=limit(12),
        cost_estimate=weight(2 * 10**9),
        name="near",
    )(packed, over_core, core_codes, table)
    over_y = lax.ppermute(joint, "blk", far_swap)
    over_both = lax.ppermute(residual, "blk", both_swap)
    send, near = pl.pallas_call(
        functools.partial(coarse_kernel, width, rows, tiles),
        out_shape=(
            jax.ShapeDtypeStruct((subs, chips, 2, rows // 4, LANES), F32),
            jax.ShapeDtypeStruct((2, 3 * rows, cols), BF16),
        ),
        in_specs=[whole()] * 6,
        out_specs=(whole(), whole()),
        compiler_params=limit(12),
        cost_estimate=weight(8 * 10**9),
        name="coarse",
    )(packed, over_core, joint, over_y, m_hi, m_low)
    flat = send.reshape((subs * shards,) + send.shape[3:])
    got = lax.all_to_all(flat, ("sub", "blk"), 0, 0, tiled=True)
    got = got.reshape((subs, shards) + flat.shape[1:])

    outgoing, far = pl.pallas_call(
        margin_kernel,
        out_shape=(
            jax.ShapeDtypeStruct((rows, margin), F32),
            jax.ShapeDtypeStruct((shards - 2, 3 * rows, cols), BF16),
        ),
        in_specs=[whole()] * 4,
        out_specs=(whole(), whole()),
        compiler_params=limit(8),
        cost_estimate=weight(4 * 10**9),
        name="margins",
    )(near, over_y, over_both, lists)
    halo = lax.ppermute(outgoing, ("sub", "blk"), neighbours)

    owned, w_hi, w_low, hot = pl.pallas_call(
        functools.partial(own_kernel, margin),
        out_shape=(
            jax.ShapeDtypeStruct((rows, cols), F32),
            jax.ShapeDtypeStruct((2, margin, cols), BF16),
            jax.ShapeDtypeStruct((2, margin, cols), BF16),
            jax.ShapeDtypeStruct((coarse_len, cols), BF16),
        ),
        in_specs=[whole(), whole(), whole(pl.ANY), whole(pl.ANY)],
        out_specs=(whole(),) * 4,
        scratch_shapes=[
            pltpu.VMEM(codes.shape, jnp.int32),
            pltpu.VMEM(fine_inverse.shape[1:], F32),
            pltpu.SemaphoreType.DMA((shards * tiles // 2 + 3,)),
        ],
        compiler_params=limit(16),
        cost_estimate=weight(40 * 10**9),
        name="owned",
    )(near, far, in_hbm(codes), in_hbm(fine_inverse))

    fine, mine = pl.pallas_call(
        mine_kernel,
        out_shape=(
            jax.ShapeDtypeStruct((rows, cols), F32),
            jax.ShapeDtypeStruct(halo.shape, F32),
        ),
        in_specs=[whole()] * 4,
        out_specs=(whole(), whole()),
        compiler_params=limit(12),
        cost_estimate=weight(4 * 10**9),
        name="mine",
    )(halo, w_hi, w_low, owned)
    other = lax.ppermute(mine, "blk", core_swap)
    fine = pl.pallas_call(
        other_kernel,
        out_shape=jax.ShapeDtypeStruct((rows, cols), F32),
        in_specs=[whole()] * 4,
        out_specs=whole(),
        compiler_params=limit(12),
        cost_estimate=weight(10**9),
        name="other",
    )(other, w_hi, w_low, fine)

    sums = pl.pallas_call(
        reduce_kernel,
        out_shape=jax.ShapeDtypeStruct(got.shape[1:], F32),
        in_specs=[whole()],
        out_specs=whole(),
        compiler_params=limit(8),
        cost_estimate=weight(10**8),
        name="reduce",
    )(got)
    other_sums = lax.ppermute(sums, "blk", core_swap)

    return pl.pallas_call(
        functools.partial(tail_kernel, width),
        out_shape=jax.ShapeDtypeStruct((rows, cols), F32),
        in_specs=[whole()] * 4,
        out_specs=whole(),
        compiler_params=limit(12),
        name="tail",
    )(sums, other_sums, hot, fine)


def solution(mesh):
    in_specs = (
        P(None, ("sub", "blk")),
        P("sub", None, "blk"),
        P("sub", "blk", None),
        P("sub", None, None),
        P("sub", None),
        P(("sub", "blk")),
    )
    out_specs = P(None, ("sub", "blk"))
    return jax.shard_map(
        on_device, mesh=mesh, in_specs=in_specs, out_specs=out_specs, check_vma=False
    )
```

```python
import functools

import jax
import jax.numpy as jnp
from jax import lax
from jax.experimental import pallas as pl
from jax.experimental.pallas import tpu as pltpu
from jax.sharding import PartitionSpec as P

BF16 = jnp.bfloat16
F32 = jnp.float32
NN = (((1,), (0,)), ((), ()))
NT = (((1,), (1,)), ((), ()))
LANES = 128
MIB = 1 << 20


def split3(x):
    hi = x.astype(BF16)
    rest = x - hi.astype(F32)
    mid = rest.astype(BF16)
    low = (rest - mid.astype(F32)).astype(BF16)
    return jnp.concatenate([hi, mid, low], axis=0)


def split2(x):
    hi = x.astype(BF16)
    low = (x - hi.astype(F32)).astype(BF16)
    return hi, low


def dot(a, b, dims=NN):
    return lax.dot_general(a, b, dims, preferred_element_type=F32)


def dot_halves(x, w_hi, w_low):
    rows = x.shape[0]
    x_hi, x_low = split2(x)
    both = dot(jnp.concatenate([x_hi, x_low], axis=0), w_hi)
    return both[:rows] + both[rows:] + dot(x_hi, w_low)


def fold3(acc):
    rows = acc.shape[0] // 3
    return acc[:rows] + acc[rows : 2 * rows] + acc[2 * rows :]


def onehot(condition):
    return condition.astype(F32).astype(BF16)


def block_rows(ref, rows, first, count):
    return jnp.concatenate([ref[pl.ds((first + t) * rows, rows)] for t in range(count)], axis=1)


def block_shard(k):
    return lax.axis_index("blk") ^ k


def facing():
    return (lax.axis_index("sub") ^ lax.axis_index("blk")) & 1


def pack_kernel(
    residual_ref, agg_ref, lists_ref, counts_ref, coarse_ref,
    out_ref, lists_out, coarse_out,
    residual_buf, agg_buf, lists_buf, counts_buf, sems,
):
    sources = (residual_ref, agg_ref, lists_ref, counts_ref, coarse_ref)
    targets = (residual_buf, agg_buf, lists_buf, counts_buf, coarse_out)
    fetches = [pltpu.make_async_copy(a, b, sems.at[k]) for k, (a, b) in enumerate(zip(sources, targets))]
    for fetch in fetches:
        fetch.start()
    rows, cols = residual_buf.shape
    tiles = cols // LANES
    fetches[0].wait()
    for t in range(tiles):
        out_ref[t * rows : (t + 1) * rows] = residual_buf[:, t * LANES : (t + 1) * LANES]
    fetches[1].wait()
    codes = [agg_buf[:, t * LANES : (t + 1) * LANES].astype(F32) for t in range(tiles)]
    codes.append(jnp.zeros((out_ref.shape[0] - rows * tiles - tiles, LANES), F32))
    out_ref[rows * tiles :] = jnp.concatenate(codes, axis=0)
    fetches[2].wait()
    fetches[3].wait()
    slots = lax.broadcasted_iota(jnp.int32, (1, lists_buf.shape[1]), 1)
    for side in range(2):
        used = slots < counts_buf[:, side : side + 1]
        lists_out[side : side + 1] = jnp.where(used, lists_buf[side : side + 1], -1)
    fetches[4].wait()


def near_kernel(
    rows, tiles, packed_ref, core_ref, core_agg_ref, coarse_ref, rhs_ref, hi_ref, low_ref
):
    coarse_len = hi_ref.shape[0]
    levels = lax.broadcasted_iota(jnp.int32, (coarse_len, tiles * LANES), 0)
    codes = [packed_ref[pl.ds(tiles * rows + t, 1)] for t in range(tiles)]
    unknowns = jnp.concatenate(codes, axis=1).astype(jnp.int32)
    rhs = dot(split3(block_rows(packed_ref, rows, 0, tiles)), onehot(levels == unknowns), NT)
    rhs = rhs + dot(split3(core_ref[...]), onehot(levels == core_agg_ref[...]), NT)
    rhs_ref[...] = fold3(rhs)
    stride = coarse_ref.shape[0] // coarse_len
    for tile in range(stride):
        at = slice(tile * LANES, (tile + 1) * LANES)
        hi_ref[:, at], low_ref[:, at] = split2(coarse_ref[pl.ds(tile, coarse_len, stride=stride), :])


def coarse_kernel(
    width, rows, tiles, sub_order, blk_order,
    packed_ref, core_ref, rhs_ref, far_ref, hi_ref, low_ref, send_ref, parts_ref,
):
    parts_ref[0] = split3(block_rows(packed_ref, rows, 0, tiles))
    parts_ref[1] = split3(core_ref[...])
    rhs = rhs_ref[...] + far_ref[...]
    half = rows // 2
    lane = lax.broadcasted_iota(jnp.int32, (half, LANES), 1)
    step = 2 * LANES
    for first in range(0, hi_ref.shape[1], step):
        at = slice(first, first + step)
        value = dot_halves(rhs, hi_ref[:, at], low_ref[:, at])
        for k in range(2):
            to = 2 * (first // LANES + k)
            part = value[:, k * LANES : (k + 1) * LANES]
            turned = pltpu.roll(part, width, 1)
            left = jnp.where(lane < width, part[:half], turned[half:])
            right = jnp.where(lane < width, turned[:half], part[half:])
            for copy in range(send_ref.shape[1] // 2):
                for core in range(2):
                    piece = slice(core * half // 2, (core + 1) * half // 2)
                    at = blk_order.index(2 * copy + core)
                    send_ref[sub_order.index(to), at] = left[piece]
                    send_ref[sub_order.index(to + 1), at] = right[piece]


def margin_kernel(tiles, near_ref, y_ref, both_ref, lists_ref, out_ref, far_ref):
    half, rows, cols = near_ref.shape
    wanted = jnp.where(facing() == 1, lists_ref[1:2], lists_ref[0:1])
    local = lax.broadcasted_iota(jnp.int32, (cols, wanted.shape[1]), 0)
    for k, ref in enumerate((y_ref, both_ref)):
        far_ref[k] = split3(block_rows(ref, rows // 3, 0, tiles))
    total = jnp.zeros((rows, wanted.shape[1]), F32)
    for k in range(2 * half):
        part = near_ref[k] if k < half else far_ref[k - half]
        total = total + dot(part, onehot(local == wanted - block_shard(k) * cols))
    out_ref[...] = fold3(total)


def own_kernel(
    margin, near_ref, far_ref, agg_ref, fine_ref, out_ref, hi_ref, low_ref, hot_ref, agg_buf, fine_buf, sems
):
    half, rows, cols = near_ref.shape
    shards = 2 * half
    rows = rows // 3
    tiles = cols // LANES
    ext = fine_ref.shape[1]
    step = 2 * LANES
    per_block = tiles * LANES // step
    starts = [
        pl.multiple_of(margin + block_shard(k) * (tiles * LANES) + part * step, step)
        for k in range(shards)
        for part in range(per_block)
    ]
    starts += [0, ext - margin]
    sizes = [step] * (len(starts) - 2) + [margin] * 2
    fetch = pltpu.make_async_copy(agg_ref, agg_buf, sems.at[len(starts)])
    fetch.start()
    copies = []
    for k, (start, size) in enumerate(zip(starts, sizes)):
        copies.append(
            pltpu.make_async_copy(
                fine_ref.at[0, pl.ds(start, size)], fine_buf.at[pl.ds(start, size)], sems.at[k]
            )
        )
        copies[k].start()
    fetch.wait()
    levels = lax.broadcasted_iota(jnp.int32, hot_ref.shape, 0)
    hot_ref[...] = onehot(levels == agg_buf[...])
    total = jnp.zeros(out_ref.shape, F32)
    for k, start in enumerate(starts[:-2]):
        part = k % per_block
        at = k // per_block
        ref = near_ref if at < half else far_ref
        block = ref[at % half, :, part * step : (part + 1) * step]
        copies[k].wait()
        w_hi, w_low = split2(fine_buf[pl.ds(start, step)])
        both = dot(block[: 2 * rows], w_hi)
        total = total + (both[:rows] + both[rows:] + dot(block[:rows], w_low))
    out_ref[...] = total
    for side in range(2):
        start = starts[side - 2]
        copies[side - 2].wait()
        hi_ref[side], low_ref[side] = split2(fine_buf[start : start + margin])


def mine_kernel(halo_ref, hi_ref, low_ref, total_ref, out_ref, copy_ref):
    halo = halo_ref[...]
    copy_ref[...] = halo
    side = 1 - facing()
    out_ref[...] = total_ref[...] + dot_halves(halo, hi_ref[side], low_ref[side])


def other_kernel(halo_ref, hi_ref, low_ref, total_ref, out_ref):
    side = facing()
    out_ref[...] = total_ref[...] + dot_halves(halo_ref[...], hi_ref[side], low_ref[side])


def reduce_kernel(blk_order, got_ref, out_ref):
    total = got_ref[0]
    for sub in range(1, got_ref.shape[0]):
        total = total + got_ref[sub]
    for k, b in enumerate(blk_order):
        out_ref[b] = total[k]


def tail_kernel(width, mine_ref, other_ref, hot_ref, total_ref, out_ref):
    odd = (lax.axis_index("blk") & 1) == 1
    chunks = []
    for k in range(mine_ref.shape[0]):
        mine, other = mine_ref[k], other_ref[k]
        pieces = [jnp.where(odd, other, mine), jnp.where(odd, mine, other)]
        chunks.append(jnp.concatenate(pieces, axis=0))
    lane = lax.broadcasted_iota(jnp.int32, chunks[0].shape, 1)
    top, bottom = [], []
    for left, right in zip(chunks[::2], chunks[1::2]):
        top.append(jnp.where(lane < width, left, pltpu.roll(right, width, 1)))
        bottom.append(jnp.where(lane < width, pltpu.roll(left, width, 1), right))
    coarse = jnp.concatenate([jnp.concatenate(top, axis=1), jnp.concatenate(bottom, axis=1)], axis=0)
    out_ref[...] = total_ref[...] + fold3(dot(split3(coarse), hot_ref[...]))


def whole(space=pltpu.VMEM):
    return pl.BlockSpec(memory_space=space)


def limit(mib):
    return pltpu.CompilerParams(vmem_limit_bytes=mib * MIB)


def in_hbm(x):
    return pltpu.with_memory_space_constraint(x, pltpu.HBM)


def weight(flops):
    return pl.CostEstimate(flops=flops, bytes_accessed=0, transcendentals=0)


def on_device(residual, fine_inverse, coarse_inverse, wanted_rows, wanted_count, aggregate):
    subs = lax.axis_size("sub")
    shards = lax.axis_size("blk")
    rows, cols = residual.shape
    tiles = cols // LANES
    margin = wanted_rows.shape[2]
    coarse_len = coarse_inverse.shape[0]
    width = coarse_len // shards
    packed_rows = -(-(rows * tiles + tiles) // 8) * 8
    lead = (subs // 2 + 1) % subs
    sub_order = [(lead + k) % subs for k in range(subs)]
    blk_order = [b ^ 2 for b in range(shards)]
    core_swap = [(b, b ^ 1) for b in range(shards)]
    far_swap = [(b, b ^ 2) for b in range(shards)]
    both_swap = [(b, b ^ 3) for b in range(shards)]
    neighbours = []
    for sub in range(subs):
        for b in range(shards):
            other = sub ^ 1 if b % 2 == 0 else (sub + 1 if sub % 2 else sub - 1)
            if 0 <= other < subs:
                neighbours.append((sub * shards + b, other * shards + b))
    codes = aggregate[None]
    lists = wanted_rows[0]
    table = coarse_inverse.reshape(-1, LANES)
    packed_shape = (packed_rows, LANES)

    packed, lists, table = pl.pallas_call(
        pack_kernel,
        out_shape=(
            jax.ShapeDtypeStruct(packed_shape, F32),
            jax.ShapeDtypeStruct(lists.shape, jnp.int32),
            jax.ShapeDtypeStruct(table.shape, F32),
        ),
        in_specs=[whole(pl.ANY)] * 5,
        out_specs=(whole(),) * 3,
        scratch_shapes=[
            pltpu.VMEM(residual.shape, F32),
            pltpu.VMEM(codes.shape, jnp.int32),
            pltpu.VMEM(lists.shape, jnp.int32),
            pltpu.VMEM(wanted_count.shape, jnp.int32),
            pltpu.SemaphoreType.DMA((5,)),
        ],
        compiler_params=limit(4),
        cost_estimate=weight(8 * 10**9),
        name="pack",
    )(in_hbm(residual), in_hbm(codes), in_hbm(lists), in_hbm(wanted_count), in_hbm(table))
    lists = lax.ppermute(lists, ("sub", "blk"), neighbours)
    over_core = lax.ppermute(residual, "blk", core_swap)
    core_codes = lax.ppermute(aggregate, "blk", core_swap)[None]

    rhs, m_hi, m_low = pl.pallas_call(
        functools.partial(near_kernel, rows, tiles),
        out_shape=(
            jax.ShapeDtypeStruct((rows, coarse_len), F32),
            jax.ShapeDtypeStruct((coarse_len, subs * width), BF16),
            jax.ShapeDtypeStruct((coarse_len, subs * width), BF16),
        ),
        in_specs=[whole()] * 4,
        out_specs=(whole(),) * 3,
        compiler_params=limit(12),
        cost_estimate=weight(2 * 10**9),
        name="near",
    )(packed, over_core, core_codes, table)
    far_rhs = lax.ppermute(rhs, "blk", far_swap)
    over_y = lax.ppermute(packed, "blk", far_swap)
    over_both = lax.ppermute(packed, "blk", both_swap)
    send, near = pl.pallas_call(
        functools.partial(coarse_kernel, width, rows, tiles, sub_order, blk_order),
        out_shape=(
            jax.ShapeDtypeStruct((subs, shards, rows // 4, LANES), F32),
            jax.ShapeDtypeStruct((2, 3 * rows, cols), BF16),
        ),
        in_specs=[whole()] * 6,
        out_specs=(whole(), whole()),
        compiler_params=limit(12),
        cost_estimate=weight(8 * 10**9),
        name="coarse",
    )(packed, over_core, rhs, far_rhs, m_hi, m_low)
    flat = send.reshape((subs * shards,) + send.shape[2:])
    members = [sub * shards + b for sub in sub_order for b in blk_order]
    got = lax.all_to_all(flat, ("sub", "blk"), 0, 0, axis_index_groups=[members], tiled=True)
    got = got.reshape((subs, shards) + flat.shape[1:])

    outgoing, far = pl.pallas_call(
        functools.partial(margin_kernel, tiles),
        out_shape=(
            jax.ShapeDtypeStruct((rows, margin), F32),
            jax.ShapeDtypeStruct((shards - 2, 3 * rows, cols), BF16),
        ),
        in_specs=[whole()] * 4,
        out_specs=(whole(), whole()),
        compiler_params=limit(8),
        cost_estimate=weight(4 * 10**9),
        name="margins",
    )(near, over_y, over_both, lists)
    halo = lax.ppermute(outgoing, ("sub", "blk"), neighbours)

    owned, w_hi, w_low, hot = pl.pallas_call(
        functools.partial(own_kernel, margin),
        out_shape=(
            jax.ShapeDtypeStruct((rows, cols), F32),
            jax.ShapeDtypeStruct((2, margin, cols), BF16),
            jax.ShapeDtypeStruct((2, margin, cols), BF16),
            jax.ShapeDtypeStruct((coarse_len, cols), BF16),
        ),
        in_specs=[whole(), whole(), whole(pl.ANY), whole(pl.ANY)],
        out_specs=(whole(),) * 4,
        scratch_shapes=[
            pltpu.VMEM(codes.shape, jnp.int32),
            pltpu.VMEM(fine_inverse.shape[1:], F32),
            pltpu.SemaphoreType.DMA((shards * tiles // 2 + 3,)),
        ],
        compiler_params=limit(16),
        cost_estimate=weight(40 * 10**9),
        name="owned",
    )(near, far, in_hbm(codes), in_hbm(fine_inverse))

    fine, mine = pl.pallas_call(
        mine_kernel,
        out_shape=(
            jax.ShapeDtypeStruct((rows, cols), F32),
            jax.ShapeDtypeStruct(halo.shape, F32),
        ),
        in_specs=[whole()] * 4,
        out_specs=(whole(), whole()),
        compiler_params=limit(12),
        cost_estimate=weight(4 * 10**9),
        name="mine",
    )(halo, w_hi, w_low, owned)
    other = lax.ppermute(mine, "blk", core_swap)
    fine = pl.pallas_call(
        other_kernel,
        out_shape=jax.ShapeDtypeStruct((rows, cols), F32),
        in_specs=[whole()] * 4,
        out_specs=whole(),
        compiler_params=limit(12),
        cost_estimate=weight(10**9),
        name="other",
    )(other, w_hi, w_low, fine)

    sums = pl.pallas_call(
        functools.partial(reduce_kernel, blk_order),
        out_shape=jax.ShapeDtypeStruct(got.shape[1:], F32),
        in_specs=[whole()],
        out_specs=whole(),
        compiler_params=limit(8),
        cost_estimate=weight(10**8),
        name="reduce",
    )(got)
    other_sums = lax.ppermute(sums, "blk", core_swap)

    return pl.pallas_call(
        functools.partial(tail_kernel, width),
        out_shape=jax.ShapeDtypeStruct((rows, cols), F32),
        in_specs=[whole()] * 4,
        out_specs=whole(),
        compiler_params=limit(12),
        name="tail",
    )(sums, other_sums, hot, fine)


def solution(mesh):
    in_specs = (
        P(None, ("sub", "blk")),
        P("sub", None, "blk"),
        P("sub", "blk", None),
        P("sub", None, None),
        P("sub", None),
        P(("sub", "blk")),
    )
    out_specs = P(None, ("sub", "blk"))
    return jax.shard_map(
        on_device, mesh=mesh, in_specs=in_specs, out_specs=out_specs, check_vma=False
    )
```

```python
import functools

import jax
import jax.numpy as jnp
from jax import lax
from jax.experimental import pallas as pl
from jax.experimental.pallas import tpu as pltpu
from jax.sharding import PartitionSpec as P

BF16 = jnp.bfloat16
F32 = jnp.float32
NN = (((1,), (0,)), ((), ()))
NT = (((1,), (1,)), ((), ()))
LANES = 128
MIB = 1 << 20


def split3(x):
    hi = x.astype(BF16)
    rest = x - hi.astype(F32)
    mid = rest.astype(BF16)
    low = (rest - mid.astype(F32)).astype(BF16)
    return jnp.concatenate([hi, mid, low], axis=0)


def split2(x):
    hi = x.astype(BF16)
    low = (x - hi.astype(F32)).astype(BF16)
    return hi, low


def dot(a, b, dims=NN):
    return lax.dot_general(a, b, dims, preferred_element_type=F32)


def dot_halves(x, w_hi, w_low):
    rows = x.shape[0]
    x_hi, x_low = split2(x)
    both = dot(jnp.concatenate([x_hi, x_low], axis=0), w_hi)
    return both[:rows] + both[rows:] + dot(x_hi, w_low)


def fold3(acc):
    rows = acc.shape[0] // 3
    return acc[:rows] + acc[rows : 2 * rows] + acc[2 * rows :]


def onehot(condition):
    return condition.astype(F32).astype(BF16)


def block_rows(ref, rows, first, count):
    return jnp.concatenate([ref[pl.ds((first + t) * rows, rows)] for t in range(count)], axis=1)


def block_shard(k):
    return lax.axis_index("blk") ^ k


def facing():
    return (lax.axis_index("sub") ^ lax.axis_index("blk")) & 1


def pack_kernel(
    residual_ref, agg_ref, lists_ref, counts_ref, coarse_ref,
    out_ref, lists_out, coarse_out,
    residual_buf, agg_buf, lists_buf, counts_buf, sems,
):
    sources = (residual_ref, agg_ref, lists_ref, counts_ref, coarse_ref)
    targets = (residual_buf, agg_buf, lists_buf, counts_buf, coarse_out)
    fetches = [pltpu.make_async_copy(a, b, sems.at[k]) for k, (a, b) in enumerate(zip(sources, targets))]
    for fetch in fetches:
        fetch.start()
    rows, cols = residual_buf.shape
    tiles = cols // LANES
    fetches[0].wait()
    for t in range(tiles):
        out_ref[t * rows : (t + 1) * rows] = residual_buf[:, t * LANES : (t + 1) * LANES]
    fetches[1].wait()
    codes = [agg_buf[:, t * LANES : (t + 1) * LANES].astype(F32) for t in range(tiles)]
    codes.append(jnp.zeros((out_ref.shape[0] - rows * tiles - tiles, LANES), F32))
    out_ref[rows * tiles :] = jnp.concatenate(codes, axis=0)
    fetches[2].wait()
    fetches[3].wait()
    slots = lax.broadcasted_iota(jnp.int32, (1, lists_buf.shape[1]), 1)
    for side in range(2):
        used = slots < counts_buf[:, side : side + 1]
        lists_out[side : side + 1] = jnp.where(used, lists_buf[side : side + 1], -1)
    fetches[4].wait()


def near_kernel(
    rows, tiles, packed_ref, core_ref, core_agg_ref, coarse_ref, rhs_ref, hi_ref, low_ref
):
    coarse_len = hi_ref.shape[0]
    levels = lax.broadcasted_iota(jnp.int32, (coarse_len, tiles * LANES), 0)
    codes = [packed_ref[pl.ds(tiles * rows + t, 1)] for t in range(tiles)]
    unknowns = jnp.concatenate(codes, axis=1).astype(jnp.int32)
    rhs = dot(split3(block_rows(packed_ref, rows, 0, tiles)), onehot(levels == unknowns), NT)
    rhs = rhs + dot(split3(core_ref[...]), onehot(levels == core_agg_ref[...]), NT)
    rhs_ref[...] = fold3(rhs)
    stride = coarse_ref.shape[0] // coarse_len
    for tile in range(stride):
        at = slice(tile * LANES, (tile + 1) * LANES)
        hi_ref[:, at], low_ref[:, at] = split2(coarse_ref[pl.ds(tile, coarse_len, stride=stride), :])


def coarse_kernel(
    width, rows, tiles, sub_order, blk_order,
    packed_ref, core_ref, rhs_ref, far_ref, hi_ref, low_ref, send_ref, parts_ref,
):
    parts_ref[0] = split3(block_rows(packed_ref, rows, 0, tiles))
    parts_ref[1] = split3(core_ref[...])
    rhs = rhs_ref[...] + far_ref[...]
    half = rows // 2
    lane = lax.broadcasted_iota(jnp.int32, (half, LANES), 1)
    step = 2 * LANES
    for first in range(0, hi_ref.shape[1], step):
        at = slice(first, first + step)
        value = dot_halves(rhs, hi_ref[:, at], low_ref[:, at])
        for k in range(2):
            to = 2 * (first // LANES + k)
            part = value[:, k * LANES : (k + 1) * LANES]
            turned = pltpu.roll(part, width, 1)
            left = jnp.where(lane < width, part[:half], turned[half:])
            right = jnp.where(lane < width, turned[:half], part[half:])
            for copy in range(send_ref.shape[1] // 2):
                for core in range(2):
                    piece = slice(core * half // 2, (core + 1) * half // 2)
                    at = blk_order.index(2 * copy + core)
                    send_ref[sub_order.index(to), at] = left[piece]
                    send_ref[sub_order.index(to + 1), at] = right[piece]


def margin_kernel(tiles, near_ref, y_ref, both_ref, lists_ref, out_ref, far_ref):
    half, rows, cols = near_ref.shape
    wanted = jnp.where(facing() == 1, lists_ref[1:2], lists_ref[0:1])
    local = lax.broadcasted_iota(jnp.int32, (cols, wanted.shape[1]), 0)
    for k, ref in enumerate((y_ref, both_ref)):
        far_ref[k] = split3(block_rows(ref, rows // 3, 0, tiles))
    total = jnp.zeros((rows, wanted.shape[1]), F32)
    for k in range(2 * half):
        part = near_ref[k] if k < half else far_ref[k - half]
        total = total + dot(part, onehot(local == wanted - block_shard(k) * cols))
    out_ref[...] = fold3(total)


def own_kernel(
    margin, near_ref, far_ref, agg_ref, fine_ref, out_ref, hi_ref, low_ref, hot_ref, agg_buf, fine_buf, sems
):
    half, rows, cols = near_ref.shape
    shards = 2 * half
    rows = rows // 3
    tiles = cols // LANES
    ext = fine_ref.shape[1]
    step = 2 * LANES
    per_block = tiles * LANES // step
    starts = [
        pl.multiple_of(margin + block_shard(k) * (tiles * LANES) + part * step, step)
        for k in range(shards)
        for part in range(per_block)
    ]
    starts += [0, ext - margin]
    sizes = [step] * (len(starts) - 2) + [margin] * 2
    fetch = pltpu.make_async_copy(agg_ref, agg_buf, sems.at[len(starts)])
    fetch.start()
    copies = []
    for k, (start, size) in enumerate(zip(starts, sizes)):
        copies.append(
            pltpu.make_async_copy(
                fine_ref.at[0, pl.ds(start, size)], fine_buf.at[pl.ds(start, size)], sems.at[k]
            )
        )
        copies[k].start()
    fetch.wait()
    levels = lax.broadcasted_iota(jnp.int32, hot_ref.shape, 0)
    hot_ref[...] = onehot(levels == agg_buf[...])
    total = jnp.zeros(out_ref.shape, F32)
    for k, start in enumerate(starts[:-2]):
        part = k % per_block
        at = k // per_block
        ref = near_ref if at < half else far_ref
        block = ref[at % half, :, part * step : (part + 1) * step]
        copies[k].wait()
        w_hi, w_low = split2(fine_buf[pl.ds(start, step)])
        both = dot(block[: 2 * rows], w_hi)
        total = total + (both[:rows] + both[rows:] + dot(block[:rows], w_low))
    out_ref[...] = total
    for side in range(2):
        start = starts[side - 2]
        copies[side - 2].wait()
        hi_ref[side], low_ref[side] = split2(fine_buf[start : start + margin])


def mine_kernel(halo_ref, hi_ref, low_ref, total_ref, out_ref, copy_ref):
    halo = halo_ref[...]
    copy_ref[...] = halo
    side = 1 - facing()
    out_ref[...] = total_ref[...] + dot_halves(halo, hi_ref[side], low_ref[side])


def other_kernel(halo_ref, hi_ref, low_ref, total_ref, out_ref):
    side = facing()
    out_ref[...] = total_ref[...] + dot_halves(halo_ref[...], hi_ref[side], low_ref[side])


def reduce_kernel(blk_order, got_ref, out_ref):
    total = got_ref[0]
    for sub in range(1, got_ref.shape[0]):
        total = total + got_ref[sub]
    for k, b in enumerate(blk_order):
        out_ref[b] = total[k]


def tail_kernel(width, mine_ref, other_ref, hot_ref, total_ref, out_ref):
    odd = (lax.axis_index("blk") & 1) == 1
    chunks = []
    for k in range(mine_ref.shape[0]):
        mine, other = mine_ref[k], other_ref[k]
        pieces = [jnp.where(odd, other, mine), jnp.where(odd, mine, other)]
        chunks.append(jnp.concatenate(pieces, axis=0))
    lane = lax.broadcasted_iota(jnp.int32, chunks[0].shape, 1)
    top, bottom = [], []
    for left, right in zip(chunks[::2], chunks[1::2]):
        top.append(jnp.where(lane < width, left, pltpu.roll(right, width, 1)))
        bottom.append(jnp.where(lane < width, pltpu.roll(left, width, 1), right))
    coarse = jnp.concatenate([jnp.concatenate(top, axis=1), jnp.concatenate(bottom, axis=1)], axis=0)
    out_ref[...] = total_ref[...] + fold3(dot(split3(coarse), hot_ref[...]))


def whole(space=pltpu.VMEM):
    return pl.BlockSpec(memory_space=space)


def limit(mib):
    return pltpu.CompilerParams(vmem_limit_bytes=mib * MIB)


def in_hbm(x):
    return pltpu.with_memory_space_constraint(x, pltpu.HBM)


def weight(flops):
    return pl.CostEstimate(flops=flops, bytes_accessed=0, transcendentals=0)


def on_device(residual, fine_inverse, coarse_inverse, wanted_rows, wanted_count, aggregate):
    subs = lax.axis_size("sub")
    shards = lax.axis_size("blk")
    rows, cols = residual.shape
    tiles = cols // LANES
    margin = wanted_rows.shape[2]
    coarse_len = coarse_inverse.shape[0]
    width = coarse_len // shards
    packed_rows = -(-(rows * tiles + tiles) // 8) * 8
    lead = subs - 1
    sub_order = [(lead + k) % subs for k in range(subs)]
    blk_order = [b ^ 2 for b in range(shards)]
    core_swap = [(b, b ^ 1) for b in range(shards)]
    far_swap = [(b, b ^ 2) for b in range(shards)]
    both_swap = [(b, b ^ 3) for b in range(shards)]
    neighbours = []
    for sub in range(subs):
        for b in range(shards):
            other = sub ^ 1 if b % 2 == 0 else (sub + 1 if sub % 2 else sub - 1)
            if 0 <= other < subs:
                neighbours.append((sub * shards + b, other * shards + b))
    codes = aggregate[None]
    lists = wanted_rows[0]
    table = coarse_inverse.reshape(-1, LANES)
    packed_shape = (packed_rows, LANES)

    packed, lists, table = pl.pallas_call(
        pack_kernel,
        out_shape=(
            jax.ShapeDtypeStruct(packed_shape, F32),
            jax.ShapeDtypeStruct(lists.shape, jnp.int32),
            jax.ShapeDtypeStruct(table.shape, F32),
        ),
        in_specs=[whole(pl.ANY)] * 5,
        out_specs=(whole(),) * 3,
        scratch_shapes=[
            pltpu.VMEM(residual.shape, F32),
            pltpu.VMEM(codes.shape, jnp.int32),
            pltpu.VMEM(lists.shape, jnp.int32),
            pltpu.VMEM(wanted_count.shape, jnp.int32),
            pltpu.SemaphoreType.DMA((5,)),
        ],
        compiler_params=limit(4),
        cost_estimate=weight(8 * 10**9),
        name="pack",
    )(in_hbm(residual), in_hbm(codes), in_hbm(lists), in_hbm(wanted_count), in_hbm(table))
    lists = lax.ppermute(lists, ("sub", "blk"), neighbours)
    over_core = lax.ppermute(residual, "blk", core_swap)
    core_codes = lax.ppermute(aggregate, "blk", core_swap)[None]

    rhs, m_hi, m_low = pl.pallas_call(
        functools.partial(near_kernel, rows, tiles),
        out_shape=(
            jax.ShapeDtypeStruct((rows, coarse_len), F32),
            jax.ShapeDtypeStruct((coarse_len, subs * width), BF16),
            jax.ShapeDtypeStruct((coarse_len, subs * width), BF16),
        ),
        in_specs=[whole()] * 4,
        out_specs=(whole(),) * 3,
        compiler_params=limit(12),
        cost_estimate=weight(2 * 10**9),
        name="near",
    )(packed, over_core, core_codes, table)
    far_rhs = lax.ppermute(rhs, "blk", far_swap)
    over_y = lax.ppermute(packed, "blk", far_swap)
    over_both = lax.ppermute(packed, "blk", both_swap)
    send, near = pl.pallas_call(
        functools.partial(coarse_kernel, width, rows, tiles, sub_order, blk_order),
        out_shape=(
            jax.ShapeDtypeStruct((subs, shards, rows // 4, LANES), F32),
            jax.ShapeDtypeStruct((2, 3 * rows, cols), BF16),
        ),
        in_specs=[whole()] * 6,
        out_specs=(whole(), whole()),
        compiler_params=limit(12),
        cost_estimate=weight(8 * 10**9),
        name="coarse",
    )(packed, over_core, rhs, far_rhs, m_hi, m_low)
    flat = send.reshape((subs * shards,) + send.shape[2:])
    members = [sub * shards + b for sub in sub_order for b in blk_order]
    got = lax.all_to_all(flat, ("sub", "blk"), 0, 0, axis_index_groups=[members], tiled=True)
    got = got.reshape((subs, shards) + flat.shape[1:])

    outgoing, far = pl.pallas_call(
        functools.partial(margin_kernel, tiles),
        out_shape=(
            jax.ShapeDtypeStruct((rows, margin), F32),
            jax.ShapeDtypeStruct((shards - 2, 3 * rows, cols), BF16),
        ),
        in_specs=[whole()] * 4,
        out_specs=(whole(), whole()),
        compiler_params=limit(8),
        cost_estimate=weight(4 * 10**9),
        name="margins",
    )(near, over_y, over_both, lists)
    halo = lax.ppermute(outgoing, ("sub", "blk"), neighbours)

    owned, w_hi, w_low, hot = pl.pallas_call(
        functools.partial(own_kernel, margin),
        out_shape=(
            jax.ShapeDtypeStruct((rows, cols), F32),
            jax.ShapeDtypeStruct((2, margin, cols), BF16),
            jax.ShapeDtypeStruct((2, margin, cols), BF16),
            jax.ShapeDtypeStruct((coarse_len, cols), BF16),
        ),
        in_specs=[whole(), whole(), whole(pl.ANY), whole(pl.ANY)],
        out_specs=(whole(),) * 4,
        scratch_shapes=[
            pltpu.VMEM(codes.shape, jnp.int32),
            pltpu.VMEM(fine_inverse.shape[1:], F32),
            pltpu.SemaphoreType.DMA((shards * tiles // 2 + 3,)),
        ],
        compiler_params=limit(16),
        cost_estimate=weight(40 * 10**9),
        name="owned",
    )(near, far, in_hbm(codes), in_hbm(fine_inverse))

    fine, mine = pl.pallas_call(
        mine_kernel,
        out_shape=(
            jax.ShapeDtypeStruct((rows, cols), F32),
            jax.ShapeDtypeStruct(halo.shape, F32),
        ),
        in_specs=[whole()] * 4,
        out_specs=(whole(), whole()),
        compiler_params=limit(12),
        cost_estimate=weight(4 * 10**9),
        name="mine",
    )(halo, w_hi, w_low, owned)
    other = lax.ppermute(mine, "blk", core_swap)
    fine = pl.pallas_call(
        other_kernel,
        out_shape=jax.ShapeDtypeStruct((rows, cols), F32),
        in_specs=[whole()] * 4,
        out_specs=whole(),
        compiler_params=limit(12),
        cost_estimate=weight(10**9),
        name="other",
    )(other, w_hi, w_low, fine)

    sums = pl.pallas_call(
        functools.partial(reduce_kernel, blk_order),
        out_shape=jax.ShapeDtypeStruct(got.shape[1:], F32),
        in_specs=[whole()],
        out_specs=whole(),
        compiler_params=limit(8),
        cost_estimate=weight(10**8),
        name="reduce",
    )(got)
    other_sums = lax.ppermute(sums, "blk", core_swap)

    return pl.pallas_call(
        functools.partial(tail_kernel, width),
        out_shape=jax.ShapeDtypeStruct((rows, cols), F32),
        in_specs=[whole()] * 4,
        out_specs=whole(),
        compiler_params=limit(12),
        name="tail",
    )(sums, other_sums, hot, fine)


def solution(mesh):
    in_specs = (
        P(None, ("sub", "blk")),
        P("sub", None, "blk"),
        P("sub", "blk", None),
        P("sub", None, None),
        P("sub", None),
        P(("sub", "blk")),
    )
    out_specs = P(None, ("sub", "blk"))
    return jax.shard_map(
        on_device, mesh=mesh, in_specs=in_specs, out_specs=out_specs, check_vma=False
    )
```

```python
import functools

import jax
import jax.numpy as jnp
from jax import lax
from jax.experimental import pallas as pl
from jax.experimental.pallas import tpu as pltpu
from jax.sharding import PartitionSpec as P

BF16 = jnp.bfloat16
F32 = jnp.float32
NN = (((1,), (0,)), ((), ()))
NT = (((1,), (1,)), ((), ()))
LANES = 128
MIB = 1 << 20


def split3(x):
    hi = x.astype(BF16)
    rest = x - hi.astype(F32)
    mid = rest.astype(BF16)
    low = (rest - mid.astype(F32)).astype(BF16)
    return jnp.concatenate([hi, mid, low], axis=0)


def split2(x):
    hi = x.astype(BF16)
    low = (x - hi.astype(F32)).astype(BF16)
    return hi, low


def dot(a, b, dims=NN):
    return lax.dot_general(a, b, dims, preferred_element_type=F32)


def dot_halves(x, w_hi, w_low):
    rows = x.shape[0]
    x_hi, x_low = split2(x)
    both = dot(jnp.concatenate([x_hi, x_low], axis=0), w_hi)
    return both[:rows] + both[rows:] + dot(x_hi, w_low)


def fold3(acc):
    rows = acc.shape[0] // 3
    return acc[:rows] + acc[rows : 2 * rows] + acc[2 * rows :]


def onehot(condition):
    return condition.astype(F32).astype(BF16)


def block_rows(ref, rows, first, count):
    return jnp.concatenate([ref[pl.ds((first + t) * rows, rows)] for t in range(count)], axis=1)


def block_shard(k):
    return lax.axis_index("blk") ^ k


def facing():
    return (lax.axis_index("sub") ^ lax.axis_index("blk")) & 1


def pack_kernel(
    residual_ref, agg_ref, lists_ref, counts_ref, coarse_ref,
    out_ref, lists_out, coarse_out,
    residual_buf, agg_buf, lists_buf, counts_buf, sems,
):
    sources = (residual_ref, agg_ref, lists_ref, counts_ref, coarse_ref)
    targets = (residual_buf, agg_buf, lists_buf, counts_buf, coarse_out)
    fetches = [pltpu.make_async_copy(a, b, sems.at[k]) for k, (a, b) in enumerate(zip(sources, targets))]
    for fetch in fetches:
        fetch.start()
    rows, cols = residual_buf.shape
    tiles = cols // LANES
    fetches[0].wait()
    for t in range(tiles):
        out_ref[t * rows : (t + 1) * rows] = residual_buf[:, t * LANES : (t + 1) * LANES]
    fetches[1].wait()
    codes = [agg_buf[:, t * LANES : (t + 1) * LANES].astype(F32) for t in range(tiles)]
    codes.append(jnp.zeros((out_ref.shape[0] - rows * tiles - tiles, LANES), F32))
    out_ref[rows * tiles :] = jnp.concatenate(codes, axis=0)
    fetches[2].wait()
    fetches[3].wait()
    slots = lax.broadcasted_iota(jnp.int32, (1, lists_buf.shape[1]), 1)
    for side in range(2):
        used = slots < counts_buf[:, side : side + 1]
        lists_out[side : side + 1] = jnp.where(used, lists_buf[side : side + 1], -1)
    fetches[4].wait()


def near_kernel(
    rows, tiles, packed_ref, core_ref, core_agg_ref, coarse_ref, rhs_ref, hi_ref, low_ref
):
    coarse_len = hi_ref.shape[0]
    levels = lax.broadcasted_iota(jnp.int32, (coarse_len, tiles * LANES), 0)
    codes = [packed_ref[pl.ds(tiles * rows + t, 1)] for t in range(tiles)]
    unknowns = jnp.concatenate(codes, axis=1).astype(jnp.int32)
    rhs = dot(split3(block_rows(packed_ref, rows, 0, tiles)), onehot(levels == unknowns), NT)
    rhs = rhs + dot(split3(core_ref[...]), onehot(levels == core_agg_ref[...]), NT)
    rhs_ref[...] = fold3(rhs)
    stride = coarse_ref.shape[0] // coarse_len
    for tile in range(stride):
        at = slice(tile * LANES, (tile + 1) * LANES)
        hi_ref[:, at], low_ref[:, at] = split2(coarse_ref[pl.ds(tile, coarse_len, stride=stride), :])


def coarse_kernel(
    width, rows, tiles, sub_order, blk_order,
    rhs_ref, far_ref, hi_ref, low_ref, send_ref, order_ref,
):
    order_ref[...] = jnp.zeros(order_ref.shape, F32)
    rhs = rhs_ref[...] + far_ref[...]
    half = rows // 2
    lane = lax.broadcasted_iota(jnp.int32, (half, LANES), 1)
    step = 2 * LANES
    for first in range(0, hi_ref.shape[1], step):
        at = slice(first, first + step)
        value = dot_halves(rhs, hi_ref[:, at], low_ref[:, at])
        for k in range(2):
            to = 2 * (first // LANES + k)
            part = value[:, k * LANES : (k + 1) * LANES]
            turned = pltpu.roll(part, width, 1)
            left = jnp.where(lane < width, part[:half], turned[half:])
            right = jnp.where(lane < width, turned[:half], part[half:])
            for copy in range(send_ref.shape[1] // 2):
                for core in range(2):
                    piece = slice(core * half // 2, (core + 1) * half // 2)
                    at = blk_order.index(2 * copy + core)
                    send_ref[sub_order.index(to), at] = left[piece]
                    send_ref[sub_order.index(to + 1), at] = right[piece]


def margin_kernel(
    tiles, packed_ref, core_ref, y_ref, both_ref, lists_ref, order_ref, out_ref, near_ref, far_ref
):
    half, rows, cols = near_ref.shape
    wanted = jnp.where(facing() == 1, lists_ref[1:2], lists_ref[0:1])
    local = lax.broadcasted_iota(jnp.int32, (cols, wanted.shape[1]), 0)
    near_ref[0] = split3(block_rows(packed_ref, rows // 3, 0, tiles))
    near_ref[1] = split3(core_ref[...])
    for k, ref in enumerate((y_ref, both_ref)):
        far_ref[k] = split3(block_rows(ref, rows // 3, 0, tiles))
    total = jnp.zeros((rows, wanted.shape[1]), F32)
    for k in range(2 * half):
        part = near_ref[k] if k < half else far_ref[k - half]
        total = total + dot(part, onehot(local == wanted - block_shard(k) * cols))
    out_ref[...] = fold3(total)


def own_kernel(
    margin, near_ref, far_ref, agg_ref, fine_ref, out_ref, hi_ref, low_ref, hot_ref, agg_buf, fine_buf, sems
):
    half, rows, cols = near_ref.shape
    shards = 2 * half
    rows = rows // 3
    tiles = cols // LANES
    ext = fine_ref.shape[1]
    step = 2 * LANES
    per_block = tiles * LANES // step
    starts = [
        pl.multiple_of(margin + block_shard(k) * (tiles * LANES) + part * step, step)
        for k in range(shards)
        for part in range(per_block)
    ]
    starts += [0, ext - margin]
    sizes = [step] * (len(starts) - 2) + [margin] * 2
    fetch = pltpu.make_async_copy(agg_ref, agg_buf, sems.at[len(starts)])
    fetch.start()
    copies = []
    for k, (start, size) in enumerate(zip(starts, sizes)):
        copies.append(
            pltpu.make_async_copy(
                fine_ref.at[0, pl.ds(start, size)], fine_buf.at[pl.ds(start, size)], sems.at[k]
            )
        )
        copies[k].start()
    fetch.wait()
    levels = lax.broadcasted_iota(jnp.int32, hot_ref.shape, 0)
    hot_ref[...] = onehot(levels == agg_buf[...])
    total = jnp.zeros(out_ref.shape, F32)
    for k, start in enumerate(starts[:-2]):
        part = k % per_block
        at = k // per_block
        ref = near_ref if at < half else far_ref
        block = ref[at % half, :, part * step : (part + 1) * step]
        copies[k].wait()
        w_hi, w_low = split2(fine_buf[pl.ds(start, step)])
        both = dot(block[: 2 * rows], w_hi)
        total = total + (both[:rows] + both[rows:] + dot(block[:rows], w_low))
    out_ref[...] = total
    for side in range(2):
        start = starts[side - 2]
        copies[side - 2].wait()
        hi_ref[side], low_ref[side] = split2(fine_buf[start : start + margin])


def mine_kernel(halo_ref, hi_ref, low_ref, total_ref, out_ref, copy_ref):
    halo = halo_ref[...]
    copy_ref[...] = halo
    side = 1 - facing()
    out_ref[...] = total_ref[...] + dot_halves(halo, hi_ref[side], low_ref[side])


def other_kernel(halo_ref, hi_ref, low_ref, total_ref, out_ref):
    side = facing()
    out_ref[...] = total_ref[...] + dot_halves(halo_ref[...], hi_ref[side], low_ref[side])


def reduce_kernel(blk_order, got_ref, out_ref):
    total = got_ref[0]
    for sub in range(1, got_ref.shape[0]):
        total = total + got_ref[sub]
    for k, b in enumerate(blk_order):
        out_ref[b] = total[k]


def tail_kernel(width, mine_ref, other_ref, hot_ref, total_ref, out_ref, out_buf, sems):
    odd = (lax.axis_index("blk") & 1) == 1
    chunks = []
    for k in range(mine_ref.shape[0]):
        mine, other = mine_ref[k], other_ref[k]
        pieces = [jnp.where(odd, other, mine), jnp.where(odd, mine, other)]
        chunks.append(jnp.concatenate(pieces, axis=0))
    lane = lax.broadcasted_iota(jnp.int32, chunks[0].shape, 1)
    top, bottom = [], []
    for left, right in zip(chunks[::2], chunks[1::2]):
        top.append(jnp.where(lane < width, left, pltpu.roll(right, width, 1)))
        bottom.append(jnp.where(lane < width, pltpu.roll(left, width, 1), right))
    coarse = jnp.concatenate([jnp.concatenate(top, axis=1), jnp.concatenate(bottom, axis=1)], axis=0)
    parts = split3(coarse)
    step = out_buf.shape[1] // 2
    sends = []
    for k in range(2):
        at = slice(k * step, (k + 1) * step)
        out_buf[:, at] = total_ref[:, at] + fold3(dot(parts, hot_ref[:, at]))
        there = pl.ds(k * step, step)
        sends.append(pltpu.make_async_copy(out_buf.at[:, there], out_ref.at[:, there], sems.at[k]))
        sends[k].start()
    for send in sends:
        send.wait()


def whole(space=pltpu.VMEM):
    return pl.BlockSpec(memory_space=space)


def limit(mib):
    return pltpu.CompilerParams(vmem_limit_bytes=mib * MIB)


def in_hbm(x):
    return pltpu.with_memory_space_constraint(x, pltpu.HBM)


def weight(flops):
    return pl.CostEstimate(flops=flops, bytes_accessed=0, transcendentals=0)


def on_device(residual, fine_inverse, coarse_inverse, wanted_rows, wanted_count, aggregate):
    subs = lax.axis_size("sub")
    shards = lax.axis_size("blk")
    rows, cols = residual.shape
    tiles = cols // LANES
    margin = wanted_rows.shape[2]
    coarse_len = coarse_inverse.shape[0]
    width = coarse_len // shards
    packed_rows = -(-(rows * tiles + tiles) // 8) * 8
    lead = (subs // 2 + 1) % subs
    sub_order = [(lead + k) % subs for k in range(subs)]
    blk_order = [b ^ 2 for b in range(shards)]
    core_swap = [(b, b ^ 1) for b in range(shards)]
    far_swap = [(b, b ^ 2) for b in range(shards)]
    both_swap = [(b, b ^ 3) for b in range(shards)]
    neighbours = []
    for sub in range(subs):
        for b in range(shards):
            other = sub ^ 1 if b % 2 == 0 else (sub + 1 if sub % 2 else sub - 1)
            if 0 <= other < subs:
                neighbours.append((sub * shards + b, other * shards + b))
    codes = aggregate[None]
    lists = wanted_rows[0]
    table = coarse_inverse.reshape(-1, LANES)
    packed_shape = (packed_rows, LANES)

    packed, lists, table = pl.pallas_call(
        pack_kernel,
        out_shape=(
            jax.ShapeDtypeStruct(packed_shape, F32),
            jax.ShapeDtypeStruct(lists.shape, jnp.int32),
            jax.ShapeDtypeStruct(table.shape, F32),
        ),
        in_specs=[whole(pl.ANY)] * 5,
        out_specs=(whole(),) * 3,
        scratch_shapes=[
            pltpu.VMEM(residual.shape, F32),
            pltpu.VMEM(codes.shape, jnp.int32),
            pltpu.VMEM(lists.shape, jnp.int32),
            pltpu.VMEM(wanted_count.shape, jnp.int32),
            pltpu.SemaphoreType.DMA((5,)),
        ],
        compiler_params=limit(4),
        cost_estimate=weight(8 * 10**9),
        name="pack",
    )(in_hbm(residual), in_hbm(codes), in_hbm(lists), in_hbm(wanted_count), in_hbm(table))
    lists = lax.ppermute(lists, ("sub", "blk"), neighbours)
    over_core = lax.ppermute(residual, "blk", core_swap)
    core_codes = lax.ppermute(aggregate, "blk", core_swap)[None]

    rhs, m_hi, m_low = pl.pallas_call(
        functools.partial(near_kernel, rows, tiles),
        out_shape=(
            jax.ShapeDtypeStruct((rows, coarse_len), F32),
            jax.ShapeDtypeStruct((coarse_len, subs * width), BF16),
            jax.ShapeDtypeStruct((coarse_len, subs * width), BF16),
        ),
        in_specs=[whole()] * 4,
        out_specs=(whole(),) * 3,
        compiler_params=limit(12),
        cost_estimate=weight(2 * 10**9),
        name="near",
    )(packed, over_core, core_codes, table)
    far_rhs = lax.ppermute(rhs, "blk", far_swap)
    over_y = lax.ppermute(packed, "blk", far_swap)
    over_both = lax.ppermute(packed, "blk", both_swap)
    send, order = pl.pallas_call(
        functools.partial(coarse_kernel, width, rows, tiles, sub_order, blk_order),
        out_shape=(
            jax.ShapeDtypeStruct((subs, shards, rows // 4, LANES), F32),
            jax.ShapeDtypeStruct((8, LANES), F32),
        ),
        in_specs=[whole()] * 4,
        out_specs=(whole(), whole()),
        compiler_params=limit(12),
        cost_estimate=weight(8 * 10**9),
        name="coarse",
    )(rhs, far_rhs, m_hi, m_low)
    flat = send.reshape((subs * shards,) + send.shape[2:])
    members = [sub * shards + b for sub in sub_order for b in blk_order]
    got = lax.all_to_all(flat, ("sub", "blk"), 0, 0, axis_index_groups=[members], tiled=True)
    got = got.reshape((subs, shards) + flat.shape[1:])

    outgoing, near, far = pl.pallas_call(
        functools.partial(margin_kernel, tiles),
        out_shape=(
            jax.ShapeDtypeStruct((rows, margin), F32),
            jax.ShapeDtypeStruct((2, 3 * rows, cols), BF16),
            jax.ShapeDtypeStruct((shards - 2, 3 * rows, cols), BF16),
        ),
        in_specs=[whole()] * 6,
        out_specs=(whole(),) * 3,
        compiler_params=limit(8),
        cost_estimate=weight(4 * 10**9),
        name="margins",
    )(packed, over_core, over_y, over_both, lists, order)
    halo = lax.ppermute(outgoing, ("sub", "blk"), neighbours)

    owned, w_hi, w_low, hot = pl.pallas_call(
        functools.partial(own_kernel, margin),
        out_shape=(
            jax.ShapeDtypeStruct((rows, cols), F32),
            jax.ShapeDtypeStruct((2, margin, cols), BF16),
            jax.ShapeDtypeStruct((2, margin, cols), BF16),
            jax.ShapeDtypeStruct((coarse_len, cols), BF16),
        ),
        in_specs=[whole(), whole(), whole(pl.ANY), whole(pl.ANY)],
        out_specs=(whole(),) * 4,
        scratch_shapes=[
            pltpu.VMEM(codes.shape, jnp.int32),
            pltpu.VMEM(fine_inverse.shape[1:], F32),
            pltpu.SemaphoreType.DMA((shards * tiles // 2 + 3,)),
        ],
        compiler_params=limit(16),
        cost_estimate=weight(40 * 10**9),
        name="owned",
    )(near, far, in_hbm(codes), in_hbm(fine_inverse))

    fine, mine = pl.pallas_call(
        mine_kernel,
        out_shape=(
            jax.ShapeDtypeStruct((rows, cols), F32),
            jax.ShapeDtypeStruct(halo.shape, F32),
        ),
        in_specs=[whole()] * 4,
        out_specs=(whole(), whole()),
        compiler_params=limit(12),
        cost_estimate=weight(4 * 10**9),
        name="mine",
    )(halo, w_hi, w_low, owned)
    other = lax.ppermute(mine, "blk", core_swap)
    fine = pl.pallas_call(
        other_kernel,
        out_shape=jax.ShapeDtypeStruct((rows, cols), F32),
        in_specs=[whole()] * 4,
        out_specs=whole(),
        compiler_params=limit(12),
        cost_estimate=weight(10**9),
        name="other",
    )(other, w_hi, w_low, fine)

    sums = pl.pallas_call(
        functools.partial(reduce_kernel, blk_order),
        out_shape=jax.ShapeDtypeStruct(got.shape[1:], F32),
        in_specs=[whole()],
        out_specs=whole(),
        compiler_params=limit(8),
        cost_estimate=weight(10**8),
        name="reduce",
    )(got)
    other_sums = lax.ppermute(sums, "blk", core_swap)

    return pl.pallas_call(
        functools.partial(tail_kernel, width),
        out_shape=jax.ShapeDtypeStruct((rows, cols), F32),
        in_specs=[whole()] * 4,
        out_specs=whole(pl.ANY),
        scratch_shapes=[pltpu.VMEM((rows, cols), F32), pltpu.SemaphoreType.DMA((2,))],
        compiler_params=limit(12),
        name="tail",
    )(sums, other_sums, hot, fine)


def solution(mesh):
    in_specs = (
        P(None, ("sub", "blk")),
        P("sub", None, "blk"),
        P("sub", "blk", None),
        P("sub", None, None),
        P("sub", None),
        P(("sub", "blk")),
    )
    out_specs = P(None, ("sub", "blk"))
    return jax.shard_map(
        on_device, mesh=mesh, in_specs=in_specs, out_specs=out_specs, check_vma=False
    )
```

```python
import functools

import jax
import jax.numpy as jnp
from jax import lax
from jax.experimental import pallas as pl
from jax.experimental.pallas import tpu as pltpu
from jax.sharding import PartitionSpec as P

BF16 = jnp.bfloat16
F32 = jnp.float32
NN = (((1,), (0,)), ((), ()))
NT = (((1,), (1,)), ((), ()))
LANES = 128
MIB = 1 << 20


def split3(x):
    hi = x.astype(BF16)
    rest = x - hi.astype(F32)
    mid = rest.astype(BF16)
    low = (rest - mid.astype(F32)).astype(BF16)
    return jnp.concatenate([hi, mid, low], axis=0)


def split2(x):
    hi = x.astype(BF16)
    low = (x - hi.astype(F32)).astype(BF16)
    return hi, low


def dot(a, b, dims=NN):
    return lax.dot_general(a, b, dims, preferred_element_type=F32)


def dot_halves(x, w_hi, w_low):
    rows = x.shape[0]
    x_hi, x_low = split2(x)
    both = dot(jnp.concatenate([x_hi, x_low], axis=0), w_hi)
    return both[:rows] + both[rows:] + dot(x_hi, w_low)


def fold3(acc):
    rows = acc.shape[0] // 3
    return acc[:rows] + acc[rows : 2 * rows] + acc[2 * rows :]


def onehot(condition):
    return condition.astype(F32).astype(BF16)


def block_rows(ref, rows, first, count):
    return jnp.concatenate([ref[pl.ds((first + t) * rows, rows)] for t in range(count)], axis=1)


def block_shard(k):
    return lax.axis_index("blk") ^ k


def facing():
    return (lax.axis_index("sub") ^ lax.axis_index("blk")) & 1


def pack_kernel(
    residual_ref, agg_ref, lists_ref, counts_ref,
    out_ref, lists_out,
    residual_buf, agg_buf, lists_buf, counts_buf, sems,
):
    sources = (residual_ref, agg_ref, lists_ref, counts_ref)
    targets = (residual_buf, agg_buf, lists_buf, counts_buf)
    fetches = [pltpu.make_async_copy(a, b, sems.at[k]) for k, (a, b) in enumerate(zip(sources, targets))]
    for fetch in fetches:
        fetch.start()
    rows, cols = residual_buf.shape
    tiles = cols // LANES
    fetches[0].wait()
    for t in range(tiles):
        out_ref[t * rows : (t + 1) * rows] = residual_buf[:, t * LANES : (t + 1) * LANES]
    fetches[1].wait()
    codes = [agg_buf[:, t * LANES : (t + 1) * LANES].astype(F32) for t in range(tiles)]
    codes.append(jnp.zeros((out_ref.shape[0] - rows * tiles - tiles, LANES), F32))
    out_ref[rows * tiles :] = jnp.concatenate(codes, axis=0)
    fetches[2].wait()
    fetches[3].wait()
    slots = lax.broadcasted_iota(jnp.int32, (1, lists_buf.shape[1]), 1)
    for side in range(2):
        used = slots < counts_buf[:, side : side + 1]
        lists_out[side : side + 1] = jnp.where(used, lists_buf[side : side + 1], -1)


def near_kernel(
    rows, tiles, packed_ref, core_ref, core_agg_ref, coarse_ref, rhs_ref, hi_ref, low_ref
):
    coarse_len = hi_ref.shape[0]
    levels = lax.broadcasted_iota(jnp.int32, (coarse_len, tiles * LANES), 0)
    codes = [packed_ref[pl.ds(tiles * rows + t, 1)] for t in range(tiles)]
    unknowns = jnp.concatenate(codes, axis=1).astype(jnp.int32)
    rhs = dot(split3(block_rows(packed_ref, rows, 0, tiles)), onehot(levels == unknowns), NT)
    rhs = rhs + dot(split3(core_ref[...]), onehot(levels == core_agg_ref[...]), NT)
    rhs_ref[...] = fold3(rhs)
    stride = coarse_ref.shape[0] // coarse_len
    for tile in range(stride):
        at = slice(tile * LANES, (tile + 1) * LANES)
        hi_ref[:, at], low_ref[:, at] = split2(coarse_ref[pl.ds(tile, coarse_len, stride=stride), :])


def coarse_kernel(
    width, rows, tiles, sub_order, blk_order,
    packed_ref, core_ref, rhs_ref, far_ref, hi_ref, low_ref, send_ref, parts_ref,
):
    parts_ref[0] = split3(block_rows(packed_ref, rows, 0, tiles))
    parts_ref[1] = split3(core_ref[...])
    rhs = rhs_ref[...] + far_ref[...]
    half = rows // 2
    lane = lax.broadcasted_iota(jnp.int32, (half, LANES), 1)
    step = 2 * LANES
    for first in range(0, hi_ref.shape[1], step):
        at = slice(first, first + step)
        value = dot_halves(rhs, hi_ref[:, at], low_ref[:, at])
        for k in range(2):
            to = 2 * (first // LANES + k)
            part = value[:, k * LANES : (k + 1) * LANES]
            turned = pltpu.roll(part, width, 1)
            left = jnp.where(lane < width, part[:half], turned[half:])
            right = jnp.where(lane < width, turned[:half], part[half:])
            for copy in range(send_ref.shape[1] // 2):
                for core in range(2):
                    piece = slice(core * half // 2, (core + 1) * half // 2)
                    at = blk_order.index(2 * copy + core)
                    send_ref[sub_order.index(to), at] = left[piece]
                    send_ref[sub_order.index(to + 1), at] = right[piece]


def margin_kernel(tiles, near_ref, y_ref, both_ref, lists_ref, out_ref, far_ref):
    half, rows, cols = near_ref.shape
    wanted = jnp.where(facing() == 1, lists_ref[1:2], lists_ref[0:1])
    local = lax.broadcasted_iota(jnp.int32, (cols, wanted.shape[1]), 0)
    for k, ref in enumerate((y_ref, both_ref)):
        far_ref[k] = split3(block_rows(ref, rows // 3, 0, tiles))
    total = jnp.zeros((rows, wanted.shape[1]), F32)
    for k in range(2 * half):
        part = near_ref[k] if k < half else far_ref[k - half]
        total = total + dot(part, onehot(local == wanted - block_shard(k) * cols))
    out_ref[...] = fold3(total)


def own_kernel(
    margin, near_ref, far_ref, agg_ref, fine_ref, out_ref, hi_ref, low_ref, hot_ref, agg_buf, fine_buf, sems
):
    half, rows, cols = near_ref.shape
    shards = 2 * half
    rows = rows // 3
    tiles = cols // LANES
    ext = fine_ref.shape[1]
    step = 2 * LANES
    per_block = tiles * LANES // step
    starts = [
        pl.multiple_of(margin + block_shard(k) * (tiles * LANES) + part * step, step)
        for k in range(shards)
        for part in range(per_block)
    ]
    starts += [0, ext - margin]
    sizes = [step] * (len(starts) - 2) + [margin] * 2
    fetch = pltpu.make_async_copy(agg_ref, agg_buf, sems.at[len(starts)])
    fetch.start()
    copies = []
    for k, (start, size) in enumerate(zip(starts, sizes)):
        copies.append(
            pltpu.make_async_copy(
                fine_ref.at[0, pl.ds(start, size)], fine_buf.at[pl.ds(start, size)], sems.at[k]
            )
        )
        copies[k].start()
    fetch.wait()
    levels = lax.broadcasted_iota(jnp.int32, hot_ref.shape, 0)
    hot_ref[...] = onehot(levels == agg_buf[...])
    total = jnp.zeros(out_ref.shape, F32)
    for k, start in enumerate(starts[:-2]):
        part = k % per_block
        at = k // per_block
        ref = near_ref if at < half else far_ref
        block = ref[at % half, :, part * step : (part + 1) * step]
        copies[k].wait()
        w_hi, w_low = split2(fine_buf[pl.ds(start, step)])
        both = dot(block[: 2 * rows], w_hi)
        total = total + (both[:rows] + both[rows:] + dot(block[:rows], w_low))
    out_ref[...] = total
    for side in range(2):
        start = starts[side - 2]
        copies[side - 2].wait()
        hi_ref[side], low_ref[side] = split2(fine_buf[start : start + margin])


def mine_kernel(halo_ref, hi_ref, low_ref, total_ref, out_ref, copy_ref):
    halo = halo_ref[...]
    copy_ref[...] = halo
    side = 1 - facing()
    out_ref[...] = total_ref[...] + dot_halves(halo, hi_ref[side], low_ref[side])


def other_kernel(halo_ref, hi_ref, low_ref, total_ref, out_ref):
    side = facing()
    out_ref[...] = total_ref[...] + dot_halves(halo_ref[...], hi_ref[side], low_ref[side])


def reduce_kernel(blk_order, got_ref, out_ref):
    total = got_ref[0]
    for sub in range(1, got_ref.shape[0]):
        total = total + got_ref[sub]
    for k, b in enumerate(blk_order):
        out_ref[b] = total[k]


def tail_kernel(width, mine_ref, other_ref, hot_ref, total_ref, out_ref):
    odd = (lax.axis_index("blk") & 1) == 1
    chunks = []
    for k in range(mine_ref.shape[0]):
        mine, other = mine_ref[k], other_ref[k]
        pieces = [jnp.where(odd, other, mine), jnp.where(odd, mine, other)]
        chunks.append(jnp.concatenate(pieces, axis=0))
    lane = lax.broadcasted_iota(jnp.int32, chunks[0].shape, 1)
    top, bottom = [], []
    for left, right in zip(chunks[::2], chunks[1::2]):
        top.append(jnp.where(lane < width, left, pltpu.roll(right, width, 1)))
        bottom.append(jnp.where(lane < width, pltpu.roll(left, width, 1), right))
    coarse = jnp.concatenate([jnp.concatenate(top, axis=1), jnp.concatenate(bottom, axis=1)], axis=0)
    out_ref[...] = total_ref[...] + fold3(dot(split3(coarse), hot_ref[...]))


def whole(space=pltpu.VMEM):
    return pl.BlockSpec(memory_space=space)


def limit(mib):
    return pltpu.CompilerParams(vmem_limit_bytes=mib * MIB)


def in_hbm(x):
    return pltpu.with_memory_space_constraint(x, pltpu.HBM)


def weight(flops):
    return pl.CostEstimate(flops=flops, bytes_accessed=0, transcendentals=0)


def on_device(residual, fine_inverse, coarse_inverse, wanted_rows, wanted_count, aggregate):
    subs = lax.axis_size("sub")
    shards = lax.axis_size("blk")
    rows, cols = residual.shape
    tiles = cols // LANES
    margin = wanted_rows.shape[2]
    coarse_len = coarse_inverse.shape[0]
    width = coarse_len // shards
    packed_rows = -(-(rows * tiles + tiles) // 8) * 8
    lead = (subs // 2 + 1) % subs
    sub_order = [(lead + k) % subs for k in range(subs)]
    blk_order = [b ^ 2 for b in range(shards)]
    core_swap = [(b, b ^ 1) for b in range(shards)]
    far_swap = [(b, b ^ 2) for b in range(shards)]
    both_swap = [(b, b ^ 3) for b in range(shards)]
    neighbours = []
    for sub in range(subs):
        for b in range(shards):
            other = sub ^ 1 if b % 2 == 0 else (sub + 1 if sub % 2 else sub - 1)
            if 0 <= other < subs:
                neighbours.append((sub * shards + b, other * shards + b))
    codes = aggregate[None]
    lists = wanted_rows[0]
    table = coarse_inverse.reshape(-1, LANES)
    packed_shape = (packed_rows, LANES)

    packed, lists = pl.pallas_call(
        pack_kernel,
        out_shape=(
            jax.ShapeDtypeStruct(packed_shape, F32),
            jax.ShapeDtypeStruct(lists.shape, jnp.int32),
        ),
        in_specs=[whole(pl.ANY)] * 4,
        out_specs=(whole(), whole()),
        scratch_shapes=[
            pltpu.VMEM(residual.shape, F32),
            pltpu.VMEM(codes.shape, jnp.int32),
            pltpu.VMEM(lists.shape, jnp.int32),
            pltpu.VMEM(wanted_count.shape, jnp.int32),
            pltpu.SemaphoreType.DMA((4,)),
        ],
        compiler_params=limit(4),
        cost_estimate=weight(8 * 10**9),
        name="pack",
    )(in_hbm(residual), in_hbm(codes), in_hbm(lists), in_hbm(wanted_count))
    lists = lax.ppermute(lists, ("sub", "blk"), neighbours)
    over_core = lax.ppermute(residual, "blk", core_swap)
    core_codes = lax.ppermute(aggregate, "blk", core_swap)[None]

    rhs, m_hi, m_low = pl.pallas_call(
        functools.partial(near_kernel, rows, tiles),
        out_shape=(
            jax.ShapeDtypeStruct((rows, coarse_len), F32),
            jax.ShapeDtypeStruct((coarse_len, subs * width), BF16),
            jax.ShapeDtypeStruct((coarse_len, subs * width), BF16),
        ),
        in_specs=[whole()] * 4,
        out_specs=(whole(),) * 3,
        compiler_params=limit(12),
        cost_estimate=weight(2 * 10**9),
        name="near",
    )(packed, over_core, core_codes, table)
    far_rhs = lax.ppermute(rhs, "blk", far_swap)
    over_y = lax.ppermute(packed, "blk", far_swap)
    over_both = lax.ppermute(packed, "blk", both_swap)
    send, near = pl.pallas_call(
        functools.partial(coarse_kernel, width, rows, tiles, sub_order, blk_order),
        out_shape=(
            jax.ShapeDtypeStruct((subs, shards, rows // 4, LANES), F32),
            jax.ShapeDtypeStruct((2, 3 * rows, cols), BF16),
        ),
        in_specs=[whole()] * 6,
        out_specs=(whole(), whole()),
        compiler_params=limit(12),
        cost_estimate=weight(8 * 10**9),
        name="coarse",
    )(packed, over_core, rhs, far_rhs, m_hi, m_low)
    flat = send.reshape((subs * shards,) + send.shape[2:])
    members = [sub * shards + b for sub in sub_order for b in blk_order]
    got = lax.all_to_all(flat, ("sub", "blk"), 0, 0, axis_index_groups=[members], tiled=True)
    got = got.reshape((subs, shards) + flat.shape[1:])

    outgoing, far = pl.pallas_call(
        functools.partial(margin_kernel, tiles),
        out_shape=(
            jax.ShapeDtypeStruct((rows, margin), F32),
            jax.ShapeDtypeStruct((shards - 2, 3 * rows, cols), BF16),
        ),
        in_specs=[whole()] * 4,
        out_specs=(whole(), whole()),
        compiler_params=limit(8),
        cost_estimate=weight(4 * 10**9),
        name="margins",
    )(near, over_y, over_both, lists)
    halo = lax.ppermute(outgoing, ("sub", "blk"), neighbours)

    owned, w_hi, w_low, hot = pl.pallas_call(
        functools.partial(own_kernel, margin),
        out_shape=(
            jax.ShapeDtypeStruct((rows, cols), F32),
            jax.ShapeDtypeStruct((2, margin, cols), BF16),
            jax.ShapeDtypeStruct((2, margin, cols), BF16),
            jax.ShapeDtypeStruct((coarse_len, cols), BF16),
        ),
        in_specs=[whole(), whole(), whole(pl.ANY), whole(pl.ANY)],
        out_specs=(whole(),) * 4,
        scratch_shapes=[
            pltpu.VMEM(codes.shape, jnp.int32),
            pltpu.VMEM(fine_inverse.shape[1:], F32),
            pltpu.SemaphoreType.DMA((shards * tiles // 2 + 3,)),
        ],
        compiler_params=limit(16),
        cost_estimate=weight(40 * 10**9),
        name="owned",
    )(near, far, in_hbm(codes), in_hbm(fine_inverse))

    fine, mine = pl.pallas_call(
        mine_kernel,
        out_shape=(
            jax.ShapeDtypeStruct((rows, cols), F32),
            jax.ShapeDtypeStruct(halo.shape, F32),
        ),
        in_specs=[whole()] * 4,
        out_specs=(whole(), whole()),
        compiler_params=limit(12),
        cost_estimate=weight(4 * 10**9),
        name="mine",
    )(halo, w_hi, w_low, owned)
    other = lax.ppermute(mine, "blk", core_swap)
    fine = pl.pallas_call(
        other_kernel,
        out_shape=jax.ShapeDtypeStruct((rows, cols), F32),
        in_specs=[whole()] * 4,
        out_specs=whole(),
        compiler_params=limit(12),
        cost_estimate=weight(10**9),
        name="other",
    )(other, w_hi, w_low, fine)

    sums = pl.pallas_call(
        functools.partial(reduce_kernel, blk_order),
        out_shape=jax.ShapeDtypeStruct(got.shape[1:], F32),
        in_specs=[whole()],
        out_specs=whole(),
        compiler_params=limit(8),
        cost_estimate=weight(10**8),
        name="reduce",
    )(got)
    other_sums = lax.ppermute(sums, "blk", core_swap)

    return pl.pallas_call(
        functools.partial(tail_kernel, width),
        out_shape=jax.ShapeDtypeStruct((rows, cols), F32),
        in_specs=[whole()] * 4,
        out_specs=whole(),
        compiler_params=limit(12),
        name="tail",
    )(sums, other_sums, hot, fine)


def solution(mesh):
    in_specs = (
        P(None, ("sub", "blk")),
        P("sub", None, "blk"),
        P("sub", "blk", None),
        P("sub", None, None),
        P("sub", None),
        P(("sub", "blk")),
    )
    out_specs = P(None, ("sub", "blk"))
    return jax.shard_map(
        on_device, mesh=mesh, in_specs=in_specs, out_specs=out_specs, check_vma=False
    )
```

```python
import functools

import jax
import jax.numpy as jnp
from jax import lax
from jax.experimental import pallas as pl
from jax.experimental.pallas import tpu as pltpu
from jax.sharding import PartitionSpec as P

BF16 = jnp.bfloat16
F32 = jnp.float32
NN = (((1,), (0,)), ((), ()))
NT = (((1,), (1,)), ((), ()))
LANES = 128
MIB = 1 << 20


def split3(x):
    hi = x.astype(BF16)
    rest = x - hi.astype(F32)
    mid = rest.astype(BF16)
    low = (rest - mid.astype(F32)).astype(BF16)
    return jnp.concatenate([hi, mid, low], axis=0)


def split2(x):
    hi = x.astype(BF16)
    low = (x - hi.astype(F32)).astype(BF16)
    return hi, low


def dot(a, b, dims=NN):
    return lax.dot_general(a, b, dims, preferred_element_type=F32)


def dot_halves(x, w_hi, w_low):
    rows = x.shape[0]
    x_hi, x_low = split2(x)
    both = dot(jnp.concatenate([x_hi, x_low], axis=0), w_hi)
    return both[:rows] + both[rows:] + dot(x_hi, w_low)


def fold3(acc):
    rows = acc.shape[0] // 3
    return acc[:rows] + acc[rows : 2 * rows] + acc[2 * rows :]


def onehot(condition):
    return condition.astype(F32).astype(BF16)


def block_rows(ref, rows, first, count):
    return jnp.concatenate([ref[pl.ds((first + t) * rows, rows)] for t in range(count)], axis=1)


def block_shard(k):
    return lax.axis_index("blk") ^ k


def facing():
    return (lax.axis_index("sub") ^ lax.axis_index("blk")) & 1


def pack_kernel(
    residual_ref, agg_ref, lists_ref, counts_ref, coarse_ref,
    out_ref, lists_out, coarse_out,
    residual_buf, agg_buf, lists_buf, counts_buf, sems,
):
    sources = (residual_ref, agg_ref, lists_ref, counts_ref, coarse_ref)
    targets = (residual_buf, agg_buf, lists_buf, counts_buf, coarse_out)
    fetches = [pltpu.make_async_copy(a, b, sems.at[k]) for k, (a, b) in enumerate(zip(sources, targets))]
    for fetch in fetches:
        fetch.start()
    rows, cols = residual_buf.shape
    tiles = cols // LANES
    fetches[0].wait()
    for t in range(tiles):
        out_ref[t * rows : (t + 1) * rows] = residual_buf[:, t * LANES : (t + 1) * LANES]
    fetches[1].wait()
    codes = [agg_buf[:, t * LANES : (t + 1) * LANES].astype(F32) for t in range(tiles)]
    codes.append(jnp.zeros((out_ref.shape[0] - rows * tiles - tiles, LANES), F32))
    out_ref[rows * tiles :] = jnp.concatenate(codes, axis=0)
    fetches[2].wait()
    fetches[3].wait()
    slots = lax.broadcasted_iota(jnp.int32, (1, lists_buf.shape[1]), 1)
    for side in range(2):
        used = slots < counts_buf[:, side : side + 1]
        lists_out[side : side + 1] = jnp.where(used, lists_buf[side : side + 1], -1)
    fetches[4].wait()


def near_kernel(
    rows, tiles, packed_ref, core_ref, core_agg_ref, coarse_ref, rhs_ref, hi_ref, low_ref
):
    coarse_len = hi_ref.shape[0]
    levels = lax.broadcasted_iota(jnp.int32, (coarse_len, tiles * LANES), 0)
    codes = [packed_ref[pl.ds(tiles * rows + t, 1)] for t in range(tiles)]
    unknowns = jnp.concatenate(codes, axis=1).astype(jnp.int32)
    rhs = dot(split3(block_rows(packed_ref, rows, 0, tiles)), onehot(levels == unknowns), NT)
    rhs = rhs + dot(split3(core_ref[...]), onehot(levels == core_agg_ref[...]), NT)
    rhs_ref[...] = fold3(rhs)
    stride = coarse_ref.shape[0] // coarse_len
    for tile in range(stride):
        at = slice(tile * LANES, (tile + 1) * LANES)
        hi_ref[:, at], low_ref[:, at] = split2(coarse_ref[pl.ds(tile, coarse_len, stride=stride), :])


def coarse_kernel(
    width, rows, tiles, sub_order, blk_order,
    packed_ref, core_ref, rhs_ref, far_ref, hi_ref, low_ref, send_ref, parts_ref,
):
    parts_ref[0] = split3(block_rows(packed_ref, rows, 0, tiles))
    parts_ref[1] = split3(core_ref[...])
    rhs = rhs_ref[...] + far_ref[...]
    half = rows // 2
    lane = lax.broadcasted_iota(jnp.int32, (half, LANES), 1)
    step = 2 * LANES
    for first in range(0, hi_ref.shape[1], step):
        at = slice(first, first + step)
        value = dot_halves(rhs, hi_ref[:, at], low_ref[:, at])
        for k in range(2):
            to = 2 * (first // LANES + k)
            part = value[:, k * LANES : (k + 1) * LANES]
            turned = pltpu.roll(part, width, 1)
            left = jnp.where(lane < width, part[:half], turned[half:])
            right = jnp.where(lane < width, turned[:half], part[half:])
            for copy in range(send_ref.shape[1] // 2):
                for core in range(2):
                    piece = slice(core * half // 2, (core + 1) * half // 2)
                    at = blk_order.index(2 * copy + core)
                    send_ref[sub_order.index(to), at] = left[piece]
                    send_ref[sub_order.index(to + 1), at] = right[piece]


def margin_kernel(tiles, near_ref, y_ref, both_ref, lists_ref, out_ref, far_ref):
    half, rows, cols = near_ref.shape
    wanted = jnp.where(facing() == 1, lists_ref[1:2], lists_ref[0:1])
    local = lax.broadcasted_iota(jnp.int32, (cols, wanted.shape[1]), 0)
    for k, ref in enumerate((y_ref, both_ref)):
        far_ref[k] = split3(block_rows(ref, rows // 3, 0, tiles))
    total = jnp.zeros((rows, wanted.shape[1]), F32)
    for k in range(2 * half):
        part = near_ref[k] if k < half else far_ref[k - half]
        total = total + dot(part, onehot(local == wanted - block_shard(k) * cols))
    out_ref[...] = fold3(total)


def own_kernel(
    margin, near_ref, far_ref, agg_ref, fine_ref, out_ref, hi_ref, low_ref, hot_ref, agg_buf, fine_buf, sems
):
    half, rows, cols = near_ref.shape
    shards = 2 * half
    rows = rows // 3
    tiles = cols // LANES
    ext = fine_ref.shape[1]
    step = 2 * LANES
    per_block = tiles * LANES // step
    starts = [
        pl.multiple_of(margin + block_shard(k) * (tiles * LANES) + part * step, step)
        for k in range(shards)
        for part in range(per_block)
    ]
    starts += [0, ext - margin]
    sizes = [step] * (len(starts) - 2) + [margin] * 2
    fetch = pltpu.make_async_copy(agg_ref, agg_buf, sems.at[len(starts)])
    fetch.start()
    copies = []
    for k, (start, size) in enumerate(zip(starts, sizes)):
        copies.append(
            pltpu.make_async_copy(
                fine_ref.at[0, pl.ds(start, size)], fine_buf.at[pl.ds(start, size)], sems.at[k]
            )
        )
        copies[k].start()
    fetch.wait()
    levels = lax.broadcasted_iota(jnp.int32, hot_ref.shape, 0)
    hot_ref[...] = onehot(levels == agg_buf[...])
    total = jnp.zeros(out_ref.shape, F32)
    for k, start in enumerate(starts[:-2]):
        part = k % per_block
        at = k // per_block
        ref = near_ref if at < half else far_ref
        block = ref[at % half, :, part * step : (part + 1) * step]
        copies[k].wait()
        w_hi, w_low = split2(fine_buf[pl.ds(start, step)])
        both = dot(block[: 2 * rows], w_hi)
        total = total + (both[:rows] + both[rows:] + dot(block[:rows], w_low))
    out_ref[...] = total
    for side in range(2):
        start = starts[side - 2]
        copies[side - 2].wait()
        hi_ref[side], low_ref[side] = split2(fine_buf[start : start + margin])


def mine_kernel(halo_ref, hi_ref, low_ref, total_ref, out_ref, copy_ref):
    halo = halo_ref[...]
    copy_ref[...] = halo
    side = 1 - facing()
    out_ref[...] = total_ref[...] + dot_halves(halo, hi_ref[side], low_ref[side])


def other_kernel(halo_ref, hi_ref, low_ref, total_ref, out_ref):
    side = facing()
    out_ref[...] = total_ref[...] + dot_halves(halo_ref[...], hi_ref[side], low_ref[side])


def reduce_kernel(blk_order, got_ref, out_ref):
    total = got_ref[0]
    for sub in range(1, got_ref.shape[0]):
        total = total + got_ref[sub]
    for k, b in enumerate(blk_order):
        out_ref[b] = total[k]


def tail_kernel(width, mine_ref, other_ref, hot_ref, total_ref, out_ref):
    odd = (lax.axis_index("blk") & 1) == 1
    chunks = []
    for k in range(mine_ref.shape[0]):
        mine, other = mine_ref[k], other_ref[k]
        pieces = [jnp.where(odd, other, mine), jnp.where(odd, mine, other)]
        chunks.append(jnp.concatenate(pieces, axis=0))
    lane = lax.broadcasted_iota(jnp.int32, chunks[0].shape, 1)
    top, bottom = [], []
    for left, right in zip(chunks[::2], chunks[1::2]):
        top.append(jnp.where(lane < width, left, pltpu.roll(right, width, 1)))
        bottom.append(jnp.where(lane < width, pltpu.roll(left, width, 1), right))
    coarse = jnp.concatenate([jnp.concatenate(top, axis=1), jnp.concatenate(bottom, axis=1)], axis=0)
    out_ref[...] = total_ref[...] + fold3(dot(split3(coarse), hot_ref[...]))


def whole(space=pltpu.VMEM):
    return pl.BlockSpec(memory_space=space)


def limit(mib):
    return pltpu.CompilerParams(vmem_limit_bytes=mib * MIB)


def in_hbm(x):
    return pltpu.with_memory_space_constraint(x, pltpu.HBM)


def weight(flops):
    return pl.CostEstimate(flops=flops, bytes_accessed=0, transcendentals=0)


def on_device(residual, fine_inverse, coarse_inverse, wanted_rows, wanted_count, aggregate):
    subs = lax.axis_size("sub")
    shards = lax.axis_size("blk")
    rows, cols = residual.shape
    tiles = cols // LANES
    margin = wanted_rows.shape[2]
    coarse_len = coarse_inverse.shape[0]
    width = coarse_len // shards
    packed_rows = -(-(rows * tiles + tiles) // 8) * 8
    lead = (subs // 2 + 1) % subs
    sub_order = [(lead - k) % subs for k in range(subs)]
    blk_order = [b ^ 2 for b in range(shards)]
    core_swap = [(b, b ^ 1) for b in range(shards)]
    far_swap = [(b, b ^ 2) for b in range(shards)]
    both_swap = [(b, b ^ 3) for b in range(shards)]
    neighbours = []
    for sub in range(subs):
        for b in range(shards):
            other = sub ^ 1 if b % 2 == 0 else (sub + 1 if sub % 2 else sub - 1)
            if 0 <= other < subs:
                neighbours.append((sub * shards + b, other * shards + b))
    codes = aggregate[None]
    lists = wanted_rows[0]
    table = coarse_inverse.reshape(-1, LANES)
    packed_shape = (packed_rows, LANES)

    packed, lists, table = pl.pallas_call(
        pack_kernel,
        out_shape=(
            jax.ShapeDtypeStruct(packed_shape, F32),
            jax.ShapeDtypeStruct(lists.shape, jnp.int32),
            jax.ShapeDtypeStruct(table.shape, F32),
        ),
        in_specs=[whole(pl.ANY)] * 5,
        out_specs=(whole(),) * 3,
        scratch_shapes=[
            pltpu.VMEM(residual.shape, F32),
            pltpu.VMEM(codes.shape, jnp.int32),
            pltpu.VMEM(lists.shape, jnp.int32),
            pltpu.VMEM(wanted_count.shape, jnp.int32),
            pltpu.SemaphoreType.DMA((5,)),
        ],
        compiler_params=limit(4),
        cost_estimate=weight(8 * 10**9),
        name="pack",
    )(in_hbm(residual), in_hbm(codes), in_hbm(lists), in_hbm(wanted_count), in_hbm(table))
    lists = lax.ppermute(lists, ("sub", "blk"), neighbours)
    over_core = lax.ppermute(residual, "blk", core_swap)
    core_codes = lax.ppermute(aggregate, "blk", core_swap)[None]

    rhs, m_hi, m_low = pl.pallas_call(
        functools.partial(near_kernel, rows, tiles),
        out_shape=(
            jax.ShapeDtypeStruct((rows, coarse_len), F32),
            jax.ShapeDtypeStruct((coarse_len, subs * width), BF16),
            jax.ShapeDtypeStruct((coarse_len, subs * width), BF16),
        ),
        in_specs=[whole()] * 4,
        out_specs=(whole(),) * 3,
        compiler_params=limit(12),
        cost_estimate=weight(2 * 10**9),
        name="near",
    )(packed, over_core, core_codes, table)
    far_rhs = lax.ppermute(rhs, "blk", far_swap)
    over_y = lax.ppermute(packed, "blk", far_swap)
    over_both = lax.ppermute(packed, "blk", both_swap)
    send, near = pl.pallas_call(
        functools.partial(coarse_kernel, width, rows, tiles, sub_order, blk_order),
        out_shape=(
            jax.ShapeDtypeStruct((subs, shards, rows // 4, LANES), F32),
            jax.ShapeDtypeStruct((2, 3 * rows, cols), BF16),
        ),
        in_specs=[whole()] * 6,
        out_specs=(whole(), whole()),
        compiler_params=limit(12),
        cost_estimate=weight(8 * 10**9),
        name="coarse",
    )(packed, over_core, rhs, far_rhs, m_hi, m_low)
    flat = send.reshape((subs * shards,) + send.shape[2:])
    members = [sub * shards + b for sub in sub_order for b in blk_order]
    got = lax.all_to_all(flat, ("sub", "blk"), 0, 0, axis_index_groups=[members], tiled=True)
    got = got.reshape((subs, shards) + flat.shape[1:])

    outgoing, far = pl.pallas_call(
        functools.partial(margin_kernel, tiles),
        out_shape=(
            jax.ShapeDtypeStruct((rows, margin), F32),
            jax.ShapeDtypeStruct((shards - 2, 3 * rows, cols), BF16),
        ),
        in_specs=[whole()] * 4,
        out_specs=(whole(), whole()),
        compiler_params=limit(8),
        cost_estimate=weight(4 * 10**9),
        name="margins",
    )(near, over_y, over_both, lists)
    halo = lax.ppermute(outgoing, ("sub", "blk"), neighbours)

    owned, w_hi, w_low, hot = pl.pallas_call(
        functools.partial(own_kernel, margin),
        out_shape=(
            jax.ShapeDtypeStruct((rows, cols), F32),
            jax.ShapeDtypeStruct((2, margin, cols), BF16),
            jax.ShapeDtypeStruct((2, margin, cols), BF16),
            jax.ShapeDtypeStruct((coarse_len, cols), BF16),
        ),
        in_specs=[whole(), whole(), whole(pl.ANY), whole(pl.ANY)],
        out_specs=(whole(),) * 4,
        scratch_shapes=[
            pltpu.VMEM(codes.shape, jnp.int32),
            pltpu.VMEM(fine_inverse.shape[1:], F32),
            pltpu.SemaphoreType.DMA((shards * tiles // 2 + 3,)),
        ],
        compiler_params=limit(16),
        cost_estimate=weight(40 * 10**9),
        name="owned",
    )(near, far, in_hbm(codes), in_hbm(fine_inverse))

    fine, mine = pl.pallas_call(
        mine_kernel,
        out_shape=(
            jax.ShapeDtypeStruct((rows, cols), F32),
            jax.ShapeDtypeStruct(halo.shape, F32),
        ),
        in_specs=[whole()] * 4,
        out_specs=(whole(), whole()),
        compiler_params=limit(12),
        cost_estimate=weight(4 * 10**9),
        name="mine",
    )(halo, w_hi, w_low, owned)
    other = lax.ppermute(mine, "blk", core_swap)
    fine = pl.pallas_call(
        other_kernel,
        out_shape=jax.ShapeDtypeStruct((rows, cols), F32),
        in_specs=[whole()] * 4,
        out_specs=whole(),
        compiler_params=limit(12),
        cost_estimate=weight(10**9),
        name="other",
    )(other, w_hi, w_low, fine)

    sums = pl.pallas_call(
        functools.partial(reduce_kernel, blk_order),
        out_shape=jax.ShapeDtypeStruct(got.shape[1:], F32),
        in_specs=[whole()],
        out_specs=whole(),
        compiler_params=limit(8),
        cost_estimate=weight(10**8),
        name="reduce",
    )(got)
    other_sums = lax.ppermute(sums, "blk", core_swap)

    return pl.pallas_call(
        functools.partial(tail_kernel, width),
        out_shape=jax.ShapeDtypeStruct((rows, cols), F32),
        in_specs=[whole()] * 4,
        out_specs=whole(),
        compiler_params=limit(12),
        name="tail",
    )(sums, other_sums, hot, fine)


def solution(mesh):
    in_specs = (
        P(None, ("sub", "blk")),
        P("sub", None, "blk"),
        P("sub", "blk", None),
        P("sub", None, None),
        P("sub", None),
        P(("sub", "blk")),
    )
    out_specs = P(None, ("sub", "blk"))
    return jax.shard_map(
        on_device, mesh=mesh, in_specs=in_specs, out_specs=out_specs, check_vma=False
    )
```

```python
import functools

import jax
import jax.numpy as jnp
from jax import lax
from jax.experimental import pallas as pl
from jax.experimental.pallas import tpu as pltpu
from jax.sharding import PartitionSpec as P

BF16 = jnp.bfloat16
F32 = jnp.float32
NN = (((1,), (0,)), ((), ()))
NT = (((1,), (1,)), ((), ()))
LANES = 128
MIB = 1 << 20


def split3(x):
    hi = x.astype(BF16)
    rest = x - hi.astype(F32)
    mid = rest.astype(BF16)
    low = (rest - mid.astype(F32)).astype(BF16)
    return jnp.concatenate([hi, mid, low], axis=0)


def split2(x):
    hi = x.astype(BF16)
    low = (x - hi.astype(F32)).astype(BF16)
    return hi, low


def dot(a, b, dims=NN):
    return lax.dot_general(a, b, dims, preferred_element_type=F32)


def dot_halves(x, w_hi, w_low):
    rows = x.shape[0]
    x_hi, x_low = split2(x)
    both = dot(jnp.concatenate([x_hi, x_low], axis=0), w_hi)
    return both[:rows] + both[rows:] + dot(x_hi, w_low)


def fold3(acc):
    rows = acc.shape[0] // 3
    return acc[:rows] + acc[rows : 2 * rows] + acc[2 * rows :]


def onehot(condition):
    return condition.astype(F32).astype(BF16)


def block_rows(ref, rows, first, count):
    return jnp.concatenate([ref[pl.ds((first + t) * rows, rows)] for t in range(count)], axis=1)


def block_shard(k):
    return lax.axis_index("blk") ^ k


def facing():
    return (lax.axis_index("sub") ^ lax.axis_index("blk")) & 1


def pack_kernel(
    residual_ref, agg_ref, lists_ref, counts_ref, coarse_ref,
    out_ref, lists_out, coarse_out,
    residual_buf, agg_buf, lists_buf, counts_buf, sems,
):
    sources = (residual_ref, agg_ref, lists_ref, counts_ref, coarse_ref)
    targets = (residual_buf, agg_buf, lists_buf, counts_buf, coarse_out)
    fetches = [pltpu.make_async_copy(a, b, sems.at[k]) for k, (a, b) in enumerate(zip(sources, targets))]
    for fetch in fetches:
        fetch.start()
    rows, cols = residual_buf.shape
    tiles = cols // LANES
    fetches[0].wait()
    for t in range(tiles):
        out_ref[t * rows : (t + 1) * rows] = residual_buf[:, t * LANES : (t + 1) * LANES]
    fetches[1].wait()
    codes = [agg_buf[:, t * LANES : (t + 1) * LANES].astype(F32) for t in range(tiles)]
    codes.append(jnp.zeros((out_ref.shape[0] - rows * tiles - tiles, LANES), F32))
    out_ref[rows * tiles :] = jnp.concatenate(codes, axis=0)
    fetches[2].wait()
    fetches[3].wait()
    slots = lax.broadcasted_iota(jnp.int32, (1, lists_buf.shape[1]), 1)
    for side in range(2):
        used = slots < counts_buf[:, side : side + 1]
        lists_out[side : side + 1] = jnp.where(used, lists_buf[side : side + 1], -1)
    fetches[4].wait()


def near_kernel(
    rows, tiles, packed_ref, core_ref, core_agg_ref, coarse_ref, rhs_ref, hi_ref, low_ref
):
    coarse_len = hi_ref.shape[0]
    levels = lax.broadcasted_iota(jnp.int32, (coarse_len, tiles * LANES), 0)
    codes = [packed_ref[pl.ds(tiles * rows + t, 1)] for t in range(tiles)]
    unknowns = jnp.concatenate(codes, axis=1).astype(jnp.int32)
    rhs = dot(split3(block_rows(packed_ref, rows, 0, tiles)), onehot(levels == unknowns), NT)
    rhs = rhs + dot(split3(core_ref[...]), onehot(levels == core_agg_ref[...]), NT)
    rhs_ref[...] = fold3(rhs)
    stride = coarse_ref.shape[0] // coarse_len
    for tile in range(stride):
        at = slice(tile * LANES, (tile + 1) * LANES)
        hi_ref[:, at], low_ref[:, at] = split2(coarse_ref[pl.ds(tile, coarse_len, stride=stride), :])


def coarse_kernel(
    width, rows, tiles, sub_order, blk_order,
    packed_ref, core_ref, rhs_ref, far_ref, hi_ref, low_ref, send_ref, parts_ref,
):
    parts_ref[0] = split3(block_rows(packed_ref, rows, 0, tiles))
    parts_ref[1] = split3(core_ref[...])
    rhs = rhs_ref[...] + far_ref[...]
    half = rows // 2
    lane = lax.broadcasted_iota(jnp.int32, (half, LANES), 1)
    step = 2 * LANES
    for first in range(0, hi_ref.shape[1], step):
        at = slice(first, first + step)
        value = dot_halves(rhs, hi_ref[:, at], low_ref[:, at])
        for k in range(2):
            to = 2 * (first // LANES + k)
            part = value[:, k * LANES : (k + 1) * LANES]
            turned = pltpu.roll(part, width, 1)
            left = jnp.where(lane < width, part[:half], turned[half:])
            right = jnp.where(lane < width, turned[:half], part[half:])
            for copy in range(send_ref.shape[1] // 2):
                for core in range(2):
                    piece = slice(core * half // 2, (core + 1) * half // 2)
                    at = blk_order.index(2 * copy + core)
                    send_ref[sub_order.index(to), at] = left[piece]
                    send_ref[sub_order.index(to + 1), at] = right[piece]


def margin_kernel(tiles, near_ref, y_ref, both_ref, lists_ref, out_ref, far_ref):
    half, rows, cols = near_ref.shape
    wanted = jnp.where(facing() == 1, lists_ref[1:2], lists_ref[0:1])
    local = lax.broadcasted_iota(jnp.int32, (cols, wanted.shape[1]), 0)
    for k, ref in enumerate((y_ref, both_ref)):
        far_ref[k] = split3(block_rows(ref, rows // 3, 0, tiles))
    total = jnp.zeros((rows, wanted.shape[1]), F32)
    for k in range(2 * half):
        part = near_ref[k] if k < half else far_ref[k - half]
        total = total + dot(part, onehot(local == wanted - block_shard(k) * cols))
    out_ref[...] = fold3(total)


def own_kernel(
    margin, near_ref, far_ref, agg_ref, fine_ref, out_ref, hi_ref, low_ref, hot_ref, agg_buf, fine_buf, sems
):
    half, rows, cols = near_ref.shape
    shards = 2 * half
    rows = rows // 3
    tiles = cols // LANES
    ext = fine_ref.shape[1]
    step = 2 * LANES
    per_block = tiles * LANES // step
    starts = [
        pl.multiple_of(margin + block_shard(k) * (tiles * LANES) + part * step, step)
        for k in range(shards)
        for part in range(per_block)
    ]
    starts += [0, ext - margin]
    sizes = [step] * (len(starts) - 2) + [margin] * 2
    fetch = pltpu.make_async_copy(agg_ref, agg_buf, sems.at[len(starts)])
    fetch.start()
    copies = []
    for k, (start, size) in enumerate(zip(starts, sizes)):
        copies.append(
            pltpu.make_async_copy(
                fine_ref.at[0, pl.ds(start, size)], fine_buf.at[pl.ds(start, size)], sems.at[k]
            )
        )
        copies[k].start()
    fetch.wait()
    levels = lax.broadcasted_iota(jnp.int32, hot_ref.shape, 0)
    hot_ref[...] = onehot(levels == agg_buf[...])
    total = jnp.zeros(out_ref.shape, F32)
    for k, start in enumerate(starts[:-2]):
        part = k % per_block
        at = k // per_block
        ref = near_ref if at < half else far_ref
        block = ref[at % half, :, part * step : (part + 1) * step]
        copies[k].wait()
        w_hi, w_low = split2(fine_buf[pl.ds(start, step)])
        both = dot(block[: 2 * rows], w_hi)
        total = total + (both[:rows] + both[rows:] + dot(block[:rows], w_low))
    out_ref[...] = total
    for side in range(2):
        start = starts[side - 2]
        copies[side - 2].wait()
        hi_ref[side], low_ref[side] = split2(fine_buf[start : start + margin])


def mine_kernel(halo_ref, hi_ref, low_ref, total_ref, out_ref, copy_ref):
    halo = halo_ref[...]
    copy_ref[...] = halo
    side = 1 - facing()
    out_ref[...] = total_ref[...] + dot_halves(halo, hi_ref[side], low_ref[side])


def other_kernel(halo_ref, hi_ref, low_ref, total_ref, out_ref):
    side = facing()
    out_ref[...] = total_ref[...] + dot_halves(halo_ref[...], hi_ref[side], low_ref[side])


def reduce_kernel(blk_order, got_ref, out_ref):
    total = got_ref[0]
    for sub in range(1, got_ref.shape[0]):
        total = total + got_ref[sub]
    for k, b in enumerate(blk_order):
        out_ref[b] = total[k]


def tail_kernel(width, mine_ref, other_ref, hot_ref, total_ref, out_ref):
    odd = (lax.axis_index("blk") & 1) == 1
    chunks = []
    for k in range(mine_ref.shape[0]):
        mine, other = mine_ref[k], other_ref[k]
        pieces = [jnp.where(odd, other, mine), jnp.where(odd, mine, other)]
        chunks.append(jnp.concatenate(pieces, axis=0))
    lane = lax.broadcasted_iota(jnp.int32, chunks[0].shape, 1)
    top, bottom = [], []
    for left, right in zip(chunks[::2], chunks[1::2]):
        top.append(jnp.where(lane < width, left, pltpu.roll(right, width, 1)))
        bottom.append(jnp.where(lane < width, pltpu.roll(left, width, 1), right))
    coarse = jnp.concatenate([jnp.concatenate(top, axis=1), jnp.concatenate(bottom, axis=1)], axis=0)
    out_ref[...] = total_ref[...] + fold3(dot(split3(coarse), hot_ref[...]))


def whole(space=pltpu.VMEM):
    return pl.BlockSpec(memory_space=space)


def limit(mib):
    return pltpu.CompilerParams(vmem_limit_bytes=mib * MIB)


def in_hbm(x):
    return pltpu.with_memory_space_constraint(x, pltpu.HBM)


def weight(flops):
    return pl.CostEstimate(flops=flops, bytes_accessed=0, transcendentals=0)


def on_device(residual, fine_inverse, coarse_inverse, wanted_rows, wanted_count, aggregate):
    subs = lax.axis_size("sub")
    shards = lax.axis_size("blk")
    rows, cols = residual.shape
    tiles = cols // LANES
    margin = wanted_rows.shape[2]
    coarse_len = coarse_inverse.shape[0]
    width = coarse_len // shards
    packed_rows = -(-(rows * tiles + tiles) // 8) * 8
    lead = (subs // 2 + 1) % subs
    sub_order = [(lead + k) % subs for k in range(subs)]
    blk_order = [b ^ 3 for b in range(shards)]
    core_swap = [(b, b ^ 1) for b in range(shards)]
    far_swap = [(b, b ^ 2) for b in range(shards)]
    both_swap = [(b, b ^ 3) for b in range(shards)]
    neighbours = []
    for sub in range(subs):
        for b in range(shards):
            other = sub ^ 1 if b % 2 == 0 else (sub + 1 if sub % 2 else sub - 1)
            if 0 <= other < subs:
                neighbours.append((sub * shards + b, other * shards + b))
    codes = aggregate[None]
    lists = wanted_rows[0]
    table = coarse_inverse.reshape(-1, LANES)
    packed_shape = (packed_rows, LANES)

    packed, lists, table = pl.pallas_call(
        pack_kernel,
        out_shape=(
            jax.ShapeDtypeStruct(packed_shape, F32),
            jax.ShapeDtypeStruct(lists.shape, jnp.int32),
            jax.ShapeDtypeStruct(table.shape, F32),
        ),
        in_specs=[whole(pl.ANY)] * 5,
        out_specs=(whole(),) * 3,
        scratch_shapes=[
            pltpu.VMEM(residual.shape, F32),
            pltpu.VMEM(codes.shape, jnp.int32),
            pltpu.VMEM(lists.shape, jnp.int32),
            pltpu.VMEM(wanted_count.shape, jnp.int32),
            pltpu.SemaphoreType.DMA((5,)),
        ],
        compiler_params=limit(4),
        cost_estimate=weight(8 * 10**9),
        name="pack",
    )(in_hbm(residual), in_hbm(codes), in_hbm(lists), in_hbm(wanted_count), in_hbm(table))
    lists = lax.ppermute(lists, ("sub", "blk"), neighbours)
    over_core = lax.ppermute(residual, "blk", core_swap)
    core_codes = lax.ppermute(aggregate, "blk", core_swap)[None]

    rhs, m_hi, m_low = pl.pallas_call(
        functools.partial(near_kernel, rows, tiles),
        out_shape=(
            jax.ShapeDtypeStruct((rows, coarse_len), F32),
            jax.ShapeDtypeStruct((coarse_len, subs * width), BF16),
            jax.ShapeDtypeStruct((coarse_len, subs * width), BF16),
        ),
        in_specs=[whole()] * 4,
        out_specs=(whole(),) * 3,
        compiler_params=limit(12),
        cost_estimate=weight(2 * 10**9),
        name="near",
    )(packed, over_core, core_codes, table)
    far_rhs = lax.ppermute(rhs, "blk", far_swap)
    over_y = lax.ppermute(packed, "blk", far_swap)
    over_both = lax.ppermute(packed, "blk", both_swap)
    send, near = pl.pallas_call(
        functools.partial(coarse_kernel, width, rows, tiles, sub_order, blk_order),
        out_shape=(
            jax.ShapeDtypeStruct((subs, shards, rows // 4, LANES), F32),
            jax.ShapeDtypeStruct((2, 3 * rows, cols), BF16),
        ),
        in_specs=[whole()] * 6,
        out_specs=(whole(), whole()),
        compiler_params=limit(12),
        cost_estimate=weight(8 * 10**9),
        name="coarse",
    )(packed, over_core, rhs, far_rhs, m_hi, m_low)
    flat = send.reshape((subs * shards,) + send.shape[2:])
    members = [sub * shards + b for sub in sub_order for b in blk_order]
    got = lax.all_to_all(flat, ("sub", "blk"), 0, 0, axis_index_groups=[members], tiled=True)
    got = got.reshape((subs, shards) + flat.shape[1:])

    outgoing, far = pl.pallas_call(
        functools.partial(margin_kernel, tiles),
        out_shape=(
            jax.ShapeDtypeStruct((rows, margin), F32),
            jax.ShapeDtypeStruct((shards - 2, 3 * rows, cols), BF16),
        ),
        in_specs=[whole()] * 4,
        out_specs=(whole(), whole()),
        compiler_params=limit(8),
        cost_estimate=weight(4 * 10**9),
        name="margins",
    )(near, over_y, over_both, lists)
    halo = lax.ppermute(outgoing, ("sub", "blk"), neighbours)

    owned, w_hi, w_low, hot = pl.pallas_call(
        functools.partial(own_kernel, margin),
        out_shape=(
            jax.ShapeDtypeStruct((rows, cols), F32),
            jax.ShapeDtypeStruct((2, margin, cols), BF16),
            jax.ShapeDtypeStruct((2, margin, cols), BF16),
            jax.ShapeDtypeStruct((coarse_len, cols), BF16),
        ),
        in_specs=[whole(), whole(), whole(pl.ANY), whole(pl.ANY)],
        out_specs=(whole(),) * 4,
        scratch_shapes=[
            pltpu.VMEM(codes.shape, jnp.int32),
            pltpu.VMEM(fine_inverse.shape[1:], F32),
            pltpu.SemaphoreType.DMA((shards * tiles // 2 + 3,)),
        ],
        compiler_params=limit(16),
        cost_estimate=weight(40 * 10**9),
        name="owned",
    )(near, far, in_hbm(codes), in_hbm(fine_inverse))

    fine, mine = pl.pallas_call(
        mine_kernel,
        out_shape=(
            jax.ShapeDtypeStruct((rows, cols), F32),
            jax.ShapeDtypeStruct(halo.shape, F32),
        ),
        in_specs=[whole()] * 4,
        out_specs=(whole(), whole()),
        compiler_params=limit(12),
        cost_estimate=weight(4 * 10**9),
        name="mine",
    )(halo, w_hi, w_low, owned)
    other = lax.ppermute(mine, "blk", core_swap)
    fine = pl.pallas_call(
        other_kernel,
        out_shape=jax.ShapeDtypeStruct((rows, cols), F32),
        in_specs=[whole()] * 4,
        out_specs=whole(),
        compiler_params=limit(12),
        cost_estimate=weight(10**9),
        name="other",
    )(other, w_hi, w_low, fine)

    sums = pl.pallas_call(
        functools.partial(reduce_kernel, blk_order),
        out_shape=jax.ShapeDtypeStruct(got.shape[1:], F32),
        in_specs=[whole()],
        out_specs=whole(),
        compiler_params=limit(8),
        cost_estimate=weight(10**8),
        name="reduce",
    )(got)
    other_sums = lax.ppermute(sums, "blk", core_swap)

    return pl.pallas_call(
        functools.partial(tail_kernel, width),
        out_shape=jax.ShapeDtypeStruct((rows, cols), F32),
        in_specs=[whole()] * 4,
        out_specs=whole(),
        compiler_params=limit(12),
        name="tail",
    )(sums, other_sums, hot, fine)


def solution(mesh):
    in_specs = (
        P(None, ("sub", "blk")),
        P("sub", None, "blk"),
        P("sub", "blk", None),
        P("sub", None, None),
        P("sub", None),
        P(("sub", "blk")),
    )
    out_specs = P(None, ("sub", "blk"))
    return jax.shard_map(
        on_device, mesh=mesh, in_specs=in_specs, out_specs=out_specs, check_vma=False
    )
```
